256 devices in a mesh: dp: 8 (over z), segment: 4 (over y), tm: 8 (over x, core).
Axes of the slice: x: 4, y: 4, z: 8, core: 2. Of those that a mesh axis runs over, the one named last changes fastest.
Arguments:
- latents: bfloat16 [16, 16, 4, 64], P('dp', 'tm'), may hold values from -6 to 6
- timesteps: int32 [16], P('dp'), may hold values from 0 to 999
- seeds: int32 [16], P('dp'), may hold values from 0 to 1073741823
- in_weight: bfloat16 [4, 320], replicated, may hold values from -3 to 3
- out_weight: bfloat16 [320, 4], replicated, may hold values from -0.3125 to 0.3125
- down_weight: bfloat16 [4, 3, 320, 320], P('segment'), may hold values from -0.1875 to 0.1875
- up_weight: bfloat16 [4, 3, 640, 320], P('segment'), may hold values from -0.125 to 0.125
- skip_weight: bfloat16 [4, 640, 320], P('segment'), may hold values from -0.25 to 0.25
Outputs:
- grad_down: float32 [4, 3, 320, 320], P('segment', None, ('dp', 'tm'))
- grad_up: float32 [4, 3, 640, 320], P('segment', None, ('dp', 'tm'))
- grad_skip: float32 [4, 640, 320], P('segment', ('dp', 'tm'))
The draws below stay inside these ranges and needn't reach their ends.
All inputs are finite; a program needn't handle non-finite values.
Results may differ from the reference program's by a relative error of at most 0.0035.
Values may be sent and summed in bfloat16 or wider, within the bound.
No kernel may reach another device: no remote copies, remote signals or barrier semaphores. Data moves between devices by JAX's collectives and lax.ppermute only.
A program may use at most 128 MiB of HBM per device.

```python
import math
import jax
import jax.numpy as jnp
from jax import lax

CH = 320
LAT = 4
GROUPS = 32
PIX = 64
SEGMENTS = 4
FRAMES = 16
BATCH = 16
N_SEGMENT = 4


def place_ends(entries, own_key, least, high):
    spot = [jax.random.randint(jax.random.fold_in(own_key, axis), (), 0, length) for axis, length in enumerate(entries.shape)]
    widest = entries.shape.index(max(entries.shape))
    next_to = spot[:widest] + [(spot[widest] + 1) % entries.shape[widest]] + spot[widest + 1:]
    return entries.at[tuple(spot)].set(least).at[tuple(next_to)].set(high)


def block_levels(own_key, extent, split, low, top_value):
    def one(axis_at, blocks):
        draws = jax.random.uniform(jax.random.fold_in(jax.random.fold_in(own_key, 6), axis_at), (blocks,), jnp.float32, low / len(split), top_value / len(split))
        return jnp.repeat(jnp.exp(draws), extent[axis_at] // blocks).reshape((-1,) + (1,) * (len(extent) - axis_at - 1))

    level = one(*split[0])
    for cut in split[1:]:
        level = level * one(*cut)
    return level


def centred(own_key, shape, deviation, limit, shards=(), held_as=jnp.bfloat16):
    values = jax.random.normal(own_key, shape, jnp.float32) * deviation
    if len(shards) > 0:
        values = block_levels(own_key, shape, shards, -0.22, 0.18) * values
    return jnp.clip(values, min=-limit, max=limit).astype(held_as)


def setup_inputs(seed: int = 0) -> dict:
    key_of = jax.random.split(jax.random.key(seed), 9)
    return {
        "latents": centred(key_of[0], (BATCH, FRAMES, LAT, PIX), 1.0, 6.0, ((0, 8), (1, 8))),
        "timesteps": place_ends(jax.random.randint(key_of[1], (BATCH,), 0, 1000), jax.random.fold_in(key_of[1], 1), 0, 999).astype(jnp.int32),
        "seeds": place_ends(jax.random.randint(key_of[2], (BATCH,), 0, 1073741824), jax.random.fold_in(key_of[2], 1), 0, 1073741823).astype(jnp.int32),
        "in_weight": centred(key_of[3], (LAT, CH), LAT ** -0.5, 3.0),
        "out_weight": centred(key_of[4], (CH, LAT), CH ** -0.5, 0.3125),
        "down_weight": centred(key_of[5], (SEGMENTS, 3, CH, CH), (3 * CH) ** -0.5, 0.1875, ((0, 4),)),
        "up_weight": centred(key_of[6], (SEGMENTS, 3, 2 * CH, CH), (6 * CH) ** -0.5, 0.125, ((0, 4),)),
        "skip_weight": centred(key_of[7], (SEGMENTS, 2 * CH, CH), (2 * CH) ** -0.5, 0.25, ((0, 4),)),
    }


def mix_bits(value):
    value = value ^ lax.shift_right_logical(value, jnp.int32(16))
    value = value * -2048144789
    value = value ^ lax.shift_right_logical(value, jnp.int32(13))
    value = value * -1028477387
    value = value ^ lax.shift_right_logical(value, jnp.int32(16))
    return value

def noise_field(seed_value, frame_start, frame_count, lat_dim, pix_dim):
    frame_ids = frame_start + jnp.arange(frame_count, dtype=jnp.int32)
    lat_ids = jnp.arange(lat_dim, dtype=jnp.int32)
    pix_ids = jnp.arange(pix_dim, dtype=jnp.int32)
    index = (frame_ids[:, None, None] * lat_dim + lat_ids[None, :, None]) * pix_dim + pix_ids[None, None, :]
    salted = seed_value * -1640531535
    first = mix_bits(index * 2 + salted)
    second = mix_bits(index * 2 + 1 + salted)
    unit_a = (lax.shift_right_logical(first, jnp.int32(8)).astype(jnp.float32) + 0.5) / 16777216.0
    unit_b = (lax.shift_right_logical(second, jnp.int32(8)).astype(jnp.float32) + 0.5) / 16777216.0
    return jnp.sqrt(-2.0 * jnp.log(unit_a)) * jnp.cos(2.0 * math.pi * unit_b)

def plan(step_value):
    theta = step_value.astype(jnp.float32) * (0.5 * math.pi / 1000.0)
    return (jnp.cos(theta), jnp.sin(theta))

def time_embedding(step_value, channels):
    half = channels // 2
    frequency = jnp.exp(-math.log(10000.0) * jnp.arange(half, dtype=jnp.float32) / half)
    phase = step_value.astype(jnp.float32) * frequency
    return jnp.concatenate([jnp.sin(phase), jnp.cos(phase)])

def project_in(noisy, in_weight):
    frames, lat_dim, pix_dim = noisy.shape
    flat = jnp.transpose(noisy, (0, 2, 1)).reshape(frames * pix_dim, lat_dim)
    result = jnp.dot(flat, in_weight, preferred_element_type=jnp.float32)
    return result.reshape(frames, pix_dim, -1).astype(jnp.bfloat16)

def group_norm(values, groups):
    frames, pixels, channels = values.shape
    grouped = values.reshape(frames, pixels, groups, channels // groups)
    center = lax.optimization_barrier(jnp.mean(grouped, axis=(1, 3), keepdims=True))
    spread = lax.optimization_barrier(jnp.mean((grouped - center) ** 2, axis=(1, 3), keepdims=True))
    return ((grouped - center) * lax.rsqrt(spread + 1e-05)).reshape(frames, pixels, channels)

def act_down(values, embedding):
    return jax.nn.silu(group_norm(values, GROUPS) + embedding)

def act_up(values):
    return jax.nn.silu(group_norm(values, GROUPS))

def stack_taps(padded):
    frames = padded.shape[0] - 2
    stacked = jnp.concatenate([padded[tap:tap + frames] for tap in range(3)], axis=-1)
    return stacked.reshape(frames * padded.shape[1], 3 * padded.shape[2])

def conv_fwd(padded, weight):
    frames = padded.shape[0] - 2
    result = jnp.dot(stack_taps(padded), weight.reshape(3 * weight.shape[1], weight.shape[2]), preferred_element_type=jnp.float32)
    return result.reshape(frames, padded.shape[1], weight.shape[2])

def conv_back(grad_out, weight):
    frames, pixels, cout = grad_out.shape
    cin = weight.shape[1]
    parts = lax.dot_general(grad_out.reshape(frames * pixels, cout), weight.reshape(3 * cin, cout), (((1,), (1,)), ((), ())), preferred_element_type=jnp.float32)
    parts = parts.reshape(frames, pixels, 3, cin)
    result = jnp.zeros((frames + 2, pixels, cin), jnp.float32)
    for tap in range(3):
        result = result.at[tap:tap + frames].add(parts[:, :, tap])
    return result

def conv_wgrad(padded, grad_out):
    cout = grad_out.shape[2]
    result = lax.dot_general(stack_taps(padded), grad_out.reshape(-1, cout), (((0,), (0,)), ((), ())), preferred_element_type=jnp.float32)
    return result.reshape(3, padded.shape[2], cout)

def flat_wgrad(joined, grad_out):
    return lax.dot_general(joined.reshape(-1, joined.shape[2]), grad_out.reshape(-1, grad_out.shape[2]), (((0,), (0,)), ((), ())), preferred_element_type=jnp.float32)

def pad_frames(values):
    return jnp.pad(values, ((1, 1), (0, 0), (0, 0)))

def reference(latents, timesteps, seeds, in_weight, out_weight, down_weight, up_weight, skip_weight):
    elements = BATCH * FRAMES * LAT * PIX
    loss_scale = 64.0 / math.sqrt(elements)
    out_wide = out_weight.astype(jnp.float32).T

    def one_clip(carry, item):
        grad_down, grad_up, grad_skip = carry
        clip, step_value, seed_value = item
        noise = noise_field(seed_value, jnp.int32(0), FRAMES, LAT, PIX)
        coef_a, coef_s = plan(step_value)
        noisy = (coef_a * clip.astype(jnp.float32) + coef_s * noise).astype(jnp.bfloat16)
        current = project_in(noisy, in_weight)
        embedding = time_embedding(step_value, CH)
        down_saved = []
        skips = []
        for segment in range(N_SEGMENT):
            activated = act_down(current.astype(jnp.float32), embedding).astype(jnp.bfloat16)
            padded = pad_frames(activated)
            down_saved.append((current, padded))
            current = (current.astype(jnp.float32) + conv_fwd(padded, down_weight[segment])).astype(jnp.bfloat16)
            skips.append(current)
        up_saved = [None] * N_SEGMENT
        below = skips[N_SEGMENT - 1]
        for segment in reversed(range(N_SEGMENT)):
            joined = jnp.concatenate([below, skips[segment]], axis=-1)
            activated = act_up(joined.astype(jnp.float32)).astype(jnp.bfloat16)
            padded = pad_frames(activated)
            shortcut = jnp.dot(joined.reshape(-1, 2 * CH), skip_weight[segment], preferred_element_type=jnp.float32).reshape(FRAMES, PIX, CH)
            below = (conv_fwd(padded, up_weight[segment]) + shortcut).astype(jnp.bfloat16)
            up_saved[segment] = (joined, padded)
        predicted = jnp.dot(below.reshape(-1, CH), out_weight, preferred_element_type=jnp.float32).reshape(FRAMES, PIX, LAT)
        errors = predicted - jnp.transpose(noise, (0, 2, 1))
        cotangent = jnp.dot((errors * loss_scale).reshape(-1, LAT), out_wide, preferred_element_type=jnp.float32, precision=lax.Precision.HIGHEST)
        cotangent = cotangent.reshape(FRAMES, PIX, CH).astype(jnp.bfloat16)
        skip_grads = [None] * N_SEGMENT
        for segment in range(N_SEGMENT):
            joined, padded = up_saved[segment]
            grad_padded = conv_back(cotangent, up_weight[segment])
            grad_up = grad_up.at[segment].add(conv_wgrad(padded, cotangent))
            grad_skip = grad_skip.at[segment].add(flat_wgrad(joined, cotangent))
            through = lax.dot_general(cotangent.reshape(-1, CH), skip_weight[segment], (((1,), (1,)), ((), ())), preferred_element_type=jnp.float32).reshape(FRAMES, PIX, 2 * CH)
            norm_grad = jax.vjp(act_up, joined.astype(jnp.float32))[1](grad_padded[1:-1])[0]
            grad_joined = (norm_grad + through).astype(jnp.bfloat16)
            cotangent = grad_joined[..., :CH]
            skip_grads[segment] = grad_joined[..., CH:]
        for segment in reversed(range(N_SEGMENT)):
            inputs, padded = down_saved[segment]
            grad_out = (skip_grads[segment].astype(jnp.float32) + cotangent.astype(jnp.float32)).astype(jnp.bfloat16)
            grad_padded = conv_back(grad_out, down_weight[segment])
            grad_down = grad_down.at[segment].add(conv_wgrad(padded, grad_out))
            norm_grad = jax.vjp(lambda values: act_down(values, embedding), inputs.astype(jnp.float32))[1](grad_padded[1:-1])[0]
            cotangent = (grad_out.astype(jnp.float32) + norm_grad).astype(jnp.bfloat16)
        return ((grad_down, grad_up, grad_skip), None)
    start = (jnp.zeros((N_SEGMENT, 3, CH, CH), jnp.float32), jnp.zeros((N_SEGMENT, 3, 2 * CH, CH), jnp.float32), jnp.zeros((N_SEGMENT, 2 * CH, CH), jnp.float32))
    final, unused = lax.scan(one_clip, start, (latents, timesteps, seeds))
    grad_down, grad_up, grad_skip = final
    return (grad_down, grad_up, grad_skip)
```

```python
import functools
import math

import jax
import jax.numpy as jnp
import numpy as np
from jax import lax
from jax.experimental import pallas as pl
from jax.experimental.pallas import tpu as pltpu
from jax.sharding import Mesh
from jax.sharding import PartitionSpec as P

CH = 320
GROUPS = 32
SEGS = 4
TOK = 1024
FRAMES = 16
LANES = 128
TILES = TOK // LANES
ROWS = 32
BF = jnp.bfloat16
F32 = jnp.float32
DOWN_SEL = 80
UP_SEL = 160


def mix_bits(value):
    value = value ^ lax.shift_right_logical(value, jnp.int32(16))
    value = value * -2048144789
    value = value ^ lax.shift_right_logical(value, jnp.int32(13))
    value = value * -1028477387
    value = value ^ lax.shift_right_logical(value, jnp.int32(16))
    return value


def noise_field(seed_value, lat_dim, pix_dim):
    lat_ids = lax.broadcasted_iota(jnp.int32, (lat_dim, pix_dim * FRAMES), 0)
    tokens = lax.broadcasted_iota(jnp.int32, (lat_dim, pix_dim * FRAMES), 1)
    frame_ids = tokens % FRAMES
    pix_ids = tokens // FRAMES
    index = (frame_ids * lat_dim + lat_ids) * pix_dim + pix_ids
    salted = seed_value * -1640531535
    first = mix_bits(index * 2 + salted)
    second = mix_bits(index * 2 + 1 + salted)
    unit_a = (lax.shift_right_logical(first, jnp.int32(8)).astype(F32) + 0.5) / 16777216.0
    unit_b = (lax.shift_right_logical(second, jnp.int32(8)).astype(F32) + 0.5) / 16777216.0
    return jnp.sqrt(-2.0 * jnp.log(unit_a)) * jnp.cos(2.0 * math.pi * unit_b)


def time_embedding(step_value, channels):
    half = channels // 2
    frequency = jnp.exp(-math.log(10000.0) * jnp.arange(half, dtype=F32) / half)
    phase = step_value.astype(F32) * frequency
    return jnp.concatenate([jnp.sin(phase), jnp.cos(phase)])


def group_matrix(size):
    ids = np.arange(CH) // size
    return (ids[:, None] == ids[None, :]).astype(np.float32)


def dot(a, b):
    return jnp.dot(a, b, preferred_element_type=F32)


def dot_nt(a, b):
    return lax.dot_general(a, b, (((1,), (1,)), ((), ())), preferred_element_type=F32)


def tile(j):
    return slice(j * LANES, (j + 1) * LANES)


def row_block(r):
    return pl.ds(pl.multiple_of(r * ROWS, ROWS), ROWS)


def fold(value):
    for step in (16, 32, 64):
        value = value + pltpu.roll(value, step, 1)
    return value


def group_sums(group, values, parts):
    pieces = []
    for value in values:
        rest = value
        for _ in range(parts):
            piece = rest.astype(BF)
            pieces.append(piece)
            rest = rest - piece.astype(F32)
    sums = dot(group, jnp.concatenate(pieces, axis=1))
    out = []
    for i in range(len(values)):
        total = sums[:, tile(i * parts)]
        for q in range(1, parts):
            total = total + sums[:, tile(i * parts + q)]
        out.append(fold(total))
    return out


def gn_stats(x_at, group, size, m_scr, q_scr, mean_at, rstd_at):
    def body(r, carry):
        rows = row_block(r)
        parts = [x_at(rows, tile(j)) for j in range(TILES)]
        total = parts[0]
        for p in parts[1:]:
            total = total + p
        mid = total * (1.0 / TILES)
        square = None
        for p in parts:
            d = p - mid
            square = d * d if square is None else square + d * d
        m_scr[rows, :] = mid
        q_scr[rows, :] = square
        return carry

    lax.fori_loop(0, CH // ROWS, body, 0)
    mid = m_scr[...]
    (mean,) = group_sums(group, [mid], 3)
    mean = mean * (1.0 / (8 * size))
    away = mid - mean
    (spread,) = group_sums(group, [q_scr[...] + (TILES * 1.0) * away * away], 2)
    mean_at[...] = mean
    rstd_at[...] = lax.rsqrt(spread * (1.0 / (64 * size)) + 1e-05)


def frame_masks():
    lane = lax.broadcasted_iota(jnp.int32, (ROWS, LANES), 1) % FRAMES
    return lane != 0, lane != FRAMES - 1


def earlier(value, masks):
    return jnp.where(masks[0], pltpu.roll(value, 1, 1), 0.0).astype(BF)


def later(value, masks):
    return jnp.where(masks[1], pltpu.roll(value, LANES - 1, 1), 0.0).astype(BF)


def silu_parts(y):
    sig = 0.5 * jnp.tanh(0.5 * y) + 0.5
    return sig, y * sig


def norm_bwd(ga_ref, ga_off, x_at, group, size, mean_at, rstd_at, emb_ref, m_scr, q_scr, emit):
    def first(r, carry):
        rows = row_block(r)
        grows = pl.ds(pl.multiple_of(ga_off + r * ROWS, ROWS), ROWS)
        mean = mean_at[rows, :]
        rstd = rstd_at[rows, :]
        emb = None if emb_ref is None else emb_ref[rows, :]
        s1 = None
        s2 = None
        for j in range(TILES):
            xhat = (x_at(rows, tile(j)) - mean) * rstd
            y = xhat if emb is None else xhat + emb
            sig, act = silu_parts(y)
            dy = ga_ref[grows, tile(j)] * (sig + act * (1.0 - sig))
            ga_ref[grows, tile(j)] = dy
            s1 = dy if s1 is None else s1 + dy
            s2 = dy * xhat if s2 is None else s2 + dy * xhat
        m_scr[rows, :] = s1
        q_scr[rows, :] = s2
        return carry

    lax.fori_loop(0, CH // ROWS, first, 0)
    s1, s2 = group_sums(group, [m_scr[...], q_scr[...]], 2)
    scale = 1.0 / (64 * size)
    m_scr[...] = s1 * scale
    q_scr[...] = s2 * scale

    def second(r, carry):
        rows = row_block(r)
        grows = pl.ds(pl.multiple_of(ga_off + r * ROWS, ROWS), ROWS)
        mean = mean_at[rows, :]
        rstd = rstd_at[rows, :]
        m1 = m_scr[rows, :]
        m2 = q_scr[rows, :]
        for j in range(TILES):
            xhat = (x_at(rows, tile(j)) - mean) * rstd
            emit(rows, tile(j), rstd * (ga_ref[grows, tile(j)] - m1 - xhat * m2))
        return carry

    lax.fori_loop(0, CH // ROWS, second, 0)


def conv_cols(body):
    def step(n, carry):
        body(pl.ds(pl.multiple_of(n * 256, 256), 256))
        return carry

    lax.fori_loop(0, TOK // 256, step, 0)


def transpose_into(dst, src, rows):
    for start in range(0, rows, LANES):
        size = min(LANES, rows - start)
        dst[:, start : start + size] = src[start : start + size, :].astype(F32).T.astype(BF)


def segment_copies(ids, own, mine, other, dest, sems):
    seg = ids[0]
    core = ids[1]
    half = mine.shape[1]
    copies = [pltpu.make_async_copy(own, dest.at[seg], sems.at[0])]
    for slot, away in enumerate((1, 3, 2)):
        s = lax.rem(seg + away, SEGS)
        for which, source, place in ((0, mine, core), (1, other, 1 - core)):
            copies.append(
                pltpu.make_async_copy(
                    source.at[slot],
                    dest.at[s, pl.ds(pl.multiple_of(place * half, 32), half), :],
                    sems.at[1 + slot * 2 + which],
                )
            )
    return copies


def down_forward_kernel(
    ids, noisy, in_t, emb, group, pick, own, mine, other,
    xs, mean, rstd, asel, wnat_out,
    wt, stack, m_scr, q_scr, sems,
):
    copies = segment_copies(ids, own, mine, other, wnat_out, sems)
    for c in copies:
        c.start()
    conv_cols(lambda cols: xs.__setitem__((0, slice(None), cols), dot(in_t[...], noisy[:, cols]).astype(BF)))
    for c in copies:
        c.wait()
    masks = frame_masks()

    def stage(s, carry):
        transpose_into(wt, wnat_out.at[s], 3 * CH)
        x_at = lambda rows, cols: xs[s, rows, cols].astype(F32)
        gn_stats(x_at, group[...], 10, m_scr, q_scr, mean.at[s], rstd.at[s])

        def act(r, c2):
            rows = row_block(r)
            mu = mean[s, rows, :]
            rs = rstd[s, rows, :]
            e = emb[rows, :]
            for j in range(TILES):
                y = (x_at(rows, tile(j)) - mu) * rs + e
                _, a = silu_parts(y)
                stack[0, rows, tile(j)] = earlier(a, masks)
                stack[1, rows, tile(j)] = a.astype(BF)
                stack[2, rows, tile(j)] = later(a, masks)
            return c2

        lax.fori_loop(0, CH // ROWS, act, 0)

        @pl.when(s == ids[0])
        def _():
            asel[...] = dot(pick[...], stack[1]).astype(BF)

        def conv(cols):
            taps = stack[:, :, cols].reshape(3 * CH, 256)
            total = dot(wt[...], taps) + xs[s, :, cols].astype(F32)
            xs[s + 1, :, cols] = total.astype(BF)

        conv_cols(conv)
        return carry

    lax.fori_loop(0, SEGS, stage, 0)


def up_kernel(
    ids, xs, group, pick, out_t, out_wide, noise, own, mine, other,
    gu, gsk, kgrad, cgrad,
    wnat, wt, wb, stack, bsel, jsel, es, umean, urstd, ga, thru, gcur, gstack, m_scr, q_scr, sems, *, scale
):
    copies = segment_copies(ids, own, mine, other, wnat, sems)
    for c in copies:
        c.start()
    for c in copies:
        c.wait()
    masks = frame_masks()
    es[SEGS] = xs[SEGS]

    def forward(i, carry):
        s = SEGS - 1 - i
        transpose_into(wt, wnat.at[s], 8 * CH)
        for half, src in ((0, es), (1, xs)):
            x_at = lambda rows, cols: src[s + 1, rows, cols].astype(F32)
            gn_stats(x_at, group[...], 20, m_scr, q_scr, umean.at[s, half], urstd.at[s, half])

            def act(r, c2):
                rows = row_block(r)
                mu = umean[s, half, rows, :]
                rs = urstd[s, half, rows, :]
                for j in range(TILES):
                    raw = src[s + 1, rows, tile(j)]
                    y = (raw.astype(F32) - mu) * rs
                    _, a = silu_parts(y)
                    stack[0 + half, rows, tile(j)] = earlier(a, masks)
                    stack[2 + half, rows, tile(j)] = a.astype(BF)
                    stack[4 + half, rows, tile(j)] = later(a, masks)
                    stack[6 + half, rows, tile(j)] = raw
                return c2

            lax.fori_loop(0, CH // ROWS, act, 0)

        @pl.when(s == ids[0])
        def _():
            bsel[...] = dot(pick[...], stack[2:4].reshape(2 * CH, TOK)).astype(BF)
            jsel[...] = dot(pick[...], stack[6:8].reshape(2 * CH, TOK)).astype(BF)

        def conv(cols):
            es[s, :, cols] = dot(wt[...], stack[:, :, cols].reshape(8 * CH, 256)).astype(BF)

        conv_cols(conv)
        return carry

    lax.fori_loop(0, SEGS, forward, 0)

    def seed(cols):
        predicted = dot(out_t[...], es[0, :, cols])
        error = (predicted[:4] - noise[:, cols]) * scale
        total = out_wide[:, 0:1] * error[0:1, :]
        for l in range(1, 4):
            total = total + out_wide[:, l : l + 1] * error[l : l + 1, :]
        gcur[:, cols] = total.astype(BF)

    conv_cols(seed)

    def backward(s, carry):
        for k in range(3):
            wb[:, k * CH : (k + 1) * CH] = wnat[s, k * 2 * CH : (k + 1) * 2 * CH, :]

        def spread(r, c2):
            rows = row_block(r)
            for j in range(TILES):
                g = gcur[rows, tile(j)]
                g32 = g.astype(F32)
                gstack[0, rows, tile(j)] = later(g32, masks)
                gstack[1, rows, tile(j)] = g
                gstack[2, rows, tile(j)] = earlier(g32, masks)
            return c2

        lax.fori_loop(0, CH // ROWS, spread, 0)

        @pl.when(s == ids[0])
        def _():
            for k in range(3):
                gu[k] = dot_nt(bsel[...], gstack[k])
            gsk[...] = dot_nt(jsel[...], gcur[...])

        def conv(cols):
            ga[:, cols] = dot(wb[...], gstack[:, :, cols].reshape(3 * CH, 256))
            thru[:, cols] = dot(wnat[s, 6 * CH :, :], gcur[:, cols])

        conv_cols(conv)
        for half, src in ((0, es), (1, xs)):
            x_at = lambda rows, cols: src[s + 1, rows, cols].astype(F32)

            def emit(rows, cols, dx):
                if half == 0:
                    gcur[rows, cols] = (dx + thru[rows, cols]).astype(BF)
                else:
                    trows = pl.ds(pl.multiple_of(rows.start + CH, ROWS), ROWS)
                    kgrad[s, rows, cols] = (dx + thru[trows, cols]).astype(BF)

            norm_bwd(
                ga, half * CH, x_at, group[...], 20, umean.at[s, half], urstd.at[s, half], None, m_scr, q_scr, emit
            )
        return carry

    lax.fori_loop(0, SEGS, backward, 0)
    cgrad[...] = gcur[...]


def down_backward_kernel(
    ids, xs, mean, rstd, asel, wnat, emb, group, kgrad, cgrad,
    gd,
    wb, hstack, ga, ccur, m_scr, q_scr,
):
    masks = frame_masks()
    ccur[...] = cgrad[...]

    def take(s):
        def spread(r, c2):
            rows = row_block(r)
            for j in range(TILES):
                h = (kgrad[s, rows, tile(j)].astype(F32) + ccur[rows, tile(j)].astype(F32)).astype(BF)
                h32 = h.astype(F32)
                hstack[0, rows, tile(j)] = later(h32, masks)
                hstack[1, rows, tile(j)] = h
                hstack[2, rows, tile(j)] = earlier(h32, masks)
            return c2

        lax.fori_loop(0, CH // ROWS, spread, 0)

        @pl.when(s == ids[0])
        def _():
            for k in range(3):
                gd[k] = dot_nt(asel[...], hstack[k])

    def stage(i, carry):
        s = SEGS - 1 - i
        take(s)
        for k in range(3):
            wb[:, k * CH : (k + 1) * CH] = wnat[s, k * CH : (k + 1) * CH, :]

        def conv(cols):
            ga[:, cols] = dot(wb[...], hstack[:, :, cols].reshape(3 * CH, 256))

        conv_cols(conv)
        x_at = lambda rows, cols: xs[s, rows, cols].astype(F32)

        def emit(rows, cols, dx):
            ccur[rows, cols] = (hstack[1, rows, cols].astype(F32) + dx).astype(BF)

        norm_bwd(ga, 0, x_at, group[...], 10, mean.at[s], rstd.at[s], emb, m_scr, q_scr, emit)
        return carry

    lax.fori_loop(0, SEGS - 1, stage, 0)
    take(0)


VMEM = pl.BlockSpec(memory_space=pltpu.VMEM)
SMEM = pl.BlockSpec(memory_space=pltpu.SMEM)
ANY = pl.BlockSpec(memory_space=pl.ANY)
PARAMS = pltpu.CompilerParams(vmem_limit_bytes=60 * 1024 * 1024)


def shape(dims, dtype=BF):
    return jax.ShapeDtypeStruct(dims, dtype)


def run_down_forward(ids, noisy, in_t, emb, group, pick, own, mine, other):
    return pl.pallas_call(
        down_forward_kernel,
        name="down_forward",
        out_shape=(
            shape((SEGS + 1, CH, TOK)),
            shape((SEGS, CH, LANES), F32),
            shape((SEGS, CH, LANES), F32),
            shape((DOWN_SEL, TOK)),
            shape((SEGS, 3 * CH, CH)),
        ),
        in_specs=[SMEM] + [VMEM] * 5 + [ANY] * 3,
        out_specs=(VMEM,) * 5,
        scratch_shapes=[
            pltpu.VMEM((CH, 3 * CH), BF),
            pltpu.VMEM((3, CH, TOK), BF),
            pltpu.VMEM((CH, LANES), F32),
            pltpu.VMEM((CH, LANES), F32),
            pltpu.SemaphoreType.DMA((7,)),
        ],
        compiler_params=PARAMS,
    )(ids, noisy, in_t, emb, group, pick, own, mine, other)


def run_up(ids, xs, group, pick, out_t, out_wide, noise, own, mine, other, scale):
    return pl.pallas_call(
        functools.partial(up_kernel, scale=scale),
        name="up_both",
        out_shape=(
            shape((3, UP_SEL, CH), F32),
            shape((UP_SEL, CH), F32),
            shape((SEGS, CH, TOK)),
            shape((CH, TOK)),
        ),
        in_specs=[SMEM] + [VMEM] * 6 + [ANY] * 3,
        out_specs=(VMEM,) * 4,
        scratch_shapes=[
            pltpu.VMEM((SEGS, 8 * CH, CH), BF),
            pltpu.VMEM((CH, 8 * CH), BF),
            pltpu.VMEM((2 * CH, 3 * CH), BF),
            pltpu.VMEM((8, CH, TOK), BF),
            pltpu.VMEM((UP_SEL, TOK), BF),
            pltpu.VMEM((UP_SEL, TOK), BF),
            pltpu.VMEM((SEGS + 1, CH, TOK), BF),
            pltpu.VMEM((SEGS, 2, CH, LANES), F32),
            pltpu.VMEM((SEGS, 2, CH, LANES), F32),
            pltpu.VMEM((2 * CH, TOK), F32),
            pltpu.VMEM((2 * CH, TOK), F32),
            pltpu.VMEM((CH, TOK), BF),
            pltpu.VMEM((3, CH, TOK), BF),
            pltpu.VMEM((CH, LANES), F32),
            pltpu.VMEM((CH, LANES), F32),
            pltpu.SemaphoreType.DMA((7,)),
        ],
        compiler_params=PARAMS,
    )(ids, xs, group, pick, out_t, out_wide, noise, own, mine, other)


def run_down_backward(ids, xs, mean, rstd, asel, wnat, emb, group, kgrad, cgrad):
    return pl.pallas_call(
        down_backward_kernel,
        name="down_backward",
        out_shape=shape((3, DOWN_SEL, CH), F32),
        in_specs=[SMEM] + [VMEM] * 9,
        out_specs=VMEM,
        scratch_shapes=[
            pltpu.VMEM((CH, 3 * CH), BF),
            pltpu.VMEM((3, CH, TOK), BF),
            pltpu.VMEM((CH, TOK), F32),
            pltpu.VMEM((CH, TOK), BF),
            pltpu.VMEM((CH, LANES), F32),
            pltpu.VMEM((CH, LANES), F32),
        ],
        compiler_params=PARAMS,
    )(ids, xs, mean, rstd, asel, wnat, emb, group, kgrad, cgrad)


def pick_matrix(x_index, per_device, channels):
    row = lax.broadcasted_iota(jnp.int32, (16 * per_device, channels), 0)
    col = lax.broadcasted_iota(jnp.int32, (16 * per_device, channels), 1)
    core = row // (8 * per_device)
    dp = (row // per_device) % 8
    want = (dp * 8 + 2 * x_index + core) * per_device + row % per_device
    return (col == want).astype(BF)


def clip_inputs(clip, step_value, seed_value, in_weight, out_weight):
    lat_dim, pix_dim, frames = clip.shape
    noise = noise_field(seed_value, lat_dim, pix_dim)
    theta = step_value.astype(F32) * (0.5 * math.pi / 1000.0)
    noisy = (
        jnp.cos(theta) * clip.reshape(lat_dim, pix_dim * frames).astype(F32) + jnp.sin(theta) * noise
    ).astype(BF)
    noisy = jnp.pad(noisy, ((0, 16 - lat_dim), (0, 0)))
    in_t = jnp.pad(in_weight.T, ((0, 0), (0, 16 - lat_dim)))
    out_t = jnp.pad(out_weight.T, ((0, 16 - lat_dim), (0, 0)))
    emb = jnp.broadcast_to(time_embedding(step_value, CH)[:, None], (CH, LANES))
    return noise, noisy, in_t, out_t, emb


def swap_core(value):
    return lax.ppermute(value, "core", [(0, 1), (1, 0)])


def from_segment(value, away):
    return lax.ppermute(value, "segment", [((i + away) % SEGS, i) for i in range(SEGS)])


def gather_sections(half):
    mine = jnp.stack([from_segment(half, away) for away in (1, 3, 2)])
    return mine, swap_core(mine)


def share(total, core):
    keep = lax.dynamic_index_in_dim(total, core, 0, keepdims=False)
    give = lax.dynamic_index_in_dim(total, 1 - core, 0, keepdims=False)
    both = keep + swap_core(give)
    parts = lax.all_to_all(both, "dp", 0, 0, tiled=True)
    return jnp.sum(parts, axis=0)


def local(latents, timesteps, seeds, in_weight, out_weight, down_weight, up_weight, skip_weight):
    seg = lax.axis_index("segment")
    core = lax.axis_index("core")
    x_index = lax.axis_index("x")
    elements = 16 * FRAMES * 4 * 64
    scale = 64.0 / math.sqrt(elements)
    ids = jnp.stack([seg, core]).astype(jnp.int32)
    down_nat = down_weight[0].reshape(3 * CH, CH)
    up_nat = jnp.concatenate([up_weight[0].reshape(6 * CH, CH), skip_weight[0]], axis=0)
    d_half = lax.dynamic_slice_in_dim(down_nat, core * (3 * CH // 2), 3 * CH // 2, 0)
    u_half = lax.dynamic_slice_in_dim(up_nat, core * 4 * CH, 4 * CH, 0)
    d_mine, d_other = gather_sections(d_half)
    u_mine, u_other = gather_sections(u_half)

    clips = lax.all_gather(latents, ("x", "core"), axis=0)
    clip = lax.dynamic_index_in_dim(clips, core, 1, keepdims=False)
    clip = jnp.transpose(clip.reshape(FRAMES, 4, 64), (1, 2, 0))
    step_value = lax.dynamic_index_in_dim(timesteps, core, 0, keepdims=False)
    seed_value = lax.dynamic_index_in_dim(seeds, core, 0, keepdims=False)
    noise, noisy, in_t, out_t, emb = clip_inputs(clip, step_value, seed_value, in_weight, out_weight)
    g10 = jnp.asarray(group_matrix(10), BF)
    g20 = jnp.asarray(group_matrix(20), BF)

    xs, mean, rstd, asel, wnat = run_down_forward(
        ids, noisy, in_t, emb, g10, pick_matrix(x_index, 5, CH), down_nat, d_mine, d_other
    )
    gu, gsk, kgrad, cgrad = run_up(
        ids, xs, g20, pick_matrix(x_index, 10, 2 * CH), out_t, out_weight.astype(F32), noise,
        up_nat, u_mine, u_other, scale,
    )
    up_all = jnp.concatenate([gu, gsk[None]], axis=0).reshape(4, 2, 8, 10, CH)
    up_all = jnp.transpose(up_all, (1, 2, 0, 3, 4)).reshape(2, 8, 40 * CH)
    up_sum = share(up_all, core).reshape(4, 10, CH)
    gd = run_down_backward(ids, xs, mean, rstd, asel, wnat, emb, g10, kgrad, cgrad)
    down_all = jnp.transpose(gd.reshape(3, 2, 8, 5, CH), (1, 2, 0, 3, 4)).reshape(2, 8, 15 * CH)
    down_sum = share(down_all, core).reshape(3, 5, CH)
    return down_sum[None], up_sum[:3][None], up_sum[3][None]


def solution(mesh):
    devices = mesh.devices
    grid = Mesh(devices.reshape(devices.shape[0], devices.shape[1], 4, 2), ("dp", "segment", "x", "core"))
    tm = ("x", "core")
    return jax.shard_map(
        local,
        mesh=grid,
        in_specs=(
            P("dp", tm, None, None),
            P("dp"),
            P("dp"),
            P(),
            P(),
            P("segment", None, None, None),
            P("segment", None, None, None),
            P("segment", None, None),
        ),
        out_specs=(
            P("segment", None, ("dp",) + tm, None),
            P("segment", None, ("dp",) + tm, None),
            P("segment", ("dp",) + tm, None),
        ),
        check_vma=False,
    )
```

```python
import functools
import math

import jax
import jax.numpy as jnp
import numpy as np
from jax import lax
from jax.experimental import pallas as pl
from jax.experimental.pallas import tpu as pltpu
from jax.sharding import Mesh
from jax.sharding import PartitionSpec as P

CH = 320
GROUPS = 32
SEGS = 4
TOK = 1024
FRAMES = 16
LANES = 128
TILES = TOK // LANES
ROWS = 32
BF = jnp.bfloat16
F32 = jnp.float32
DOWN_SEL = 80
UP_SEL = 160


def mix_bits(value):
    value = value ^ lax.shift_right_logical(value, jnp.int32(16))
    value = value * -2048144789
    value = value ^ lax.shift_right_logical(value, jnp.int32(13))
    value = value * -1028477387
    value = value ^ lax.shift_right_logical(value, jnp.int32(16))
    return value


def noise_field(seed_value, lat_dim, pix_dim):
    lat_ids = lax.broadcasted_iota(jnp.int32, (lat_dim, pix_dim * FRAMES), 0)
    tokens = lax.broadcasted_iota(jnp.int32, (lat_dim, pix_dim * FRAMES), 1)
    frame_ids = tokens % FRAMES
    pix_ids = tokens // FRAMES
    index = (frame_ids * lat_dim + lat_ids) * pix_dim + pix_ids
    salted = seed_value * -1640531535
    first = mix_bits(index * 2 + salted)
    second = mix_bits(index * 2 + 1 + salted)
    unit_a = (lax.shift_right_logical(first, jnp.int32(8)).astype(F32) + 0.5) / 16777216.0
    unit_b = (lax.shift_right_logical(second, jnp.int32(8)).astype(F32) + 0.5) / 16777216.0
    return jnp.sqrt(-2.0 * jnp.log(unit_a)) * jnp.cos(2.0 * math.pi * unit_b)


def time_embedding(step_value, channels):
    half = channels // 2
    frequency = jnp.exp(-math.log(10000.0) * jnp.arange(half, dtype=F32) / half)
    phase = step_value.astype(F32) * frequency
    return jnp.concatenate([jnp.sin(phase), jnp.cos(phase)])


def group_matrix(size):
    ids = np.arange(CH) // size
    return (ids[:, None] == ids[None, :]).astype(np.float32)


def dot(a, b):
    return jnp.dot(a, b, preferred_element_type=F32)


def dot_nt(a, b):
    return lax.dot_general(a, b, (((1,), (1,)), ((), ())), preferred_element_type=F32)


def tile(j):
    return slice(j * LANES, (j + 1) * LANES)


def row_block(r):
    return pl.ds(pl.multiple_of(r * ROWS, ROWS), ROWS)


def fold(value):
    for step in (16, 32, 64):
        value = value + pltpu.roll(value, step, 1)
    return value


def group_sums(group, values, parts):
    pieces = []
    for value in values:
        rest = value
        for _ in range(parts):
            piece = rest.astype(BF)
            pieces.append(piece)
            rest = rest - piece.astype(F32)
    sums = dot(group, jnp.concatenate(pieces, axis=1))
    out = []
    for i in range(len(values)):
        total = sums[:, tile(i * parts)]
        for q in range(1, parts):
            total = total + sums[:, tile(i * parts + q)]
        out.append(fold(total))
    return out


def gn_stats(x_at, group, size, m_scr, q_scr, mean_at, rstd_at):
    def body(r, carry):
        rows = row_block(r)
        parts = [x_at(rows, tile(j)) for j in range(TILES)]
        total = parts[0]
        for p in parts[1:]:
            total = total + p
        mid = total * (1.0 / TILES)
        square = None
        for p in parts:
            d = p - mid
            square = d * d if square is None else square + d * d
        m_scr[rows, :] = mid
        q_scr[rows, :] = square
        return carry

    lax.fori_loop(0, CH // ROWS, body, 0)
    mid = m_scr[...]
    (mean,) = group_sums(group, [mid], 3)
    mean = mean * (1.0 / (8 * size))
    away = mid - mean
    (spread,) = group_sums(group, [q_scr[...] + (TILES * 1.0) * away * away], 2)
    mean_at[...] = mean
    rstd_at[...] = lax.rsqrt(spread * (1.0 / (64 * size)) + 1e-05)


def shift_matrix():
    lane = np.arange(LANES)
    out = np.zeros((LANES, 2 * LANES), np.float32)
    for l in lane:
        if l % FRAMES != 0:
            out[l - 1, l] = 1.0
        if l % FRAMES != FRAMES - 1:
            out[l + 1, LANES + l] = 1.0
    return out


def neighbours(value, shift):
    both = dot(value, shift).astype(BF)
    return both[:, :LANES], both[:, LANES:]


def silu_parts(y):
    sig = 0.5 * jnp.tanh(0.5 * y) + 0.5
    return sig, y * sig


def norm_bwd(ga_ref, ga_off, x_at, group, size, mean_at, rstd_at, emb_ref, m_scr, q_scr, emit):
    def first(r, carry):
        rows = row_block(r)
        grows = pl.ds(pl.multiple_of(ga_off + r * ROWS, ROWS), ROWS)
        mean = mean_at[rows, :]
        rstd = rstd_at[rows, :]
        emb = None if emb_ref is None else emb_ref[rows, :]
        s1 = None
        s2 = None
        for j in range(TILES):
            xhat = (x_at(rows, tile(j)) - mean) * rstd
            y = xhat if emb is None else xhat + emb
            sig, act = silu_parts(y)
            dy = ga_ref[grows, tile(j)] * (sig + act * (1.0 - sig))
            ga_ref[grows, tile(j)] = dy
            s1 = dy if s1 is None else s1 + dy
            s2 = dy * xhat if s2 is None else s2 + dy * xhat
        m_scr[rows, :] = s1
        q_scr[rows, :] = s2
        return carry

    lax.fori_loop(0, CH // ROWS, first, 0)
    s1, s2 = group_sums(group, [m_scr[...], q_scr[...]], 2)
    scale = 1.0 / (64 * size)
    m_scr[...] = s1 * scale
    q_scr[...] = s2 * scale

    def second(r, carry):
        rows = row_block(r)
        grows = pl.ds(pl.multiple_of(ga_off + r * ROWS, ROWS), ROWS)
        mean = mean_at[rows, :]
        rstd = rstd_at[rows, :]
        m1 = m_scr[rows, :]
        m2 = q_scr[rows, :]
        for j in range(TILES):
            xhat = (x_at(rows, tile(j)) - mean) * rstd
            emit(rows, tile(j), rstd * (ga_ref[grows, tile(j)] - m1 - xhat * m2))
        return carry

    lax.fori_loop(0, CH // ROWS, second, 0)


MAIN = 256
REST = CH - MAIN


def copy_bytes(ref, sem):
    return pltpu.make_async_copy(ref, ref, sem)


def section_of(seg, slot):
    return lax.rem(seg + (1, 3, 2)[slot], SEGS)


def start_down_copies(ids, own, parts, dest, sems):
    half = 3 * CH // 2
    pltpu.make_async_copy(own, dest.at[ids[0]], sems.at[ids[0]]).start()
    for slot in range(3):
        s = section_of(ids[0], slot)
        for source, place in ((parts[slot], ids[1]), (parts[3 + slot], 1 - ids[1])):
            rows = pl.ds(pl.multiple_of(place * half, 32), half)
            pltpu.make_async_copy(source, dest.at[s, rows, :], sems.at[s]).start()


def start_up_copies(ids, own_up, own_skip, parts, dest, sems):
    half = CH // 2
    seg = ids[0]
    for k in range(4):
        source = own_up.at[k] if k < 3 else own_skip
        pltpu.make_async_copy(source, dest.at[seg, :, k * 640 : (k + 1) * 640], sems.at[seg]).start()
    for slot in range(3):
        s = section_of(seg, slot)
        for source, place in ((parts[slot], ids[1]), (parts[3 + slot], 1 - ids[1])):
            rows = pl.ds(pl.multiple_of(place * half, 32), half)
            for k in range(4):
                pltpu.make_async_copy(
                    source.at[k], dest.at[s, rows, k * 640 : (k + 1) * 640], sems.at[s]
                ).start()


def activate(x_at, mean_at, rstd_at, emb_ref, put):
    def act(r, carry):
        rows = row_block(r)
        mu = mean_at[rows, :]
        rs = rstd_at[rows, :]
        e = None if emb_ref is None else emb_ref[rows, :]
        for j in range(TILES):
            y = (x_at(rows, tile(j)) - mu) * rs
            if e is not None:
                y = y + e
            put(rows, tile(j), silu_parts(y)[1].astype(BF))
        return carry

    lax.fori_loop(0, CH // ROWS, act, 0)


def down_forward_kernel(
    ids, noisy, in_t, emb, g10, g20, shift, pick, own, p0, p1, p2, q0, q1, q2,
    xs, mean, rstd, asel, wnat, dstack, dmean, drstd,
    wt, stack, m_scr, q_scr, sems,
):
    start_down_copies(ids, own, (p0, p1, p2, q0, q1, q2), wnat, sems)
    xs[0] = dot(in_t[...], noisy[...]).astype(BF)

    def stage(s, carry):
        x_at = lambda rows, cols: xs[s, rows, cols].astype(F32)
        gn_stats(x_at, g10[...], 10, m_scr, q_scr, mean.at[s], rstd.at[s])

        def put(rows, cols, a):
            stack[1, rows, cols] = a

        activate(x_at, mean.at[s], rstd.at[s], emb, put)
        for j in range(TILES):
            before, after = neighbours(stack[1, :, tile(j)], shift[...])
            stack[0, :, tile(j)] = before
            stack[2, :, tile(j)] = after

        @pl.when(s == ids[0])
        def _():
            asel[...] = dot(pick[...], stack[1]).astype(BF)

        copy_bytes(wnat.at[s], sems.at[s]).wait()
        for begin in range(0, 3 * CH, LANES):
            size = min(LANES, 3 * CH - begin)
            wt[:, begin : begin + size] = wnat[s, begin : begin + size, :].T
        total = dot(wt[...], stack[...].reshape(3 * CH, TOK)) + xs[s].astype(F32)
        xs[s + 1] = total.astype(BF)
        return carry

    lax.fori_loop(0, SEGS, stage, 0)

    def ahead(s, carry):
        x_at = lambda rows, cols: xs[s + 1, rows, cols].astype(F32)
        gn_stats(x_at, g20[...], 20, m_scr, q_scr, dmean.at[s], drstd.at[s])

        def put(rows, cols, a):
            dstack[s, 1, rows, cols] = a

        activate(x_at, dmean.at[s], drstd.at[s], None, put)
        for j in range(TILES):
            before, after = neighbours(dstack[s, 1, :, tile(j)], shift[...])
            dstack[s, 0, :, tile(j)] = before
            dstack[s, 2, :, tile(j)] = after
        dstack[s, 3] = xs[s + 1]
        return carry

    lax.fori_loop(0, SEGS, ahead, 0)


def spread_grad(value, shift, gstack):
    for j in range(TILES):
        g = value(tile(j))
        before, after = neighbours(g, shift)
        for k, part in ((0, after), (1, g), (2, before)):
            gstack[k * MAIN : (k + 1) * MAIN, tile(j)] = part[:MAIN]
            gstack[3 * MAIN + k * REST : 3 * MAIN + (k + 1) * REST, tile(j)] = part[MAIN:]


def up_kernel(
    ids, xs, dmean, drstd, g20, shift, pick, out_t, out_wide, noise,
    dstack, own_up, own_skip, p0, p1, p2, q0, q1, q2,
    gu, kgrad, cgrad,
    wt, wb, stack, bsel, jsel, es, emean, erstd, ga, thru, gcur, gstack, m_scr, q_scr, sems, dsems, *, scale
):
    start_up_copies(ids, own_up, own_skip, (p0, p1, p2, q0, q1, q2), wt, sems)

    def fetch(s):
        slot = lax.rem(s, 2)
        for k in range(4):
            pltpu.make_async_copy(dstack.at[s, k], stack.at[slot, k, 1], dsems.at[slot, k]).start()

    fetch(jnp.int32(SEGS - 1))
    es[SEGS] = xs[SEGS]

    def forward(i, carry):
        s = SEGS - 1 - i
        slot = lax.rem(s, 2)

        @pl.when(s > 0)
        def _():
            fetch(s - 1)

        x_at = lambda rows, cols: es[s + 1, rows, cols].astype(F32)
        gn_stats(x_at, g20[...], 20, m_scr, q_scr, emean.at[s], erstd.at[s])

        def put(rows, cols, a):
            stack[slot, 1, 0, rows, cols] = a

        activate(x_at, emean.at[s], erstd.at[s], None, put)
        for j in range(TILES):
            before, after = neighbours(stack[slot, 1, 0, :, tile(j)], shift[...])
            stack[slot, 0, 0, :, tile(j)] = before
            stack[slot, 2, 0, :, tile(j)] = after
        stack[slot, 3, 0] = es[s + 1]
        for k in range(4):
            pltpu.make_async_copy(dstack.at[s, k], stack.at[slot, k, 1], dsems.at[slot, k]).wait()

        @pl.when(s == ids[0])
        def _():
            bsel[...] = dot(pick[...], stack[slot, 1].reshape(2 * CH, TOK)).astype(BF)
            jsel[...] = dot(pick[...], stack[slot, 3].reshape(2 * CH, TOK)).astype(BF)

        copy_bytes(wt.at[s], sems.at[s]).wait()
        es[s] = dot(wt[s], stack[slot].reshape(8 * CH, TOK)).astype(BF)
        return carry

    lax.fori_loop(0, SEGS, forward, 0)

    predicted = dot(out_t[...], es[0])
    thru[0:4, :] = (predicted[:4] - noise[...]) * scale

    def seed(r, carry):
        rows = row_block(r)
        for j in range(TILES):
            total = out_wide[rows, 0:1] * thru[0:1, tile(j)]
            for l in range(1, 4):
                total = total + out_wide[rows, l : l + 1] * thru[l : l + 1, tile(j)]
            gcur[rows, tile(j)] = total.astype(BF)
        return carry

    lax.fori_loop(0, CH // ROWS, seed, 0)

    def backward(s, carry):
        for k in range(3):
            for b in range(2):
                wb[:, k * MAIN + b * LANES : k * MAIN + (b + 1) * LANES] = wt[
                    s, b * LANES : (b + 1) * LANES, k * 640 : (k + 1) * 640
                ].T
        tops = [wt[s, MAIN:, k * 640 : (k + 1) * 640] for k in range(3)]
        wb[:, 3 * MAIN : 3 * MAIN + LANES] = jnp.concatenate(tops[:2], axis=0).T
        wb[:, 3 * MAIN + LANES : 3 * CH] = tops[2].T
        for b in range(2):
            wb[:, 1024 + b * LANES : 1024 + (b + 1) * LANES] = wt[s, b * LANES : (b + 1) * LANES, 1920:].T
        wb[:, 1024 + MAIN : 1024 + CH] = wt[s, MAIN:, 1920:].T
        spread_grad(lambda cols: gcur[:, cols], shift[...], gstack)

        @pl.when(s == ids[0])
        def _():
            gu[:, : 3 * CH] = dot_nt(bsel[...], gstack[...])
            gu[:, 3 * CH :] = dot_nt(jsel[...], gcur[...])

        ga[...] = dot(wb[:, : 3 * CH], gstack[...])
        thru[...] = dot(wb[:, 1024 : 1024 + CH], gcur[...])

        def emit_e(rows, cols, dx):
            gcur[rows, cols] = (dx + thru[rows, cols]).astype(BF)

        def emit_d(rows, cols, dx):
            trows = pl.ds(pl.multiple_of(rows.start + CH, ROWS), ROWS)
            kgrad[s, rows, cols] = (dx + thru[trows, cols]).astype(BF)

        e_at = lambda rows, cols: es[s + 1, rows, cols].astype(F32)
        d_at = lambda rows, cols: xs[s + 1, rows, cols].astype(F32)
        norm_bwd(ga, 0, e_at, g20[...], 20, emean.at[s], erstd.at[s], None, m_scr, q_scr, emit_e)
        norm_bwd(ga, CH, d_at, g20[...], 20, dmean.at[s], drstd.at[s], None, m_scr, q_scr, emit_d)
        return carry

    lax.fori_loop(0, SEGS, backward, 0)
    cgrad[...] = gcur[...]


def down_backward_kernel(
    ids, xs, mean, rstd, asel, wnat, emb, g10, shift, kgrad, cgrad,
    gd,
    wb, hstack, hcur, ga, ccur, m_scr, q_scr,
):
    ccur[...] = cgrad[...]

    def take(s):
        def value(cols):
            h = (kgrad[s, :, cols].astype(F32) + ccur[:, cols].astype(F32)).astype(BF)
            hcur[:, cols] = h
            return h

        spread_grad(value, shift[...], hstack)

        @pl.when(s == ids[0])
        def _():
            gd[...] = dot_nt(asel[...], hstack[...])

    def stage(i, carry):
        s = SEGS - 1 - i
        take(s)
        for k in range(3):
            wb[:, k * MAIN : (k + 1) * MAIN] = wnat[s, k * CH : (k + 1) * CH, :MAIN]
            wb[:, 3 * MAIN + k * REST : 3 * MAIN + (k + 1) * REST] = wnat[s, k * CH : (k + 1) * CH, MAIN:]
        ga[...] = dot(wb[...], hstack[...])
        x_at = lambda rows, cols: xs[s, rows, cols].astype(F32)

        def emit(rows, cols, dx):
            ccur[rows, cols] = (hcur[rows, cols].astype(F32) + dx).astype(BF)

        norm_bwd(ga, 0, x_at, g10[...], 10, mean.at[s], rstd.at[s], emb, m_scr, q_scr, emit)
        return carry

    lax.fori_loop(0, SEGS - 1, stage, 0)
    take(0)


VMEM = pl.BlockSpec(memory_space=pltpu.VMEM)
SMEM = pl.BlockSpec(memory_space=pltpu.SMEM)
ANY = pl.BlockSpec(memory_space=pl.ANY)
PARAMS = pltpu.CompilerParams(vmem_limit_bytes=60 * 1024 * 1024)


def shape(dims, dtype=BF):
    return jax.ShapeDtypeStruct(dims, dtype)


def cost(microseconds):
    return pl.CostEstimate(flops=int(microseconds * 1e9), bytes_accessed=0, transcendentals=0)


def run_down_forward(*args):
    return pl.pallas_call(
        down_forward_kernel,
        name="down_forward",
        out_shape=(
            shape((SEGS + 1, CH, TOK)),
            shape((SEGS, CH, LANES), F32),
            shape((SEGS, CH, LANES), F32),
            shape((DOWN_SEL, TOK)),
            shape((SEGS, 3 * CH, CH)),
            shape((SEGS, 4, CH, TOK)),
            shape((SEGS, CH, LANES), F32),
            shape((SEGS, CH, LANES), F32),
        ),
        in_specs=[SMEM] + [VMEM] * 7 + [ANY] * 7,
        out_specs=(VMEM,) * 8,
        scratch_shapes=[
            pltpu.VMEM((CH, 3 * CH), BF),
            pltpu.VMEM((3, CH, TOK), BF),
            pltpu.VMEM((CH, LANES), F32),
            pltpu.VMEM((CH, LANES), F32),
            pltpu.SemaphoreType.DMA((SEGS,)),
        ],
        compiler_params=PARAMS,
        cost_estimate=cost(20),
    )(*args)


def run_up(*args, scale):
    return pl.pallas_call(
        functools.partial(up_kernel, scale=scale),
        name="up_both",
        out_shape=(
            shape((UP_SEL, 4 * CH), F32),
            shape((SEGS, CH, TOK)),
            shape((CH, TOK)),
        ),
        in_specs=[SMEM] + [VMEM] * 9 + [ANY] * 9,
        out_specs=(VMEM,) * 3,
        scratch_shapes=[
            pltpu.VMEM((SEGS, CH, 8 * CH), BF),
            pltpu.VMEM((2 * CH, 1024 + 384), BF),
            pltpu.VMEM((2, 4, 2, CH, TOK), BF),
            pltpu.VMEM((UP_SEL, TOK), BF),
            pltpu.VMEM((UP_SEL, TOK), BF),
            pltpu.VMEM((SEGS + 1, CH, TOK), BF),
            pltpu.VMEM((SEGS, CH, LANES), F32),
            pltpu.VMEM((SEGS, CH, LANES), F32),
            pltpu.VMEM((2 * CH, TOK), F32),
            pltpu.VMEM((2 * CH, TOK), F32),
            pltpu.VMEM((CH, TOK), BF),
            pltpu.VMEM((3 * CH, TOK), BF),
            pltpu.VMEM((CH, LANES), F32),
            pltpu.VMEM((CH, LANES), F32),
            pltpu.SemaphoreType.DMA((SEGS,)),
            pltpu.SemaphoreType.DMA((2, 4)),
        ],
        compiler_params=PARAMS,
        cost_estimate=cost(50),
    )(*args)


def run_down_backward(*args):
    return pl.pallas_call(
        down_backward_kernel,
        name="down_backward",
        out_shape=shape((DOWN_SEL, 3 * CH), F32),
        in_specs=[SMEM] + [VMEM] * 10,
        out_specs=VMEM,
        scratch_shapes=[
            pltpu.VMEM((CH, 3 * CH), BF),
            pltpu.VMEM((3 * CH, TOK), BF),
            pltpu.VMEM((CH, TOK), BF),
            pltpu.VMEM((CH, TOK), F32),
            pltpu.VMEM((CH, TOK), BF),
            pltpu.VMEM((CH, LANES), F32),
            pltpu.VMEM((CH, LANES), F32),
        ],
        compiler_params=PARAMS,
        cost_estimate=cost(15),
    )(*args)


def pick_matrix(x_index, per_device, channels):
    row = lax.broadcasted_iota(jnp.int32, (16 * per_device, channels), 0)
    col = lax.broadcasted_iota(jnp.int32, (16 * per_device, channels), 1)
    core = row // (8 * per_device)
    dp = (row // per_device) % 8
    want = (dp * 8 + 2 * x_index + core) * per_device + row % per_device
    return (col == want).astype(BF)


def clip_inputs(clip, step_value, seed_value, in_weight, out_weight):
    lat_dim, pix_dim, frames = clip.shape
    noise = noise_field(seed_value, lat_dim, pix_dim)
    theta = step_value.astype(F32) * (0.5 * math.pi / 1000.0)
    noisy = (
        jnp.cos(theta) * clip.reshape(lat_dim, pix_dim * frames).astype(F32) + jnp.sin(theta) * noise
    ).astype(BF)
    noisy = jnp.pad(noisy, ((0, 16 - lat_dim), (0, 0)))
    in_t = jnp.pad(in_weight.T, ((0, 0), (0, 16 - lat_dim)))
    out_t = jnp.pad(out_weight.T, ((0, 16 - lat_dim), (0, 0)))
    emb = jnp.broadcast_to(time_embedding(step_value, CH)[:, None], (CH, LANES))
    return noise, noisy, in_t, out_t, emb


def swap_core(value):
    return lax.ppermute(value, "core", [(0, 1), (1, 0)])


def from_segment(value, away):
    return lax.ppermute(value, "segment", [((i + away) % SEGS, i) for i in range(SEGS)])


def fetch_sections(half):
    return [from_segment(half, away) for away in (1, 3, 2)]


def cores_sum(total, core, rows):
    size = 8 * rows
    keep = lax.dynamic_slice_in_dim(total, core * size, size, 0)
    give = lax.dynamic_slice_in_dim(total, (1 - core) * size, size, 0)
    return (keep + swap_core(give)).reshape(8, -1)


def dp_sum(both, rows):
    parts = lax.all_to_all(both, "dp", 0, 0, tiled=True)
    return jnp.sum(parts, axis=0).reshape(rows, -1)


def taps(value):
    return jnp.stack(
        [
            jnp.concatenate(
                [
                    value[:, k * MAIN : (k + 1) * MAIN],
                    value[:, 3 * MAIN + k * REST : 3 * MAIN + (k + 1) * REST],
                ],
                axis=1,
            )
            for k in range(3)
        ]
    )


def clip_gradients(ids, clip, step_value, seed_value, x_index, in_weight, out_weight, down, up, reduce_up):
    noise, noisy, in_t, out_t, emb = clip_inputs(clip, step_value, seed_value, in_weight, out_weight)
    g10 = jnp.asarray(group_matrix(10), BF)
    g20 = jnp.asarray(group_matrix(20), BF)
    shift = jnp.asarray(shift_matrix(), BF)
    pick_d = pick_matrix(x_index, 5, CH)
    pick_u = pick_matrix(x_index, 10, 2 * CH)
    xs, mean, rstd, asel, wnat, dstack, dmean, drstd = run_down_forward(
        ids, noisy, in_t, emb, g10, g20, shift, pick_d, *down()
    )
    xs, up_args = up(xs)
    gu, kgrad, cgrad = run_up(
        ids, xs, dmean, drstd, g20, shift, pick_u, out_t, out_weight.astype(F32), noise, dstack, *up_args,
        scale=64.0 / math.sqrt(16 * FRAMES * 4 * 64),
    )
    up_part, kgrad = reduce_up(gu, kgrad)
    gd = run_down_backward(ids, xs, mean, rstd, asel, wnat, emb, g10, shift, kgrad, cgrad)
    return gd, up_part


def local(latents, timesteps, seeds, in_weight, out_weight, down_weight, up_weight, skip_weight):
    seg = lax.axis_index("segment")
    core = lax.axis_index("core")
    x_index = lax.axis_index("x")
    ids = jnp.stack([seg, core]).astype(jnp.int32)
    down_nat = down_weight[0].reshape(3 * CH, CH)
    up_t = jnp.transpose(up_weight[0], (0, 2, 1))
    skip_t = skip_weight[0].T
    d_half = lax.dynamic_slice_in_dim(down_nat, core * (3 * CH // 2), 3 * CH // 2, 0)
    u_half = jnp.concatenate(
        [
            lax.dynamic_slice_in_dim(up_t, core * (CH // 2), CH // 2, 1),
            lax.dynamic_slice_in_dim(skip_t, core * (CH // 2), CH // 2, 0)[None],
        ],
        axis=0,
    )
    d_mine = fetch_sections(d_half)
    *d_mine, u_half = lax.optimization_barrier((*d_mine, u_half))
    u_mine = fetch_sections(u_half)

    clips = lax.all_gather(latents, ("x", "core"), axis=0)
    clip = lax.dynamic_index_in_dim(clips, core, 1, keepdims=False)
    clip = jnp.transpose(clip.reshape(FRAMES, 4, 64), (1, 2, 0))
    step_value = lax.dynamic_index_in_dim(timesteps, core, 0, keepdims=False)
    seed_value = lax.dynamic_index_in_dim(seeds, core, 0, keepdims=False)

    def down():
        return [down_nat, *d_mine, *[swap_core(p) for p in d_mine]]

    def up(xs):
        *parts, xs = lax.optimization_barrier((*u_mine, xs))
        return xs, [up_t, skip_t, *parts, *[swap_core(p) for p in parts]]

    def reduce_up(gu, kgrad):
        return lax.optimization_barrier((cores_sum(gu, core, 10), kgrad))

    gd, up_part = clip_gradients(
        ids, clip, step_value, seed_value, x_index, in_weight, out_weight, down, up, reduce_up
    )
    up_sum = dp_sum(up_part, 10)
    gd, up_sum = lax.optimization_barrier((gd, up_sum))
    down_sum = taps(dp_sum(cores_sum(gd, core, 5), 5))
    return down_sum[None], taps(up_sum[:, : 3 * CH])[None], up_sum[:, 3 * CH :][None]


def solution(mesh):
    devices = mesh.devices
    grid = Mesh(devices.reshape(devices.shape[0], devices.shape[1], 4, 2), ("dp", "segment", "x", "core"))
    tm = ("x", "core")
    return jax.shard_map(
        local,
        mesh=grid,
        in_specs=(
            P("dp", tm, None, None),
            P("dp"),
            P("dp"),
            P(),
            P(),
            P("segment", None, None, None),
            P("segment", None, None, None),
            P("segment", None, None),
        ),
        out_specs=(
            P("segment", None, ("dp",) + tm, None),
            P("segment", None, ("dp",) + tm, None),
            P("segment", ("dp",) + tm, None),
        ),
        check_vma=False,
    )
```

```python
import functools
import math

import jax
import jax.numpy as jnp
import numpy as np
from jax import lax
from jax.experimental import pallas as pl
from jax.experimental.pallas import tpu as pltpu
from jax.sharding import Mesh
from jax.sharding import PartitionSpec as P

CH = 320
GROUPS = 32
SEGS = 4
TOK = 1024
FRAMES = 16
LANES = 128
TILES = TOK // LANES
ROWS = 32
BF = jnp.bfloat16
F32 = jnp.float32
DOWN_SEL = 80
UP_SEL = 160


def mix_bits(value):
    value = value ^ lax.shift_right_logical(value, jnp.int32(16))
    value = value * -2048144789
    value = value ^ lax.shift_right_logical(value, jnp.int32(13))
    value = value * -1028477387
    value = value ^ lax.shift_right_logical(value, jnp.int32(16))
    return value


def noise_field(seed_value, lat_dim, pix_dim):
    lat_ids = lax.broadcasted_iota(jnp.int32, (lat_dim, pix_dim * FRAMES), 0)
    tokens = lax.broadcasted_iota(jnp.int32, (lat_dim, pix_dim * FRAMES), 1)
    frame_ids = tokens % FRAMES
    pix_ids = tokens // FRAMES
    index = (frame_ids * lat_dim + lat_ids) * pix_dim + pix_ids
    salted = seed_value * -1640531535
    first = mix_bits(index * 2 + salted)
    second = mix_bits(index * 2 + 1 + salted)
    unit_a = (lax.shift_right_logical(first, jnp.int32(8)).astype(F32) + 0.5) / 16777216.0
    unit_b = (lax.shift_right_logical(second, jnp.int32(8)).astype(F32) + 0.5) / 16777216.0
    return jnp.sqrt(-2.0 * jnp.log(unit_a)) * jnp.cos(2.0 * math.pi * unit_b)


def time_embedding(step_value, channels):
    half = channels // 2
    frequency = jnp.exp(-math.log(10000.0) * jnp.arange(half, dtype=F32) / half)
    phase = step_value.astype(F32) * frequency
    return jnp.concatenate([jnp.sin(phase), jnp.cos(phase)])


def group_matrix(size):
    ids = np.arange(CH) // size
    return (ids[:, None] == ids[None, :]).astype(np.float32)


def dot(a, b):
    return jnp.dot(a, b, preferred_element_type=F32)


def dot_nt(a, b):
    return lax.dot_general(a, b, (((1,), (1,)), ((), ())), preferred_element_type=F32)


def tile(j):
    return slice(j * LANES, (j + 1) * LANES)


def row_block(r):
    return pl.ds(pl.multiple_of(r * ROWS, ROWS), ROWS)


def fold(value):
    for step in (16, 32, 64):
        value = value + pltpu.roll(value, step, 1)
    return value


def group_sums(group, values, parts):
    pieces = []
    for value in values:
        rest = value
        for _ in range(parts):
            piece = rest.astype(BF)
            pieces.append(piece)
            rest = rest - piece.astype(F32)
    sums = dot(group, jnp.concatenate(pieces, axis=1))
    out = []
    for i in range(len(values)):
        total = sums[:, tile(i * parts)]
        for q in range(1, parts):
            total = total + sums[:, tile(i * parts + q)]
        out.append(fold(total))
    return out


def gn_stats(x_at, group, size, m_scr, q_scr, mean_at, rstd_at):
    def body(r, carry):
        rows = row_block(r)
        parts = [x_at(rows, tile(j)) for j in range(TILES)]
        total = parts[0]
        for p in parts[1:]:
            total = total + p
        mid = total * (1.0 / TILES)
        square = None
        for p in parts:
            d = p - mid
            square = d * d if square is None else square + d * d
        m_scr[rows, :] = mid
        q_scr[rows, :] = square
        return carry

    lax.fori_loop(0, CH // ROWS, body, 0, unroll=True)
    mid = m_scr[...]
    (mean,) = group_sums(group, [mid], 3)
    mean = mean * (1.0 / (8 * size))
    away = mid - mean
    (spread,) = group_sums(group, [q_scr[...] + (TILES * 1.0) * away * away], 2)
    mean_at[...] = mean
    rstd_at[...] = lax.rsqrt(spread * (1.0 / (64 * size)) + 1e-05)


def shift_matrix():
    lane = np.arange(LANES)
    out = np.zeros((LANES, 2 * LANES), np.float32)
    for l in lane:
        if l % FRAMES != 0:
            out[l - 1, l] = 1.0
        if l % FRAMES != FRAMES - 1:
            out[l + 1, LANES + l] = 1.0
    return out


def neighbours(value, shift):
    both = dot(value, shift).astype(BF)
    return both[:, :LANES], both[:, LANES:]


def silu_parts(y):
    sig = 0.5 * jnp.tanh(0.5 * y) + 0.5
    return sig, y * sig


def norm_bwd(ga_ref, ga_off, x_at, group, size, mean_at, rstd_at, emb_ref, m_scr, q_scr, emit):
    def first(r, carry):
        rows = row_block(r)
        grows = pl.ds(pl.multiple_of(ga_off + r * ROWS, ROWS), ROWS)
        mean = mean_at[rows, :]
        rstd = rstd_at[rows, :]
        emb = None if emb_ref is None else emb_ref[rows, :]
        s1 = None
        s2 = None
        for j in range(TILES):
            xhat = (x_at(rows, tile(j)) - mean) * rstd
            y = xhat if emb is None else xhat + emb
            sig, act = silu_parts(y)
            dy = ga_ref[grows, tile(j)] * (sig + act * (1.0 - sig))
            ga_ref[grows, tile(j)] = dy
            s1 = dy if s1 is None else s1 + dy
            s2 = dy * xhat if s2 is None else s2 + dy * xhat
        m_scr[rows, :] = s1
        q_scr[rows, :] = s2
        return carry

    lax.fori_loop(0, CH // ROWS, first, 0, unroll=True)
    s1, s2 = group_sums(group, [m_scr[...], q_scr[...]], 2)
    scale = 1.0 / (64 * size)
    m_scr[...] = s1 * scale
    q_scr[...] = s2 * scale

    def second(r, carry):
        rows = row_block(r)
        grows = pl.ds(pl.multiple_of(ga_off + r * ROWS, ROWS), ROWS)
        mean = mean_at[rows, :]
        rstd = rstd_at[rows, :]
        m1 = m_scr[rows, :]
        m2 = q_scr[rows, :]
        for j in range(TILES):
            xhat = (x_at(rows, tile(j)) - mean) * rstd
            emit(rows, tile(j), rstd * (ga_ref[grows, tile(j)] - m1 - xhat * m2))
        return carry

    lax.fori_loop(0, CH // ROWS, second, 0, unroll=True)


MAIN = 256
REST = CH - MAIN


def copy_bytes(ref, sem):
    return pltpu.make_async_copy(ref, ref, sem)


def section_of(seg, slot):
    return lax.rem(seg + (1, 3, 2)[slot], SEGS)


def start_down_copies(ids, own, parts, dest, sems):
    half = 3 * CH // 2
    pltpu.make_async_copy(own, dest.at[ids[0]], sems.at[ids[0]]).start()
    for slot in range(3):
        s = section_of(ids[0], slot)
        for source, place in ((parts[slot], ids[1]), (parts[3 + slot], 1 - ids[1])):
            rows = pl.ds(pl.multiple_of(place * half, 32), half)
            pltpu.make_async_copy(source, dest.at[s, rows, :], sems.at[s]).start()


def start_up_copies(ids, own_up, own_skip, parts, dest, sems):
    half = CH // 2
    seg = ids[0]
    for k in range(4):
        source = own_up.at[k] if k < 3 else own_skip
        pltpu.make_async_copy(source, dest.at[seg, :, k * 640 : (k + 1) * 640], sems.at[seg]).start()
    for slot in range(3):
        s = section_of(seg, slot)
        for source, place in ((parts[slot], ids[1]), (parts[3 + slot], 1 - ids[1])):
            rows = pl.ds(pl.multiple_of(place * half, 32), half)
            for k in range(4):
                pltpu.make_async_copy(
                    source.at[k], dest.at[s, rows, k * 640 : (k + 1) * 640], sems.at[s]
                ).start()


def activate(x_at, mean_at, rstd_at, emb_ref, put):
    def act(r, carry):
        rows = row_block(r)
        mu = mean_at[rows, :]
        rs = rstd_at[rows, :]
        e = None if emb_ref is None else emb_ref[rows, :]
        for j in range(TILES):
            y = (x_at(rows, tile(j)) - mu) * rs
            if e is not None:
                y = y + e
            put(rows, tile(j), silu_parts(y)[1].astype(BF))
        return carry

    lax.fori_loop(0, CH // ROWS, act, 0, unroll=True)


def down_forward_kernel(
    ids, noisy, in_t, emb, g10, g20, shift, pick, own, p0, p1, p2, q0, q1, q2,
    xs, mean, rstd, asel, wnat, dstack, dmean, drstd,
    wt, stack, m_scr, q_scr, sems,
):
    start_down_copies(ids, own, (p0, p1, p2, q0, q1, q2), wnat, sems)
    xs[0] = dot(in_t[...], noisy[...]).astype(BF)

    def stage(s, carry):
        x_at = lambda rows, cols: xs[s, rows, cols].astype(F32)
        gn_stats(x_at, g10[...], 10, m_scr, q_scr, mean.at[s], rstd.at[s])

        def put(rows, cols, a):
            stack[1, rows, cols] = a

        activate(x_at, mean.at[s], rstd.at[s], emb, put)
        for j in range(TILES):
            before, after = neighbours(stack[1, :, tile(j)], shift[...])
            stack[0, :, tile(j)] = before
            stack[2, :, tile(j)] = after

        @pl.when(s == ids[0])
        def _():
            asel[...] = dot(pick[...], stack[1]).astype(BF)

        copy_bytes(wnat.at[s], sems.at[s]).wait()
        for begin in range(0, 3 * CH, LANES):
            size = min(LANES, 3 * CH - begin)
            wt[:, begin : begin + size] = wnat[s, begin : begin + size, :].T
        total = dot(wt[...], stack[...].reshape(3 * CH, TOK)) + xs[s].astype(F32)
        xs[s + 1] = total.astype(BF)
        return carry

    lax.fori_loop(0, SEGS, stage, 0)

    def ahead(s, carry):
        x_at = lambda rows, cols: xs[s + 1, rows, cols].astype(F32)
        gn_stats(x_at, g20[...], 20, m_scr, q_scr, dmean.at[s], drstd.at[s])

        def put(rows, cols, a):
            dstack[s, 1, rows, cols] = a

        activate(x_at, dmean.at[s], drstd.at[s], None, put)
        for j in range(TILES):
            before, after = neighbours(dstack[s, 1, :, tile(j)], shift[...])
            dstack[s, 0, :, tile(j)] = before
            dstack[s, 2, :, tile(j)] = after
        dstack[s, 3] = xs[s + 1]
        return carry

    lax.fori_loop(0, SEGS, ahead, 0)


def spread_grad(value, shift, gstack):
    for j in range(TILES):
        g = value(tile(j))
        before, after = neighbours(g, shift)
        for k, part in ((0, after), (1, g), (2, before)):
            gstack[k * MAIN : (k + 1) * MAIN, tile(j)] = part[:MAIN]
            gstack[3 * MAIN + k * REST : 3 * MAIN + (k + 1) * REST, tile(j)] = part[MAIN:]


def up_kernel(
    ids, xs, dmean, drstd, g20, shift, pick, out_t, out_wide, noise,
    dstack, own_up, own_skip, p0, p1, p2, q0, q1, q2,
    gu, kgrad, cgrad,
    wt, wb, stack, bsel, jsel, es, emean, erstd, ga, thru, gcur, gstack, m_scr, q_scr, sems, dsems, *, scale
):
    start_up_copies(ids, own_up, own_skip, (p0, p1, p2, q0, q1, q2), wt, sems)

    def fetch(s):
        slot = lax.rem(s, 2)
        for k in range(4):
            pltpu.make_async_copy(dstack.at[s, k], stack.at[slot, k, 1], dsems.at[slot, k]).start()

    fetch(jnp.int32(SEGS - 1))
    es[SEGS] = xs[SEGS]

    def forward(i, carry):
        s = SEGS - 1 - i
        slot = lax.rem(s, 2)

        @pl.when(s > 0)
        def _():
            fetch(s - 1)

        x_at = lambda rows, cols: es[s + 1, rows, cols].astype(F32)
        gn_stats(x_at, g20[...], 20, m_scr.at[0], q_scr.at[0], emean.at[s], erstd.at[s])

        def put(rows, cols, a):
            stack[slot, 1, 0, rows, cols] = a

        activate(x_at, emean.at[s], erstd.at[s], None, put)
        for j in range(TILES):
            before, after = neighbours(stack[slot, 1, 0, :, tile(j)], shift[...])
            stack[slot, 0, 0, :, tile(j)] = before
            stack[slot, 2, 0, :, tile(j)] = after
        stack[slot, 3, 0] = es[s + 1]
        for k in range(4):
            pltpu.make_async_copy(dstack.at[s, k], stack.at[slot, k, 1], dsems.at[slot, k]).wait()

        @pl.when(s == ids[0])
        def _():
            bsel[...] = dot(pick[...], stack[slot, 1].reshape(2 * CH, TOK)).astype(BF)
            jsel[...] = dot(pick[...], stack[slot, 3].reshape(2 * CH, TOK)).astype(BF)

        copy_bytes(wt.at[s], sems.at[s]).wait()
        es[s] = dot(wt[s], stack[slot].reshape(8 * CH, TOK)).astype(BF)
        return carry

    lax.fori_loop(0, SEGS, forward, 0)

    predicted = dot(out_t[...], es[0])
    thru[0:4, :] = (predicted[:4] - noise[...]) * scale

    def seed(r, carry):
        rows = row_block(r)
        for j in range(TILES):
            total = out_wide[rows, 0:1] * thru[0:1, tile(j)]
            for l in range(1, 4):
                total = total + out_wide[rows, l : l + 1] * thru[l : l + 1, tile(j)]
            gcur[rows, tile(j)] = total.astype(BF)
        return carry

    lax.fori_loop(0, CH // ROWS, seed, 0, unroll=True)

    def backward(s, carry):
        for k in range(3):
            for b in range(2):
                wb[:, k * MAIN + b * LANES : k * MAIN + (b + 1) * LANES] = wt[
                    s, b * LANES : (b + 1) * LANES, k * 640 : (k + 1) * 640
                ].T
        tops = [wt[s, MAIN:, k * 640 : (k + 1) * 640] for k in range(3)]
        wb[:, 3 * MAIN : 3 * MAIN + LANES] = jnp.concatenate(tops[:2], axis=0).T
        wb[:, 3 * MAIN + LANES : 3 * CH] = tops[2].T
        for b in range(2):
            wb[:, 1024 + b * LANES : 1024 + (b + 1) * LANES] = wt[s, b * LANES : (b + 1) * LANES, 1920:].T
        wb[:, 1024 + MAIN : 1024 + CH] = wt[s, MAIN:, 1920:].T
        spread_grad(lambda cols: gcur[:, cols], shift[...], gstack)

        @pl.when(s == ids[0])
        def _():
            gu[:, : 3 * CH] = dot_nt(bsel[...], gstack[...])
            gu[:, 3 * CH :] = dot_nt(jsel[...], gcur[...])

        ga[...] = dot(wb[:, : 3 * CH], gstack[...])
        thru[...] = dot(wb[:, 1024 : 1024 + CH], gcur[...])

        def emit_e(rows, cols, dx):
            gcur[rows, cols] = (dx + thru[rows, cols]).astype(BF)

        def emit_d(rows, cols, dx):
            trows = pl.ds(pl.multiple_of(rows.start + CH, ROWS), ROWS)
            kgrad[s, rows, cols] = (dx + thru[trows, cols]).astype(BF)

        e_at = lambda rows, cols: es[s + 1, rows, cols].astype(F32)
        d_at = lambda rows, cols: xs[s + 1, rows, cols].astype(F32)
        norm_bwd(ga, 0, e_at, g20[...], 20, emean.at[s], erstd.at[s], None, m_scr.at[0], q_scr.at[0], emit_e)
        norm_bwd(ga, CH, d_at, g20[...], 20, dmean.at[s], drstd.at[s], None, m_scr.at[1], q_scr.at[1], emit_d)
        return carry

    lax.fori_loop(0, SEGS, backward, 0)
    cgrad[...] = gcur[...]


def down_backward_kernel(
    ids, xs, mean, rstd, asel, wnat, emb, g10, shift, kgrad, cgrad,
    gd,
    wb, hstack, hcur, ga, ccur, m_scr, q_scr,
):
    ccur[...] = cgrad[...]

    def take(s):
        def value(cols):
            h = (kgrad[s, :, cols].astype(F32) + ccur[:, cols].astype(F32)).astype(BF)
            hcur[:, cols] = h
            return h

        spread_grad(value, shift[...], hstack)

        @pl.when(s == ids[0])
        def _():
            gd[...] = dot_nt(asel[...], hstack[...])

    def stage(i, carry):
        s = SEGS - 1 - i
        take(s)
        for k in range(3):
            wb[:, k * MAIN : (k + 1) * MAIN] = wnat[s, k * CH : (k + 1) * CH, :MAIN]
            wb[:, 3 * MAIN + k * REST : 3 * MAIN + (k + 1) * REST] = wnat[s, k * CH : (k + 1) * CH, MAIN:]
        ga[...] = dot(wb[...], hstack[...])
        x_at = lambda rows, cols: xs[s, rows, cols].astype(F32)

        def emit(rows, cols, dx):
            ccur[rows, cols] = (hcur[rows, cols].astype(F32) + dx).astype(BF)

        norm_bwd(ga, 0, x_at, g10[...], 10, mean.at[s], rstd.at[s], emb, m_scr, q_scr, emit)
        return carry

    lax.fori_loop(0, SEGS - 1, stage, 0)
    take(0)


VMEM = pl.BlockSpec(memory_space=pltpu.VMEM)
SMEM = pl.BlockSpec(memory_space=pltpu.SMEM)
ANY = pl.BlockSpec(memory_space=pl.ANY)
PARAMS = pltpu.CompilerParams(vmem_limit_bytes=60 * 1024 * 1024)


def shape(dims, dtype=BF):
    return jax.ShapeDtypeStruct(dims, dtype)


def cost(microseconds):
    return pl.CostEstimate(flops=int(microseconds * 1e9), bytes_accessed=0, transcendentals=0)


def run_down_forward(*args):
    return pl.pallas_call(
        down_forward_kernel,
        name="down_forward",
        out_shape=(
            shape((SEGS + 1, CH, TOK)),
            shape((SEGS, CH, LANES), F32),
            shape((SEGS, CH, LANES), F32),
            shape((DOWN_SEL, TOK)),
            shape((SEGS, 3 * CH, CH)),
            shape((SEGS, 4, CH, TOK)),
            shape((SEGS, CH, LANES), F32),
            shape((SEGS, CH, LANES), F32),
        ),
        in_specs=[SMEM] + [VMEM] * 7 + [ANY] * 7,
        out_specs=(VMEM,) * 8,
        scratch_shapes=[
            pltpu.VMEM((CH, 3 * CH), BF),
            pltpu.VMEM((3, CH, TOK), BF),
            pltpu.VMEM((CH, LANES), F32),
            pltpu.VMEM((CH, LANES), F32),
            pltpu.SemaphoreType.DMA((SEGS,)),
        ],
        compiler_params=PARAMS,
        cost_estimate=cost(20),
    )(*args)


def run_up(*args, scale):
    return pl.pallas_call(
        functools.partial(up_kernel, scale=scale),
        name="up_both",
        out_shape=(
            shape((UP_SEL, 4 * CH), F32),
            shape((SEGS, CH, TOK)),
            shape((CH, TOK)),
        ),
        in_specs=[SMEM] + [VMEM] * 9 + [ANY] * 9,
        out_specs=(VMEM,) * 3,
        scratch_shapes=[
            pltpu.VMEM((SEGS, CH, 8 * CH), BF),
            pltpu.VMEM((2 * CH, 1024 + 384), BF),
            pltpu.VMEM((2, 4, 2, CH, TOK), BF),
            pltpu.VMEM((UP_SEL, TOK), BF),
            pltpu.VMEM((UP_SEL, TOK), BF),
            pltpu.VMEM((SEGS + 1, CH, TOK), BF),
            pltpu.VMEM((SEGS, CH, LANES), F32),
            pltpu.VMEM((SEGS, CH, LANES), F32),
            pltpu.VMEM((2 * CH, TOK), F32),
            pltpu.VMEM((2 * CH, TOK), F32),
            pltpu.VMEM((CH, TOK), BF),
            pltpu.VMEM((3 * CH, TOK), BF),
            pltpu.VMEM((2, CH, LANES), F32),
            pltpu.VMEM((2, CH, LANES), F32),
            pltpu.SemaphoreType.DMA((SEGS,)),
            pltpu.SemaphoreType.DMA((2, 4)),
        ],
        compiler_params=PARAMS,
        cost_estimate=cost(50),
    )(*args)


def run_down_backward(*args):
    return pl.pallas_call(
        down_backward_kernel,
        name="down_backward",
        out_shape=shape((DOWN_SEL, 3 * CH), F32),
        in_specs=[SMEM] + [VMEM] * 10,
        out_specs=VMEM,
        scratch_shapes=[
            pltpu.VMEM((CH, 3 * CH), BF),
            pltpu.VMEM((3 * CH, TOK), BF),
            pltpu.VMEM((CH, TOK), BF),
            pltpu.VMEM((CH, TOK), F32),
            pltpu.VMEM((CH, TOK), BF),
            pltpu.VMEM((CH, LANES), F32),
            pltpu.VMEM((CH, LANES), F32),
        ],
        compiler_params=PARAMS,
        cost_estimate=cost(15),
    )(*args)


def pick_matrix(x_index, core, per_device, channels):
    row = lax.broadcasted_iota(jnp.int32, (16 * per_device, channels), 0)
    col = lax.broadcasted_iota(jnp.int32, (16 * per_device, channels), 1)
    place = core ^ (row // (8 * per_device))
    dp = (row // per_device) % 8
    want = (dp * 8 + 2 * x_index + place) * per_device + row % per_device
    return (col == want).astype(BF)


def clip_inputs(clip, step_value, seed_value, in_weight, out_weight):
    lat_dim, pix_dim, frames = clip.shape
    noise = noise_field(seed_value, lat_dim, pix_dim)
    theta = step_value.astype(F32) * (0.5 * math.pi / 1000.0)
    noisy = (
        jnp.cos(theta) * clip.reshape(lat_dim, pix_dim * frames).astype(F32) + jnp.sin(theta) * noise
    ).astype(BF)
    noisy = jnp.pad(noisy, ((0, 16 - lat_dim), (0, 0)))
    in_t = jnp.pad(in_weight.T, ((0, 0), (0, 16 - lat_dim)))
    out_t = jnp.pad(out_weight.T, ((0, 16 - lat_dim), (0, 0)))
    emb = jnp.broadcast_to(time_embedding(step_value, CH)[:, None], (CH, LANES))
    return noise, noisy, in_t, out_t, emb


def swap_core(value):
    return lax.ppermute(value, "core", [(0, 1), (1, 0)])


def from_segment(value, away):
    return lax.ppermute(value, "segment", [((i + away) % SEGS, i) for i in range(SEGS)])


def fetch_sections(half):
    return [from_segment(half, away) for away in (1, 3, 2)]


def cores_sum(total):
    return (total[0] + swap_core(total[1])).reshape(8, -1)


def taps(value):
    return jnp.stack(
        [
            jnp.concatenate(
                [
                    value[:, k * MAIN : (k + 1) * MAIN],
                    value[:, 3 * MAIN + k * REST : 3 * MAIN + (k + 1) * REST],
                ],
                axis=1,
            )
            for k in range(3)
        ]
    )


def clip_gradients(ids, clip, step_value, seed_value, x_index, in_weight, out_weight, down, up, reduce_up):
    noise, noisy, in_t, out_t, emb = clip_inputs(clip, step_value, seed_value, in_weight, out_weight)
    g10 = jnp.asarray(group_matrix(10), BF)
    g20 = jnp.asarray(group_matrix(20), BF)
    shift = jnp.asarray(shift_matrix(), BF)
    pick_d = pick_matrix(x_index, ids[1], 5, CH)
    pick_u = pick_matrix(x_index, ids[1], 10, 2 * CH)
    xs, mean, rstd, asel, wnat, dstack, dmean, drstd = run_down_forward(
        ids, noisy, in_t, emb, g10, g20, shift, pick_d, *down()
    )
    xs, up_args = up(xs)
    gu, kgrad, cgrad = run_up(
        ids, xs, dmean, drstd, g20, shift, pick_u, out_t, out_weight.astype(F32), noise, dstack, *up_args,
        scale=64.0 / math.sqrt(16 * FRAMES * 4 * 64),
    )
    up_part = reduce_up(gu)
    gd = run_down_backward(ids, xs, mean, rstd, asel, wnat, emb, g10, shift, kgrad, cgrad)
    return gd, up_part


def whole_clip(latents, core, x_index):
    own = lax.dynamic_index_in_dim(latents, core, 0, keepdims=False)
    got = swap_core(lax.dynamic_index_in_dim(latents, 1 - core, 0, keepdims=False))
    half = lax.broadcasted_iota(jnp.int32, (2,) + own.shape, 0)
    quad = jnp.where(half == core, own[None], got[None])
    quads = [quad] + [
        lax.ppermute(quad, "x", [((i + away) % 4, i) for i in range(4)]) for away in (1, 2, 3)
    ]
    away = (lax.broadcasted_iota(jnp.int32, (4,) + quad.shape, 0) - x_index) & 3
    whole = quads[3][None]
    for i in (2, 1, 0):
        whole = jnp.where(away == i, quads[i][None], whole)
    return whole.reshape((FRAMES,) + own.shape[1:])


def local(latents, timesteps, seeds, in_weight, out_weight, down_weight, up_weight, skip_weight):
    seg = lax.axis_index("segment")
    core = lax.axis_index("core")
    x_index = lax.axis_index("x")
    ids = jnp.stack([seg, core]).astype(jnp.int32)
    down_nat = down_weight[0].reshape(3 * CH, CH)
    up_t = jnp.transpose(up_weight[0], (0, 2, 1))
    skip_t = skip_weight[0].T
    d_half = lax.dynamic_slice_in_dim(down_nat, core * (3 * CH // 2), 3 * CH // 2, 0)
    u_half = jnp.concatenate(
        [
            lax.dynamic_slice_in_dim(up_t, core * (CH // 2), CH // 2, 1),
            lax.dynamic_slice_in_dim(skip_t, core * (CH // 2), CH // 2, 0)[None],
        ],
        axis=0,
    )
    d_mine = fetch_sections(d_half)
    *d_mine, u_half = lax.optimization_barrier((*d_mine, u_half))
    u_mine = fetch_sections(u_half)

    clip = jnp.transpose(whole_clip(latents, core, x_index), (1, 2, 0))
    step_value = lax.dynamic_index_in_dim(timesteps, core, 0, keepdims=False)
    seed_value = lax.dynamic_index_in_dim(seeds, core, 0, keepdims=False)

    def down():
        return [down_nat, *d_mine, *[swap_core(p) for p in d_mine]]

    def up(xs):
        *parts, xs = lax.optimization_barrier((*u_mine, xs))
        return xs, [up_t, skip_t, *parts, *[swap_core(p) for p in parts]]

    def reduce_up(gu):
        return cores_sum(gu.reshape(2, UP_SEL // 2, 4 * CH))

    gd, up_part = clip_gradients(
        ids, clip, step_value, seed_value, x_index, in_weight, out_weight, down, up, reduce_up
    )
    down_part = cores_sum(gd.reshape(2, DOWN_SEL // 2, 3 * CH))
    parts = lax.all_to_all(jnp.concatenate([down_part, up_part], axis=1), "dp", 0, 0, tiled=True)
    total = jnp.sum(parts, axis=0)
    down_sum = taps(total[: down_part.shape[1]].reshape(5, -1))
    up_sum = total[down_part.shape[1] :].reshape(10, -1)
    return down_sum[None], taps(up_sum[:, : 3 * CH])[None], up_sum[:, 3 * CH :][None]


def solution(mesh):
    devices = mesh.devices
    grid = Mesh(devices.reshape(devices.shape[0], devices.shape[1], 4, 2), ("dp", "segment", "x", "core"))
    tm = ("x", "core")
    return jax.shard_map(
        local,
        mesh=grid,
        in_specs=(
            P("dp", tm, None, None),
            P("dp"),
            P("dp"),
            P(),
            P(),
            P("segment", None, None, None),
            P("segment", None, None, None),
            P("segment", None, None),
        ),
        out_specs=(
            P("segment", None, ("dp",) + tm, None),
            P("segment", None, ("dp",) + tm, None),
            P("segment", ("dp",) + tm, None),
        ),
        check_vma=False,
    )
```

```python
import functools
import math

import jax
import jax.numpy as jnp
import numpy as np
from jax import lax
from jax.experimental import pallas as pl
from jax.experimental.pallas import tpu as pltpu
from jax.sharding import Mesh
from jax.sharding import PartitionSpec as P

CH = 320
GROUPS = 32
SEGS = 4
TOK = 1024
FRAMES = 16
LANES = 128
TILES = TOK // LANES
ROWS = 32
BF = jnp.bfloat16
F32 = jnp.float32
DOWN_SEL = 80
UP_SEL = 160


def mix_bits(value):
    value = value ^ lax.shift_right_logical(value, jnp.int32(16))
    value = value * -2048144789
    value = value ^ lax.shift_right_logical(value, jnp.int32(13))
    value = value * -1028477387
    value = value ^ lax.shift_right_logical(value, jnp.int32(16))
    return value


def noise_field(seed_value, lat_dim, pix_dim):
    lat_ids = lax.broadcasted_iota(jnp.int32, (lat_dim, pix_dim * FRAMES), 0)
    tokens = lax.broadcasted_iota(jnp.int32, (lat_dim, pix_dim * FRAMES), 1)
    frame_ids = tokens % FRAMES
    pix_ids = tokens // FRAMES
    index = (frame_ids * lat_dim + lat_ids) * pix_dim + pix_ids
    salted = seed_value * -1640531535
    first = mix_bits(index * 2 + salted)
    second = mix_bits(index * 2 + 1 + salted)
    unit_a = (lax.shift_right_logical(first, jnp.int32(8)).astype(F32) + 0.5) / 16777216.0
    unit_b = (lax.shift_right_logical(second, jnp.int32(8)).astype(F32) + 0.5) / 16777216.0
    return jnp.sqrt(-2.0 * jnp.log(unit_a)) * jnp.cos(2.0 * math.pi * unit_b)


def time_embedding(step_value, channels):
    half = channels // 2
    frequency = jnp.exp(-math.log(10000.0) * jnp.arange(half, dtype=F32) / half)
    phase = step_value.astype(F32) * frequency
    return jnp.concatenate([jnp.sin(phase), jnp.cos(phase)])


def group_matrix(size):
    ids = np.arange(CH) // size
    return (ids[:, None] == ids[None, :]).astype(np.float32)


def dot(a, b):
    return jnp.dot(a, b, preferred_element_type=F32)


def dot_nt(a, b):
    return lax.dot_general(a, b, (((1,), (1,)), ((), ())), preferred_element_type=F32)


def tile(j):
    return slice(j * LANES, (j + 1) * LANES)


def row_block(r):
    return pl.ds(pl.multiple_of(r * ROWS, ROWS), ROWS)


def fold(value):
    for step in (16, 32, 64):
        value = value + pltpu.roll(value, step, 1)
    return value


def group_sums(group, values, parts):
    pieces = []
    for value in values:
        rest = value
        for _ in range(parts):
            piece = rest.astype(BF)
            pieces.append(piece)
            rest = rest - piece.astype(F32)
    sums = dot(group, jnp.concatenate(pieces, axis=1))
    out = []
    for i in range(len(values)):
        total = sums[:, tile(i * parts)]
        for q in range(1, parts):
            total = total + sums[:, tile(i * parts + q)]
        out.append(fold(total))
    return out


def gn_stats(x_at, group, size, m_scr, q_scr, mean_at, rstd_at):
    def body(r, carry):
        rows = row_block(r)
        parts = [x_at(rows, tile(j)) for j in range(TILES)]
        total = parts[0]
        for p in parts[1:]:
            total = total + p
        mid = total * (1.0 / TILES)
        square = None
        for p in parts:
            d = p - mid
            square = d * d if square is None else square + d * d
        m_scr[rows, :] = mid
        q_scr[rows, :] = square
        return carry

    lax.fori_loop(0, CH // ROWS, body, 0, unroll=True)
    mid = m_scr[...]
    (mean,) = group_sums(group, [mid], 3)
    mean = mean * (1.0 / (8 * size))
    away = mid - mean
    (spread,) = group_sums(group, [q_scr[...] + (TILES * 1.0) * away * away], 2)
    mean_at[...] = mean
    rstd_at[...] = lax.rsqrt(spread * (1.0 / (64 * size)) + 1e-05)


def shift_matrix():
    lane = np.arange(LANES)
    out = np.zeros((LANES, 2 * LANES), np.float32)
    for l in lane:
        if l % FRAMES != 0:
            out[l - 1, l] = 1.0
        if l % FRAMES != FRAMES - 1:
            out[l + 1, LANES + l] = 1.0
    return out


def neighbours(value, shift):
    both = dot(value, shift).astype(BF)
    return both[:, :LANES], both[:, LANES:]


def silu_parts(y):
    sig = 0.5 * jnp.tanh(0.5 * y) + 0.5
    return sig, y * sig


def norm_bwd(ga_ref, ga_off, x_at, group, size, mean_at, rstd_at, emb_ref, m_scr, q_scr, emit):
    def first(r, carry):
        rows = row_block(r)
        grows = pl.ds(pl.multiple_of(ga_off + r * ROWS, ROWS), ROWS)
        mean = mean_at[rows, :]
        rstd = rstd_at[rows, :]
        emb = None if emb_ref is None else emb_ref[rows, :]
        s1 = None
        s2 = None
        for j in range(TILES):
            xhat = (x_at(rows, tile(j)) - mean) * rstd
            y = xhat if emb is None else xhat + emb
            sig, act = silu_parts(y)
            dy = ga_ref[grows, tile(j)] * (sig + act * (1.0 - sig))
            ga_ref[grows, tile(j)] = dy
            s1 = dy if s1 is None else s1 + dy
            s2 = dy * xhat if s2 is None else s2 + dy * xhat
        m_scr[rows, :] = s1
        q_scr[rows, :] = s2
        return carry

    lax.fori_loop(0, CH // ROWS, first, 0, unroll=True)
    s1, s2 = group_sums(group, [m_scr[...], q_scr[...]], 2)
    scale = 1.0 / (64 * size)
    m_scr[...] = s1 * scale
    q_scr[...] = s2 * scale

    def second(r, carry):
        rows = row_block(r)
        grows = pl.ds(pl.multiple_of(ga_off + r * ROWS, ROWS), ROWS)
        mean = mean_at[rows, :]
        rstd = rstd_at[rows, :]
        m1 = m_scr[rows, :]
        m2 = q_scr[rows, :]
        for j in range(TILES):
            xhat = (x_at(rows, tile(j)) - mean) * rstd
            emit(rows, tile(j), rstd * (ga_ref[grows, tile(j)] - m1 - xhat * m2))
        return carry

    lax.fori_loop(0, CH // ROWS, second, 0, unroll=True)


MAIN = 256
REST = CH - MAIN


def copy_bytes(ref, sem):
    return pltpu.make_async_copy(ref, ref, sem)


def section_of(seg, slot):
    return lax.rem(seg + (1, 3, 2)[slot], SEGS)


def start_section(ids, s, own, pieces):
    away = lax.rem(s + SEGS - ids[0], SEGS)
    pl.when(away == 0)(own)
    for slot, distance in enumerate((1, 3, 2)):

        @pl.when(away == distance)
        def _():
            pieces(slot, ids[1])
            pieces(3 + slot, 1 - ids[1])


def start_down_copies(ids, s, own, parts, dest, sems):
    half = 3 * CH // 2

    def pieces(part, place):
        rows = pl.ds(pl.multiple_of(place * half, 32), half)
        pltpu.make_async_copy(parts[part], dest.at[s, rows, :], sems.at[s]).start()

    start_section(ids, s, lambda: pltpu.make_async_copy(own, dest.at[s], sems.at[s]).start(), pieces)


def start_up_copies(ids, s, own_up, own_skip, parts, dest, sems):
    half = CH // 2

    def mine():
        for k in range(4):
            source = own_up.at[k] if k < 3 else own_skip
            pltpu.make_async_copy(source, dest.at[s, :, k * 640 : (k + 1) * 640], sems.at[s]).start()

    def pieces(part, place):
        rows = pl.ds(pl.multiple_of(place * half, 32), half)
        for k in range(4):
            pltpu.make_async_copy(
                parts[part].at[k], dest.at[s, rows, k * 640 : (k + 1) * 640], sems.at[s]
            ).start()

    start_section(ids, s, mine, pieces)


def activate(x_at, mean_at, rstd_at, emb_ref, put):
    def act(r, carry):
        rows = row_block(r)
        mu = mean_at[rows, :]
        rs = rstd_at[rows, :]
        e = None if emb_ref is None else emb_ref[rows, :]
        for j in range(TILES):
            y = (x_at(rows, tile(j)) - mu) * rs
            if e is not None:
                y = y + e
            put(rows, tile(j), silu_parts(y)[1].astype(BF))
        return carry

    lax.fori_loop(0, CH // ROWS, act, 0, unroll=True)


def down_forward_kernel(
    ids, noisy, in_t, emb, g10, g20, shift, pick, own, p0, p1, p2, q0, q1, q2,
    xs_out, mean_out, rstd_out, asel, dstack_out, dmean_out, drstd_out,
    xs, mean, rstd, dstack, dmean, drstd, wnat, wt, stack, m_scr, q_scr, sems, osems,
):
    def send(array, out, index, sem):
        pltpu.make_async_copy(array.at[index], out.at[index], osems.at[sem]).start()

    for s in range(SEGS):
        start_down_copies(ids, s, own, (p0, p1, p2, q0, q1, q2), wnat, sems)
    xs[0] = dot(in_t[...], noisy[...]).astype(BF)
    send(xs, xs_out, 0, 0)

    def ahead(s):
        x_at = lambda rows, cols: xs[s + 1, rows, cols].astype(F32)
        gn_stats(x_at, g20[...], 20, m_scr.at[1], q_scr.at[1], dmean.at[s], drstd.at[s])

        def put(rows, cols, a):
            dstack[s, 1, rows, cols] = a

        activate(x_at, dmean.at[s], drstd.at[s], None, put)
        for j in range(TILES):
            before, after = neighbours(dstack[s, 1, :, tile(j)], shift[...])
            dstack[s, 0, :, tile(j)] = before
            dstack[s, 2, :, tile(j)] = after
        dstack[s, 3] = xs[s + 1]

    def send_ahead(s):
        send(dstack, dstack_out, s, 3)
        send(dmean, dmean_out, s, 4)
        send(drstd, drstd_out, s, 5)

    def stage(s, behind):
        x_at = lambda rows, cols: xs[s, rows, cols].astype(F32)
        gn_stats(x_at, g10[...], 10, m_scr.at[0], q_scr.at[0], mean.at[s], rstd.at[s])

        def put(rows, cols, a):
            stack[1, rows, cols] = a

        activate(x_at, mean.at[s], rstd.at[s], emb, put)
        for j in range(TILES):
            before, after = neighbours(stack[1, :, tile(j)], shift[...])
            stack[0, :, tile(j)] = before
            stack[2, :, tile(j)] = after

        @pl.when(s == ids[0])
        def _():
            asel[...] = dot(pick[...], stack[1]).astype(BF)

        copy_bytes(wnat.at[s], sems.at[s]).wait()
        for begin in range(0, 3 * CH, LANES):
            size = min(LANES, 3 * CH - begin)
            wt[:, begin : begin + size] = wnat[s, begin : begin + size, :].T
        total = dot(wt[...], stack[...].reshape(3 * CH, TOK)) + xs[s].astype(F32)
        xs[s + 1] = total.astype(BF)
        if behind:
            ahead(s - 1)
            send_ahead(s - 1)
        send(xs, xs_out, s + 1, 0)
        send(mean, mean_out, s, 1)
        send(rstd, rstd_out, s, 2)

    stage(0, False)

    def later_stage(s, carry):
        stage(s, True)
        return carry

    lax.fori_loop(1, SEGS, later_stage, 0)
    ahead(SEGS - 1)
    send_ahead(SEGS - 1)
    for sem, array in enumerate((xs, mean, rstd, dstack, dmean, drstd)):
        copy_bytes(array, osems.at[sem]).wait()


def spread_grad(value, shift, gstack):
    for j in range(TILES):
        g = value(tile(j))
        before, after = neighbours(g, shift)
        for k, part in ((0, after), (1, g), (2, before)):
            gstack[k * MAIN : (k + 1) * MAIN, tile(j)] = part[:MAIN]
            gstack[3 * MAIN + k * REST : 3 * MAIN + (k + 1) * REST, tile(j)] = part[MAIN:]


def up_kernel(
    ids, g20, shift, pick, out_t, out_wide, noise,
    xs_in, dmean_in, drstd_in, dstack, own_up, own_skip, p0, p1, p2, q0, q1, q2,
    gu_keep, gu_give, cgrad, kgrad_out,
    xs, dmean, drstd, kgrad, wt, wb, stack, bsel, jsel, es, emean, erstd, ga, thru, gcur, gstack, m_scr, q_scr,
    sems, dsems, isems, *, scale
):
    top = pltpu.make_async_copy(xs_in.at[SEGS], es.at[SEGS], isems.at[0])
    top.start()

    def fetch(s):
        slot = lax.rem(s, 2)
        for k in range(4):
            pltpu.make_async_copy(dstack.at[s, k], stack.at[slot, k, 1], dsems.at[slot, k]).start()

    fetch(jnp.int32(SEGS - 1))
    for s in reversed(range(SEGS)):
        start_up_copies(ids, s, own_up, own_skip, (p0, p1, p2, q0, q1, q2), wt, sems)
    late = [
        pltpu.make_async_copy(a, b, isems.at[1 + i])
        for i, (a, b) in enumerate(((xs_in, xs), (dmean_in, dmean), (drstd_in, drstd)))
    ]
    for c in late:
        c.start()
    top.wait()

    def forward(i, carry):
        s = SEGS - 1 - i
        slot = lax.rem(s, 2)

        @pl.when(s > 0)
        def _():
            fetch(s - 1)

        x_at = lambda rows, cols: es[s + 1, rows, cols].astype(F32)
        gn_stats(x_at, g20[...], 20, m_scr.at[0], q_scr.at[0], emean.at[s], erstd.at[s])

        def put(rows, cols, a):
            stack[slot, 1, 0, rows, cols] = a

        activate(x_at, emean.at[s], erstd.at[s], None, put)
        for j in range(TILES):
            before, after = neighbours(stack[slot, 1, 0, :, tile(j)], shift[...])
            stack[slot, 0, 0, :, tile(j)] = before
            stack[slot, 2, 0, :, tile(j)] = after
        stack[slot, 3, 0] = es[s + 1]
        for k in range(4):
            pltpu.make_async_copy(dstack.at[s, k], stack.at[slot, k, 1], dsems.at[slot, k]).wait()

        @pl.when(s == ids[0])
        def _():
            bsel[...] = dot(pick[...], stack[slot, 1].reshape(2 * CH, TOK)).astype(BF)
            jsel[...] = dot(pick[...], stack[slot, 3].reshape(2 * CH, TOK)).astype(BF)

        copy_bytes(wt.at[s], sems.at[s]).wait()
        es[s] = dot(wt[s], stack[slot].reshape(8 * CH, TOK)).astype(BF)
        return carry

    lax.fori_loop(0, SEGS, forward, 0)

    for c in late:
        c.wait()
    predicted = dot(out_t[...], es[0])
    thru[0:4, :] = (predicted[:4] - noise[...]) * scale

    def seed(r, carry):
        rows = row_block(r)
        for j in range(TILES):
            total = out_wide[rows, 0:1] * thru[0:1, tile(j)]
            for l in range(1, 4):
                total = total + out_wide[rows, l : l + 1] * thru[l : l + 1, tile(j)]
            gcur[rows, tile(j)] = total.astype(BF)
        return carry

    lax.fori_loop(0, CH // ROWS, seed, 0, unroll=True)

    def backward(s, carry):
        for k in range(3):
            for b in range(2):
                wb[:, k * MAIN + b * LANES : k * MAIN + (b + 1) * LANES] = wt[
                    s, b * LANES : (b + 1) * LANES, k * 640 : (k + 1) * 640
                ].T
        tops = [wt[s, MAIN:, k * 640 : (k + 1) * 640] for k in range(3)]
        wb[:, 3 * MAIN : 3 * MAIN + LANES] = jnp.concatenate(tops[:2], axis=0).T
        wb[:, 3 * MAIN + LANES : 3 * CH] = tops[2].T
        for b in range(2):
            wb[:, 1024 + b * LANES : 1024 + (b + 1) * LANES] = wt[s, b * LANES : (b + 1) * LANES, 1920:].T
        wb[:, 1024 + MAIN : 1024 + CH] = wt[s, MAIN:, 1920:].T
        spread_grad(lambda cols: gcur[:, cols], shift[...], gstack)

        @pl.when(s == ids[0])
        def _():
            for i, gu in enumerate((gu_keep, gu_give)):
                rows = slice(i * (UP_SEL // 2), (i + 1) * (UP_SEL // 2))
                gu[:, : 3 * CH] = dot_nt(bsel[rows, :], gstack[...])
                gu[:, 3 * CH :] = dot_nt(jsel[rows, :], gcur[...])

        ga[...] = dot(wb[:, : 3 * CH], gstack[...])
        thru[...] = dot(wb[:, 1024 : 1024 + CH], gcur[...])

        def emit_e(rows, cols, dx):
            gcur[rows, cols] = (dx + thru[rows, cols]).astype(BF)

        def emit_d(rows, cols, dx):
            trows = pl.ds(pl.multiple_of(rows.start + CH, ROWS), ROWS)
            kgrad[s, rows, cols] = (dx + thru[trows, cols]).astype(BF)

        e_at = lambda rows, cols: es[s + 1, rows, cols].astype(F32)
        d_at = lambda rows, cols: xs[s + 1, rows, cols].astype(F32)
        norm_bwd(ga, 0, e_at, g20[...], 20, emean.at[s], erstd.at[s], None, m_scr.at[0], q_scr.at[0], emit_e)
        norm_bwd(ga, CH, d_at, g20[...], 20, dmean.at[s], drstd.at[s], None, m_scr.at[1], q_scr.at[1], emit_d)
        pltpu.make_async_copy(kgrad.at[s], kgrad_out.at[s], isems.at[4]).start()
        return carry

    lax.fori_loop(0, SEGS, backward, 0)
    cgrad[...] = gcur[...]
    copy_bytes(kgrad, isems.at[4]).wait()


def down_backward_kernel(
    ids, asel, emb, g10, shift, cgrad,
    xs_in, mean_in, rstd_in, kgrad_in, own, p0, p1, p2, q0, q1, q2,
    gd_keep, gd_give,
    xs, mean, rstd, kgrad, wnat, wb, hstack, hcur, ga, ccur, m_scr, q_scr, sems, isems,
):
    arrays = ((kgrad_in, kgrad), (xs_in, xs), (mean_in, mean), (rstd_in, rstd))

    def inputs(s):
        return [pltpu.make_async_copy(a.at[s], b.at[s], isems.at[i, s]) for i, (a, b) in enumerate(arrays)]

    for s in reversed(range(SEGS)):
        inputs(s)[0].start()
        start_down_copies(ids, s, own, (p0, p1, p2, q0, q1, q2), wnat, sems)
        for c in inputs(s)[1:]:
            c.start()
    ccur[...] = cgrad[...]

    def take(s):
        for c in inputs(s):
            c.wait()
        copy_bytes(wnat.at[s], sems.at[s]).wait()

        def value(cols):
            h = (kgrad[s, :, cols].astype(F32) + ccur[:, cols].astype(F32)).astype(BF)
            hcur[:, cols] = h
            return h

        spread_grad(value, shift[...], hstack)

        @pl.when(s == ids[0])
        def _():
            for i, gd in enumerate((gd_keep, gd_give)):
                gd[...] = dot_nt(asel[i * (DOWN_SEL // 2) : (i + 1) * (DOWN_SEL // 2), :], hstack[...])

    def stage(i, carry):
        s = SEGS - 1 - i
        take(s)
        for k in range(3):
            wb[:, k * MAIN : (k + 1) * MAIN] = wnat[s, k * CH : (k + 1) * CH, :MAIN]
            wb[:, 3 * MAIN + k * REST : 3 * MAIN + (k + 1) * REST] = wnat[s, k * CH : (k + 1) * CH, MAIN:]
        ga[...] = dot(wb[...], hstack[...])
        x_at = lambda rows, cols: xs[s, rows, cols].astype(F32)

        def emit(rows, cols, dx):
            ccur[rows, cols] = (hcur[rows, cols].astype(F32) + dx).astype(BF)

        norm_bwd(ga, 0, x_at, g10[...], 10, mean.at[s], rstd.at[s], emb, m_scr, q_scr, emit)
        return carry

    lax.fori_loop(0, SEGS - 1, stage, 0)
    take(0)


VMEM = pl.BlockSpec(memory_space=pltpu.VMEM)
SMEM = pl.BlockSpec(memory_space=pltpu.SMEM)
ANY = pl.BlockSpec(memory_space=pl.ANY)
PARAMS = pltpu.CompilerParams(vmem_limit_bytes=60 * 1024 * 1024)


def shape(dims, dtype=BF):
    return jax.ShapeDtypeStruct(dims, dtype)


def cost(microseconds):
    return pl.CostEstimate(flops=int(microseconds * 1e9), bytes_accessed=0, transcendentals=0)


def run_down_forward(*args):
    return pl.pallas_call(
        down_forward_kernel,
        name="down_forward",
        out_shape=(
            shape((SEGS + 1, CH, TOK)),
            shape((SEGS, CH, LANES), F32),
            shape((SEGS, CH, LANES), F32),
            shape((DOWN_SEL, TOK)),
            shape((SEGS, 4, CH, TOK)),
            shape((SEGS, CH, LANES), F32),
            shape((SEGS, CH, LANES), F32),
        ),
        in_specs=[SMEM] + [VMEM] * 7 + [ANY] * 7,
        out_specs=(ANY,) * 3 + (VMEM,) + (ANY,) * 3,
        scratch_shapes=[
            pltpu.VMEM((SEGS + 1, CH, TOK), BF),
            pltpu.VMEM((SEGS, CH, LANES), F32),
            pltpu.VMEM((SEGS, CH, LANES), F32),
            pltpu.VMEM((SEGS, 4, CH, TOK), BF),
            pltpu.VMEM((SEGS, CH, LANES), F32),
            pltpu.VMEM((SEGS, CH, LANES), F32),
            pltpu.VMEM((SEGS, 3 * CH, CH), BF),
            pltpu.VMEM((CH, 3 * CH), BF),
            pltpu.VMEM((3, CH, TOK), BF),
            pltpu.VMEM((2, CH, LANES), F32),
            pltpu.VMEM((2, CH, LANES), F32),
            pltpu.SemaphoreType.DMA((SEGS,)),
            pltpu.SemaphoreType.DMA((6,)),
        ],
        compiler_params=PARAMS,
        cost_estimate=cost(1),
    )(*args)


def run_up(*args, scale):
    return pl.pallas_call(
        functools.partial(up_kernel, scale=scale),
        name="up_both",
        out_shape=(
            shape((UP_SEL // 2, 4 * CH), F32),
            shape((UP_SEL // 2, 4 * CH), F32),
            shape((CH, TOK)),
            shape((SEGS, CH, TOK)),
        ),
        in_specs=[SMEM] + [VMEM] * 6 + [ANY] * 12,
        out_specs=(VMEM,) * 3 + (ANY,),
        scratch_shapes=[
            pltpu.VMEM((SEGS + 1, CH, TOK), BF),
            pltpu.VMEM((SEGS, CH, LANES), F32),
            pltpu.VMEM((SEGS, CH, LANES), F32),
            pltpu.VMEM((SEGS, CH, TOK), BF),
            pltpu.VMEM((SEGS, CH, 8 * CH), BF),
            pltpu.VMEM((2 * CH, 1024 + 384), BF),
            pltpu.VMEM((2, 4, 2, CH, TOK), BF),
            pltpu.VMEM((UP_SEL, TOK), BF),
            pltpu.VMEM((UP_SEL, TOK), BF),
            pltpu.VMEM((SEGS + 1, CH, TOK), BF),
            pltpu.VMEM((SEGS, CH, LANES), F32),
            pltpu.VMEM((SEGS, CH, LANES), F32),
            pltpu.VMEM((2 * CH, TOK), F32),
            pltpu.VMEM((2 * CH, TOK), F32),
            pltpu.VMEM((CH, TOK), BF),
            pltpu.VMEM((3 * CH, TOK), BF),
            pltpu.VMEM((2, CH, LANES), F32),
            pltpu.VMEM((2, CH, LANES), F32),
            pltpu.SemaphoreType.DMA((SEGS,)),
            pltpu.SemaphoreType.DMA((2, 4)),
            pltpu.SemaphoreType.DMA((5,)),
        ],
        compiler_params=PARAMS,
        cost_estimate=cost(50),
    )(*args)


def run_down_backward(*args):
    return pl.pallas_call(
        down_backward_kernel,
        name="down_backward",
        out_shape=(shape((DOWN_SEL // 2, 3 * CH), F32),) * 2,
        in_specs=[SMEM] + [VMEM] * 5 + [ANY] * 11,
        out_specs=(VMEM,) * 2,
        scratch_shapes=[
            pltpu.VMEM((SEGS, CH, TOK), BF),
            pltpu.VMEM((SEGS, CH, LANES), F32),
            pltpu.VMEM((SEGS, CH, LANES), F32),
            pltpu.VMEM((SEGS, CH, TOK), BF),
            pltpu.VMEM((SEGS, 3 * CH, CH), BF),
            pltpu.VMEM((CH, 3 * CH), BF),
            pltpu.VMEM((3 * CH, TOK), BF),
            pltpu.VMEM((CH, TOK), BF),
            pltpu.VMEM((CH, TOK), F32),
            pltpu.VMEM((CH, TOK), BF),
            pltpu.VMEM((CH, LANES), F32),
            pltpu.VMEM((CH, LANES), F32),
            pltpu.SemaphoreType.DMA((SEGS,)),
            pltpu.SemaphoreType.DMA((4, SEGS)),
        ],
        compiler_params=PARAMS,
        cost_estimate=cost(15),
    )(*args)


def pick_matrix(x_index, core, per_device, channels):
    row = lax.broadcasted_iota(jnp.int32, (16 * per_device, 1), 0)
    col = lax.broadcasted_iota(jnp.int32, (16 * per_device, channels), 1)
    place = core ^ (row // (8 * per_device))
    want = ((row // per_device) % 8 * 8 + 2 * x_index + place) * per_device + row % per_device
    return (col == want).astype(BF)


def clip_inputs(clip, step_value, seed_value, in_weight, out_weight):
    lat_dim, pix_dim, frames = clip.shape
    noise = noise_field(seed_value, lat_dim, pix_dim)
    theta = step_value.astype(F32) * (0.5 * math.pi / 1000.0)
    noisy = (
        jnp.cos(theta) * clip.reshape(lat_dim, pix_dim * frames).astype(F32) + jnp.sin(theta) * noise
    ).astype(BF)
    noisy = jnp.pad(noisy, ((0, 16 - lat_dim), (0, 0)))
    in_t = jnp.pad(in_weight.T, ((0, 0), (0, 16 - lat_dim)))
    out_t = jnp.pad(out_weight.T, ((0, 16 - lat_dim), (0, 0)))
    emb = jnp.broadcast_to(time_embedding(step_value, CH)[:, None], (CH, LANES))
    return noise, noisy, in_t, out_t, emb


def swap_core(value):
    return lax.ppermute(value, "core", [(0, 1), (1, 0)])


def from_segment(value, away):
    return lax.ppermute(value, "segment", [((i + away) % SEGS, i) for i in range(SEGS)])


def fetch_sections(half):
    return [from_segment(half, away) for away in (1, 3, 2)]


def taps(value):
    return jnp.stack(
        [
            jnp.concatenate(
                [
                    value[:, k * MAIN : (k + 1) * MAIN],
                    value[:, 3 * MAIN + k * REST : 3 * MAIN + (k + 1) * REST],
                ],
                axis=1,
            )
            for k in range(3)
        ]
    )


def clip_gradients(ids, clip, step_value, seed_value, x_index, in_weight, out_weight, down, up, reduce_up):
    noise, noisy, in_t, out_t, emb = clip_inputs(clip, step_value, seed_value, in_weight, out_weight)
    g10 = jnp.asarray(group_matrix(10), BF)
    g20 = jnp.asarray(group_matrix(20), BF)
    shift = jnp.asarray(shift_matrix(), BF)
    pick_d = pick_matrix(x_index, ids[1], 5, CH)
    pick_u = pick_matrix(x_index, ids[1], 10, 2 * CH)
    weights = down()
    xs, mean, rstd, asel, dstack, dmean, drstd = run_down_forward(
        ids, noisy, in_t, emb, g10, g20, shift, pick_d, *weights
    )
    xs, up_args = up(xs)
    gu_keep, gu_give, cgrad, kgrad = run_up(
        ids, g20, shift, pick_u, out_t, out_weight.astype(F32), noise, xs, dmean, drstd, dstack, *up_args,
        scale=64.0 / math.sqrt(16 * FRAMES * 4 * 64),
    )
    up_part = reduce_up(gu_keep, gu_give)
    gd = run_down_backward(ids, asel, emb, g10, shift, cgrad, xs, mean, rstd, kgrad, *weights)
    return gd, up_part


def whole_clip(latents, core, x_index):
    own = lax.dynamic_index_in_dim(latents, core, 0, keepdims=False)
    got = swap_core(lax.dynamic_index_in_dim(latents, 1 - core, 0, keepdims=False))
    half = lax.broadcasted_iota(jnp.int32, (2,) + own.shape, 0)
    quad = jnp.where(half == core, own[None], got[None])
    quads = [quad] + [
        lax.ppermute(quad, "x", [((i + away) % 4, i) for i in range(4)]) for away in (1, 2, 3)
    ]
    away = (lax.broadcasted_iota(jnp.int32, (4,) + quad.shape, 0) - x_index) & 3
    whole = quads[3][None]
    for i in (2, 1, 0):
        whole = jnp.where(away == i, quads[i][None], whole)
    return whole.reshape((FRAMES,) + own.shape[1:])


def local(latents, timesteps, seeds, in_weight, out_weight, down_weight, up_weight, skip_weight):
    seg = lax.axis_index("segment")
    core = lax.axis_index("core")
    x_index = lax.axis_index("x")
    ids = jnp.stack([seg, core]).astype(jnp.int32)
    down_nat = down_weight[0].reshape(3 * CH, CH)
    up_t = jnp.transpose(up_weight[0], (0, 2, 1))
    skip_t = skip_weight[0].T
    d_half = lax.dynamic_slice_in_dim(down_nat, core * (3 * CH // 2), 3 * CH // 2, 0)
    u_half = jnp.concatenate(
        [
            lax.dynamic_slice_in_dim(up_t, core * (CH // 2), CH // 2, 1),
            lax.dynamic_slice_in_dim(skip_t, core * (CH // 2), CH // 2, 0)[None],
        ],
        axis=0,
    )
    d_mine = fetch_sections(d_half)
    d_mine[0], u_half = lax.optimization_barrier((d_mine[0], u_half))
    u_mine = fetch_sections(u_half)

    clip = jnp.transpose(whole_clip(latents, core, x_index), (1, 2, 0))
    step_value = lax.dynamic_index_in_dim(timesteps, core, 0, keepdims=False)
    seed_value = lax.dynamic_index_in_dim(seeds, core, 0, keepdims=False)

    def down():
        return [down_nat, *d_mine, *[swap_core(p) for p in d_mine]]

    def up(xs):
        *parts, xs = lax.optimization_barrier((*u_mine, xs))
        return xs, [up_t, skip_t, *parts, *[swap_core(p) for p in parts]]

    def cores_sum(keep, give):
        return (keep + swap_core(give)).reshape(8, -1)

    gd, up_part = clip_gradients(
        ids, clip, step_value, seed_value, x_index, in_weight, out_weight, down, up, cores_sum
    )
    down_part = cores_sum(*gd)
    parts = lax.all_to_all(jnp.concatenate([down_part, up_part], axis=1), "dp", 0, 0, tiled=True)
    total = jnp.sum(parts, axis=0)
    down_sum = taps(total[: down_part.shape[1]].reshape(5, -1))
    up_sum = total[down_part.shape[1] :].reshape(10, -1)
    return down_sum[None], taps(up_sum[:, : 3 * CH])[None], up_sum[:, 3 * CH :][None]


def solution(mesh):
    devices = mesh.devices
    grid = Mesh(devices.reshape(devices.shape[0], devices.shape[1], 4, 2), ("dp", "segment", "x", "core"))
    tm = ("x", "core")
    return jax.shard_map(
        local,
        mesh=grid,
        in_specs=(
            P("dp", tm, None, None),
            P("dp"),
            P("dp"),
            P(),
            P(),
            P("segment", None, None, None),
            P("segment", None, None, None),
            P("segment", None, None),
        ),
        out_specs=(
            P("segment", None, ("dp",) + tm, None),
            P("segment", None, ("dp",) + tm, None),
            P("segment", ("dp",) + tm, None),
        ),
        check_vma=False,
    )
```

```python
import functools
import math

import jax
import jax.numpy as jnp
import numpy as np
from jax import lax
from jax.experimental import pallas as pl
from jax.experimental.pallas import tpu as pltpu
from jax.sharding import Mesh
from jax.sharding import PartitionSpec as P

CH = 320
GROUPS = 32
SEGS = 4
TOK = 1024
FRAMES = 16
LANES = 128
TILES = TOK // LANES
ROWS = 32
BF = jnp.bfloat16
F32 = jnp.float32
DOWN_SEL = 80
UP_SEL = 160


def mix_bits(value):
    value = value ^ lax.shift_right_logical(value, jnp.int32(16))
    value = value * -2048144789
    value = value ^ lax.shift_right_logical(value, jnp.int32(13))
    value = value * -1028477387
    value = value ^ lax.shift_right_logical(value, jnp.int32(16))
    return value


def noise_field(seed_value, lat_dim, pix_dim):
    lat_ids = lax.broadcasted_iota(jnp.int32, (lat_dim, pix_dim * FRAMES), 0)
    tokens = lax.broadcasted_iota(jnp.int32, (lat_dim, pix_dim * FRAMES), 1)
    frame_ids = tokens % FRAMES
    pix_ids = tokens // FRAMES
    index = (frame_ids * lat_dim + lat_ids) * pix_dim + pix_ids
    salted = seed_value * -1640531535
    first = mix_bits(index * 2 + salted)
    second = mix_bits(index * 2 + 1 + salted)
    unit_a = (lax.shift_right_logical(first, jnp.int32(8)).astype(F32) + 0.5) / 16777216.0
    unit_b = (lax.shift_right_logical(second, jnp.int32(8)).astype(F32) + 0.5) / 16777216.0
    return jnp.sqrt(-2.0 * jnp.log(unit_a)) * jnp.cos(2.0 * math.pi * unit_b)


def time_embedding(step_value, channels):
    half = channels // 2
    frequency = jnp.exp(-math.log(10000.0) * jnp.arange(half, dtype=F32) / half)
    phase = step_value.astype(F32) * frequency
    return jnp.concatenate([jnp.sin(phase), jnp.cos(phase)])


def group_matrix(size):
    ids = np.arange(CH) // size
    return (ids[:, None] == ids[None, :]).astype(np.float32)


def dot(a, b):
    return jnp.dot(a, b, preferred_element_type=F32)


def dot_nt(a, b):
    return lax.dot_general(a, b, (((1,), (1,)), ((), ())), preferred_element_type=F32)


def tile(j):
    return slice(j * LANES, (j + 1) * LANES)


def row_block(r):
    return pl.ds(pl.multiple_of(r * ROWS, ROWS), ROWS)


def fold(value):
    for step in (16, 32, 64):
        value = value + pltpu.roll(value, step, 1)
    return value


def group_sums(group, values, parts):
    pieces = []
    for value in values:
        rest = value
        for _ in range(parts):
            piece = rest.astype(BF)
            pieces.append(piece)
            rest = rest - piece.astype(F32)
    sums = dot(group, jnp.concatenate(pieces, axis=1))
    out = []
    for i in range(len(values)):
        total = sums[:, tile(i * parts)]
        for q in range(1, parts):
            total = total + sums[:, tile(i * parts + q)]
        out.append(fold(total))
    return out


def gn_stats(x_at, group, size, m_scr, q_scr, mean_at, rstd_at):
    def body(r, carry):
        rows = row_block(r)
        parts = [x_at(rows, tile(j)) for j in range(TILES)]
        total = parts[0]
        for p in parts[1:]:
            total = total + p
        mid = total * (1.0 / TILES)
        square = None
        for p in parts:
            d = p - mid
            square = d * d if square is None else square + d * d
        m_scr[rows, :] = mid
        q_scr[rows, :] = square
        return carry

    lax.fori_loop(0, CH // ROWS, body, 0, unroll=True)
    mid = m_scr[...]
    (mean,) = group_sums(group, [mid], 3)
    mean = mean * (1.0 / (8 * size))
    away = mid - mean
    (spread,) = group_sums(group, [q_scr[...] + (TILES * 1.0) * away * away], 2)
    mean_at[...] = mean
    rstd_at[...] = lax.rsqrt(spread * (1.0 / (64 * size)) + 1e-05)


def shift_matrix():
    lane = np.arange(LANES)
    out = np.zeros((LANES, 2 * LANES), np.float32)
    for l in lane:
        if l % FRAMES != 0:
            out[l - 1, l] = 1.0
        if l % FRAMES != FRAMES - 1:
            out[l + 1, LANES + l] = 1.0
    return out


def neighbours(value, shift):
    both = dot(value, shift).astype(BF)
    return both[:, :LANES], both[:, LANES:]


def silu_parts(y):
    sig = 0.5 * jnp.tanh(0.5 * y) + 0.5
    return sig, y * sig


def norm_bwd(ga_ref, ga_off, x_at, group, size, mean_at, rstd_at, emb_ref, m_scr, q_scr, emit):
    def first(r, carry):
        rows = row_block(r)
        grows = pl.ds(pl.multiple_of(ga_off + r * ROWS, ROWS), ROWS)
        mean = mean_at[rows, :]
        rstd = rstd_at[rows, :]
        emb = None if emb_ref is None else emb_ref[rows, :]
        s1 = None
        s2 = None
        for j in range(TILES):
            xhat = (x_at(rows, tile(j)) - mean) * rstd
            y = xhat if emb is None else xhat + emb
            sig, act = silu_parts(y)
            dy = ga_ref[grows, tile(j)] * (sig + act * (1.0 - sig))
            ga_ref[grows, tile(j)] = dy
            s1 = dy if s1 is None else s1 + dy
            s2 = dy * xhat if s2 is None else s2 + dy * xhat
        m_scr[rows, :] = s1
        q_scr[rows, :] = s2
        return carry

    lax.fori_loop(0, CH // ROWS, first, 0, unroll=True)
    s1, s2 = group_sums(group, [m_scr[...], q_scr[...]], 2)
    scale = 1.0 / (64 * size)
    m_scr[...] = s1 * scale
    q_scr[...] = s2 * scale

    def second(r, carry):
        rows = row_block(r)
        grows = pl.ds(pl.multiple_of(ga_off + r * ROWS, ROWS), ROWS)
        mean = mean_at[rows, :]
        rstd = rstd_at[rows, :]
        m1 = m_scr[rows, :]
        m2 = q_scr[rows, :]
        for j in range(TILES):
            xhat = (x_at(rows, tile(j)) - mean) * rstd
            emit(rows, tile(j), rstd * (ga_ref[grows, tile(j)] - m1 - xhat * m2))
        return carry

    lax.fori_loop(0, CH // ROWS, second, 0, unroll=True)


MAIN = 256
REST = CH - MAIN


def copy_bytes(ref, sem):
    return pltpu.make_async_copy(ref, ref, sem)


def section_of(seg, slot):
    return lax.rem(seg + (1, 3, 2)[slot], SEGS)


def start_section(ids, s, own, pieces):
    away = lax.rem(s + SEGS - ids[0], SEGS)
    pl.when(away == 0)(own)
    for slot, distance in enumerate((1, 3, 2)):

        @pl.when(away == distance)
        def _():
            pieces(slot, ids[1])
            pieces(3 + slot, 1 - ids[1])


def start_down_copies(ids, s, own, parts, dest, sems):
    half = 3 * CH // 2

    def pieces(part, place):
        rows = pl.ds(pl.multiple_of(place * half, 32), half)
        pltpu.make_async_copy(parts[part], dest.at[s, rows, :], sems.at[s]).start()

    start_section(ids, s, lambda: pltpu.make_async_copy(own, dest.at[s], sems.at[s]).start(), pieces)


def start_up_copies(ids, s, own_up, own_skip, parts, dest, sems):
    half = CH // 2

    def mine():
        for k in range(4):
            source = own_up.at[k] if k < 3 else own_skip
            pltpu.make_async_copy(source, dest.at[s, :, k * 640 : (k + 1) * 640], sems.at[s]).start()

    def pieces(part, place):
        rows = pl.ds(pl.multiple_of(place * half, 32), half)
        for k in range(4):
            pltpu.make_async_copy(
                parts[part].at[k], dest.at[s, rows, k * 640 : (k + 1) * 640], sems.at[s]
            ).start()

    start_section(ids, s, mine, pieces)


def activate(x_at, mean_at, rstd_at, emb_ref, put):
    def act(r, carry):
        rows = row_block(r)
        mu = mean_at[rows, :]
        rs = rstd_at[rows, :]
        e = None if emb_ref is None else emb_ref[rows, :]
        for j in range(TILES):
            y = (x_at(rows, tile(j)) - mu) * rs
            if e is not None:
                y = y + e
            put(rows, tile(j), silu_parts(y)[1].astype(BF))
        return carry

    lax.fori_loop(0, CH // ROWS, act, 0, unroll=True)


def down_forward_kernel(
    ids, noisy, in_t, emb, g10, g20, shift, pick, own, p0, p1, p2, q0, q1, q2,
    xs_out, mean_out, rstd_out, asel, dstack_out, dmean_out, drstd_out,
    xs, mean, rstd, dstack, dmean, drstd, wnat, wt, stack, m_scr, q_scr, sems, osems,
):
    def send(array, out, index, sem):
        pltpu.make_async_copy(array.at[index], out.at[index], osems.at[sem]).start()

    for s in range(SEGS):
        start_down_copies(ids, s, own, (p0, p1, p2, q0, q1, q2), wnat, sems)
    xs[0] = dot(in_t[...], noisy[...]).astype(BF)
    send(xs, xs_out, 0, 0)

    def ahead(s):
        x_at = lambda rows, cols: xs[s + 1, rows, cols].astype(F32)
        gn_stats(x_at, g20[...], 20, m_scr.at[1], q_scr.at[1], dmean.at[s], drstd.at[s])

        def put(rows, cols, a):
            dstack[s, 1, rows, cols] = a

        activate(x_at, dmean.at[s], drstd.at[s], None, put)
        for j in range(TILES):
            before, after = neighbours(dstack[s, 1, :, tile(j)], shift[...])
            dstack[s, 0, :, tile(j)] = before
            dstack[s, 2, :, tile(j)] = after
        dstack[s, 3] = xs[s + 1]

    def send_ahead(s):
        send(dstack, dstack_out, s, 3)
        send(dmean, dmean_out, s, 4)
        send(drstd, drstd_out, s, 5)

    def stage(s, behind):
        x_at = lambda rows, cols: xs[s, rows, cols].astype(F32)
        gn_stats(x_at, g10[...], 10, m_scr.at[0], q_scr.at[0], mean.at[s], rstd.at[s])

        def put(rows, cols, a):
            stack[1, rows, cols] = a

        activate(x_at, mean.at[s], rstd.at[s], emb, put)
        for j in range(TILES):
            before, after = neighbours(stack[1, :, tile(j)], shift[...])
            stack[0, :, tile(j)] = before
            stack[2, :, tile(j)] = after

        @pl.when(s == ids[0])
        def _():
            asel[...] = dot(pick[...], stack[1]).astype(BF)

        copy_bytes(wnat.at[s], sems.at[s]).wait()
        for begin in range(0, 3 * CH, LANES):
            size = min(LANES, 3 * CH - begin)
            wt[:, begin : begin + size] = wnat[s, begin : begin + size, :].T
        total = dot(wt[...], stack[...].reshape(3 * CH, TOK)) + xs[s].astype(F32)
        xs[s + 1] = total.astype(BF)
        if behind:
            ahead(s - 1)
            send_ahead(s - 1)
        send(xs, xs_out, s + 1, 0)
        send(mean, mean_out, s, 1)
        send(rstd, rstd_out, s, 2)

    stage(0, False)

    def later_stage(s, carry):
        stage(s, True)
        return carry

    lax.fori_loop(1, SEGS, later_stage, 0)
    ahead(SEGS - 1)
    send_ahead(SEGS - 1)
    for sem, array in enumerate((xs, mean, rstd, dstack, dmean, drstd)):
        copy_bytes(array, osems.at[sem]).wait()


def spread_grad(value, shift, gstack):
    for j in range(TILES):
        g = value(tile(j))
        before, after = neighbours(g, shift)
        for k, part in ((0, after), (1, g), (2, before)):
            gstack[k * MAIN : (k + 1) * MAIN, tile(j)] = part[:MAIN]
            gstack[3 * MAIN + k * REST : 3 * MAIN + (k + 1) * REST, tile(j)] = part[MAIN:]


def up_kernel(
    ids, g20, shift, pick, out_t, out_wide, noise,
    xs_in, dmean_in, drstd_in, dstack, own_up, own_skip, p0, p1, p2, q0, q1, q2,
    gu_keep, gu_give, cgrad, kgrad_out,
    xs, dmean, drstd, kgrad, wt, wb, stack, bsel, jsel, es, emean, erstd, ga, thru, gcur, gstack, m_scr, q_scr,
    sems, dsems, isems, *, scale
):
    top = pltpu.make_async_copy(xs_in.at[SEGS], es.at[SEGS], isems.at[0])
    top.start()

    def fetch(s):
        slot = lax.rem(s, 2)
        for k in range(4):
            pltpu.make_async_copy(dstack.at[s, k], stack.at[slot, k, 1], dsems.at[slot, k]).start()

    fetch(jnp.int32(SEGS - 1))
    for s in reversed(range(SEGS)):
        start_up_copies(ids, s, own_up, own_skip, (p0, p1, p2, q0, q1, q2), wt, sems)
    late = [
        pltpu.make_async_copy(a, b, isems.at[1 + i])
        for i, (a, b) in enumerate(((xs_in, xs), (dmean_in, dmean), (drstd_in, drstd)))
    ]
    for c in late:
        c.start()
    top.wait()

    def forward(i, carry):
        s = SEGS - 1 - i
        slot = lax.rem(s, 2)

        @pl.when(s > 0)
        def _():
            fetch(s - 1)

        x_at = lambda rows, cols: es[s + 1, rows, cols].astype(F32)
        gn_stats(x_at, g20[...], 20, m_scr.at[0], q_scr.at[0], emean.at[s], erstd.at[s])

        def put(rows, cols, a):
            stack[slot, 1, 0, rows, cols] = a

        activate(x_at, emean.at[s], erstd.at[s], None, put)
        for j in range(TILES):
            before, after = neighbours(stack[slot, 1, 0, :, tile(j)], shift[...])
            stack[slot, 0, 0, :, tile(j)] = before
            stack[slot, 2, 0, :, tile(j)] = after
        stack[slot, 3, 0] = es[s + 1]
        for k in range(4):
            pltpu.make_async_copy(dstack.at[s, k], stack.at[slot, k, 1], dsems.at[slot, k]).wait()

        @pl.when(s == ids[0])
        def _():
            bsel[...] = dot(pick[...], stack[slot, 1].reshape(2 * CH, TOK)).astype(BF)
            jsel[...] = dot(pick[...], stack[slot, 3].reshape(2 * CH, TOK)).astype(BF)

        copy_bytes(wt.at[s], sems.at[s]).wait()
        es[s] = dot(wt[s], stack[slot].reshape(8 * CH, TOK)).astype(BF)
        return carry

    lax.fori_loop(0, SEGS, forward, 0)

    for c in late:
        c.wait()
    predicted = dot(out_t[...], es[0])
    thru[0:4, :] = (predicted[:4] - noise[...]) * scale

    def seed(r, carry):
        rows = row_block(r)
        for j in range(TILES):
            total = out_wide[rows, 0:1] * thru[0:1, tile(j)]
            for l in range(1, 4):
                total = total + out_wide[rows, l : l + 1] * thru[l : l + 1, tile(j)]
            gcur[rows, tile(j)] = total.astype(BF)
        return carry

    lax.fori_loop(0, CH // ROWS, seed, 0, unroll=True)

    def backward(s, carry):
        for k in range(3):
            for b in range(2):
                wb[:, k * MAIN + b * LANES : k * MAIN + (b + 1) * LANES] = wt[
                    s, b * LANES : (b + 1) * LANES, k * 640 : (k + 1) * 640
                ].T
        tops = [wt[s, MAIN:, k * 640 : (k + 1) * 640] for k in range(3)]
        wb[:, 3 * MAIN : 3 * MAIN + LANES] = jnp.concatenate(tops[:2], axis=0).T
        wb[:, 3 * MAIN + LANES : 3 * CH] = tops[2].T
        for b in range(2):
            wb[:, 1024 + b * LANES : 1024 + (b + 1) * LANES] = wt[s, b * LANES : (b + 1) * LANES, 1920:].T
        wb[:, 1024 + MAIN : 1024 + CH] = wt[s, MAIN:, 1920:].T
        spread_grad(lambda cols: gcur[:, cols], shift[...], gstack)

        @pl.when(s == ids[0])
        def _():
            for i, gu in enumerate((gu_keep, gu_give)):
                rows = slice(i * (UP_SEL // 2), (i + 1) * (UP_SEL // 2))
                gu[:, : 3 * CH] = dot_nt(bsel[rows, :], gstack[...])
                gu[:, 3 * CH :] = dot_nt(jsel[rows, :], gcur[...])

        ga[...] = dot(wb[:, : 3 * CH], gstack[...])
        thru[...] = dot(wb[:, 1024 : 1024 + CH], gcur[...])

        def emit_e(rows, cols, dx):
            gcur[rows, cols] = (dx + thru[rows, cols]).astype(BF)

        def emit_d(rows, cols, dx):
            trows = pl.ds(pl.multiple_of(rows.start + CH, ROWS), ROWS)
            kgrad[s, rows, cols] = (dx + thru[trows, cols]).astype(BF)

        e_at = lambda rows, cols: es[s + 1, rows, cols].astype(F32)
        d_at = lambda rows, cols: xs[s + 1, rows, cols].astype(F32)
        norm_bwd(ga, 0, e_at, g20[...], 20, emean.at[s], erstd.at[s], None, m_scr.at[0], q_scr.at[0], emit_e)
        norm_bwd(ga, CH, d_at, g20[...], 20, dmean.at[s], drstd.at[s], None, m_scr.at[1], q_scr.at[1], emit_d)
        pltpu.make_async_copy(kgrad.at[s], kgrad_out.at[s], isems.at[4]).start()
        return carry

    lax.fori_loop(0, SEGS, backward, 0)
    cgrad[...] = gcur[...]
    copy_bytes(kgrad, isems.at[4]).wait()


def down_backward_kernel(
    ids, asel, emb, g10, shift, cgrad,
    xs_in, mean_in, rstd_in, kgrad_in, own, p0, p1, p2, q0, q1, q2,
    gd_keep, gd_give,
    xs, mean, rstd, kgrad, wnat, wb, hstack, hcur, ga, ccur, m_scr, q_scr, sems, isems,
):
    arrays = ((kgrad_in, kgrad), (xs_in, xs), (mean_in, mean), (rstd_in, rstd))

    def inputs(s):
        return [pltpu.make_async_copy(a.at[s], b.at[s], isems.at[i, s]) for i, (a, b) in enumerate(arrays)]

    for s in reversed(range(SEGS)):
        inputs(s)[0].start()
        start_down_copies(ids, s, own, (p0, p1, p2, q0, q1, q2), wnat, sems)
        for c in inputs(s)[1:]:
            c.start()
    ccur[...] = cgrad[...]

    def take(s):
        for c in inputs(s):
            c.wait()
        copy_bytes(wnat.at[s], sems.at[s]).wait()

        def value(cols):
            h = (kgrad[s, :, cols].astype(F32) + ccur[:, cols].astype(F32)).astype(BF)
            hcur[:, cols] = h
            return h

        spread_grad(value, shift[...], hstack)

        @pl.when(s == ids[0])
        def _():
            for i, gd in enumerate((gd_keep, gd_give)):
                gd[...] = dot_nt(asel[i * (DOWN_SEL // 2) : (i + 1) * (DOWN_SEL // 2), :], hstack[...])

    def stage(i, carry):
        s = SEGS - 1 - i
        take(s)
        for k in range(3):
            wb[:, k * MAIN : (k + 1) * MAIN] = wnat[s, k * CH : (k + 1) * CH, :MAIN]
            wb[:, 3 * MAIN + k * REST : 3 * MAIN + (k + 1) * REST] = wnat[s, k * CH : (k + 1) * CH, MAIN:]
        ga[...] = dot(wb[...], hstack[...])
        x_at = lambda rows, cols: xs[s, rows, cols].astype(F32)

        def emit(rows, cols, dx):
            ccur[rows, cols] = (hcur[rows, cols].astype(F32) + dx).astype(BF)

        norm_bwd(ga, 0, x_at, g10[...], 10, mean.at[s], rstd.at[s], emb, m_scr, q_scr, emit)
        return carry

    lax.fori_loop(0, SEGS - 1, stage, 0)
    take(0)


VMEM = pl.BlockSpec(memory_space=pltpu.VMEM)
SMEM = pl.BlockSpec(memory_space=pltpu.SMEM)
ANY = pl.BlockSpec(memory_space=pl.ANY)
PARAMS = pltpu.CompilerParams(vmem_limit_bytes=60 * 1024 * 1024)


def shape(dims, dtype=BF):
    return jax.ShapeDtypeStruct(dims, dtype)


def cost(microseconds):
    return pl.CostEstimate(flops=int(microseconds * 1e9), bytes_accessed=0, transcendentals=0)


def run_down_forward(*args):
    return pl.pallas_call(
        down_forward_kernel,
        name="down_forward",
        out_shape=(
            shape((SEGS + 1, CH, TOK)),
            shape((SEGS, CH, LANES), F32),
            shape((SEGS, CH, LANES), F32),
            shape((DOWN_SEL, TOK)),
            shape((SEGS, 4, CH, TOK)),
            shape((SEGS, CH, LANES), F32),
            shape((SEGS, CH, LANES), F32),
        ),
        in_specs=[SMEM] + [VMEM] * 7 + [ANY] * 7,
        out_specs=(ANY,) * 3 + (VMEM,) + (ANY,) * 3,
        scratch_shapes=[
            pltpu.VMEM((SEGS + 1, CH, TOK), BF),
            pltpu.VMEM((SEGS, CH, LANES), F32),
            pltpu.VMEM((SEGS, CH, LANES), F32),
            pltpu.VMEM((SEGS, 4, CH, TOK), BF),
            pltpu.VMEM((SEGS, CH, LANES), F32),
            pltpu.VMEM((SEGS, CH, LANES), F32),
            pltpu.VMEM((SEGS, 3 * CH, CH), BF),
            pltpu.VMEM((CH, 3 * CH), BF),
            pltpu.VMEM((3, CH, TOK), BF),
            pltpu.VMEM((2, CH, LANES), F32),
            pltpu.VMEM((2, CH, LANES), F32),
            pltpu.SemaphoreType.DMA((SEGS,)),
            pltpu.SemaphoreType.DMA((6,)),
        ],
        compiler_params=PARAMS,
        cost_estimate=cost(1),
    )(*args)


def run_up(*args, scale):
    return pl.pallas_call(
        functools.partial(up_kernel, scale=scale),
        name="up_both",
        out_shape=(
            shape((UP_SEL // 2, 4 * CH), F32),
            shape((UP_SEL // 2, 4 * CH), F32),
            shape((CH, TOK)),
            shape((SEGS, CH, TOK)),
        ),
        in_specs=[SMEM] + [VMEM] * 6 + [ANY] * 12,
        out_specs=(VMEM,) * 3 + (ANY,),
        scratch_shapes=[
            pltpu.VMEM((SEGS + 1, CH, TOK), BF),
            pltpu.VMEM((SEGS, CH, LANES), F32),
            pltpu.VMEM((SEGS, CH, LANES), F32),
            pltpu.VMEM((SEGS, CH, TOK), BF),
            pltpu.VMEM((SEGS, CH, 8 * CH), BF),
            pltpu.VMEM((2 * CH, 1024 + 384), BF),
            pltpu.VMEM((2, 4, 2, CH, TOK), BF),
            pltpu.VMEM((UP_SEL, TOK), BF),
            pltpu.VMEM((UP_SEL, TOK), BF),
            pltpu.VMEM((SEGS + 1, CH, TOK), BF),
            pltpu.VMEM((SEGS, CH, LANES), F32),
            pltpu.VMEM((SEGS, CH, LANES), F32),
            pltpu.VMEM((2 * CH, TOK), F32),
            pltpu.VMEM((2 * CH, TOK), F32),
            pltpu.VMEM((CH, TOK), BF),
            pltpu.VMEM((3 * CH, TOK), BF),
            pltpu.VMEM((2, CH, LANES), F32),
            pltpu.VMEM((2, CH, LANES), F32),
            pltpu.SemaphoreType.DMA((SEGS,)),
            pltpu.SemaphoreType.DMA((2, 4)),
            pltpu.SemaphoreType.DMA((5,)),
        ],
        compiler_params=PARAMS,
        cost_estimate=cost(50),
    )(*args)


def run_down_backward(*args):
    return pl.pallas_call(
        down_backward_kernel,
        name="down_backward",
        out_shape=(shape((DOWN_SEL // 2, 3 * CH), F32),) * 2,
        in_specs=[SMEM] + [VMEM] * 5 + [ANY] * 11,
        out_specs=(VMEM,) * 2,
        scratch_shapes=[
            pltpu.VMEM((SEGS, CH, TOK), BF),
            pltpu.VMEM((SEGS, CH, LANES), F32),
            pltpu.VMEM((SEGS, CH, LANES), F32),
            pltpu.VMEM((SEGS, CH, TOK), BF),
            pltpu.VMEM((SEGS, 3 * CH, CH), BF),
            pltpu.VMEM((CH, 3 * CH), BF),
            pltpu.VMEM((3 * CH, TOK), BF),
            pltpu.VMEM((CH, TOK), BF),
            pltpu.VMEM((CH, TOK), F32),
            pltpu.VMEM((CH, TOK), BF),
            pltpu.VMEM((CH, LANES), F32),
            pltpu.VMEM((CH, LANES), F32),
            pltpu.SemaphoreType.DMA((SEGS,)),
            pltpu.SemaphoreType.DMA((4, SEGS)),
        ],
        compiler_params=PARAMS,
        cost_estimate=cost(15),
    )(*args)


def pick_matrix(x_index, core, per_device, channels):
    row = lax.broadcasted_iota(jnp.int32, (16 * per_device, 1), 0)
    col = lax.broadcasted_iota(jnp.int32, (16 * per_device, channels), 1)
    place = core ^ (row // (8 * per_device))
    want = ((row // per_device) % 8 * 8 + 2 * x_index + place) * per_device + row % per_device
    return (col == want).astype(BF)


def clip_inputs(clip, step_value, seed_value, in_weight, out_weight):
    lat_dim, pix_dim, frames = clip.shape
    noise = noise_field(seed_value, lat_dim, pix_dim)
    theta = step_value.astype(F32) * (0.5 * math.pi / 1000.0)
    noisy = (
        jnp.cos(theta) * clip.reshape(lat_dim, pix_dim * frames).astype(F32) + jnp.sin(theta) * noise
    ).astype(BF)
    noisy = jnp.pad(noisy, ((0, 16 - lat_dim), (0, 0)))
    in_t = jnp.pad(in_weight.T, ((0, 0), (0, 16 - lat_dim)))
    out_t = jnp.pad(out_weight.T, ((0, 16 - lat_dim), (0, 0)))
    emb = jnp.broadcast_to(time_embedding(step_value, CH)[:, None], (CH, LANES))
    return noise, noisy, in_t, out_t, emb


def swap_core(value):
    return lax.ppermute(value, "core", [(0, 1), (1, 0)])


def from_segment(value, away):
    return lax.ppermute(value, "segment", [((i + away) % SEGS, i) for i in range(SEGS)])


def fetch_sections(half):
    return [from_segment(half, away) for away in (1, 3, 2)]


def taps(value):
    return jnp.stack(
        [
            jnp.concatenate(
                [
                    value[:, k * MAIN : (k + 1) * MAIN],
                    value[:, 3 * MAIN + k * REST : 3 * MAIN + (k + 1) * REST],
                ],
                axis=1,
            )
            for k in range(3)
        ]
    )


def clip_gradients(ids, clip, step_value, seed_value, x_index, in_weight, out_weight, down, up, reduce_up):
    noise, noisy, in_t, out_t, emb = clip_inputs(clip, step_value, seed_value, in_weight, out_weight)
    g10 = jnp.asarray(group_matrix(10), BF)
    g20 = jnp.asarray(group_matrix(20), BF)
    shift = jnp.asarray(shift_matrix(), BF)
    pick_d = pick_matrix(x_index, ids[1], 5, CH)
    pick_u = pick_matrix(x_index, ids[1], 10, 2 * CH)
    weights = down()
    xs, mean, rstd, asel, dstack, dmean, drstd = run_down_forward(
        ids, noisy, in_t, emb, g10, g20, shift, pick_d, *weights
    )
    xs, up_args = up(xs)
    gu_keep, gu_give, cgrad, kgrad = run_up(
        ids, g20, shift, pick_u, out_t, out_weight.astype(F32), noise, xs, dmean, drstd, dstack, *up_args,
        scale=64.0 / math.sqrt(16 * FRAMES * 4 * 64),
    )
    up_part = reduce_up(gu_keep, gu_give)
    gd = run_down_backward(ids, asel, emb, g10, shift, cgrad, xs, mean, rstd, kgrad, *weights)
    return gd, up_part


def clip_parts(latents, core):
    own = lax.dynamic_index_in_dim(latents, core, 0, keepdims=False)
    got = swap_core(lax.dynamic_index_in_dim(latents, 1 - core, 0, keepdims=False))
    half = lax.broadcasted_iota(jnp.int32, (2,) + own.shape, 0)
    quad = jnp.where(half == core, own[None], got[None])
    return [quad] + [lax.ppermute(quad, "x", [((i + away) % 4, i) for i in range(4)]) for away in (1, 2, 3)]


def whole_clip(quads, x_index):
    quad = quads[0]
    away = (lax.broadcasted_iota(jnp.int32, (4,) + quad.shape, 0) - x_index) & 3
    whole = quads[3][None]
    for i in (2, 1, 0):
        whole = jnp.where(away == i, quads[i][None], whole)
    return whole.reshape((FRAMES,) + quad.shape[2:])


def local(latents, timesteps, seeds, in_weight, out_weight, down_weight, up_weight, skip_weight):
    seg = lax.axis_index("segment")
    core = lax.axis_index("core")
    x_index = lax.axis_index("x")
    ids = jnp.stack([seg, core]).astype(jnp.int32)
    down_nat = down_weight[0].reshape(3 * CH, CH)
    up_t = jnp.transpose(up_weight[0], (0, 2, 1))
    skip_t = skip_weight[0].T
    d_half = lax.dynamic_slice_in_dim(down_nat, core * (3 * CH // 2), 3 * CH // 2, 0)
    u_half = jnp.concatenate(
        [
            lax.dynamic_slice_in_dim(up_t, core * (CH // 2), CH // 2, 1),
            lax.dynamic_slice_in_dim(skip_t, core * (CH // 2), CH // 2, 0)[None],
        ],
        axis=0,
    )
    d_mine = fetch_sections(d_half)
    quads = clip_parts(latents, core)
    *moved, u_half = lax.optimization_barrier((*d_mine, *quads, u_half))
    d_mine, quads = moved[:3], moved[3:]
    u_mine = fetch_sections(u_half)

    clip = jnp.transpose(whole_clip(quads, x_index), (1, 2, 0))
    step_value = lax.dynamic_index_in_dim(timesteps, core, 0, keepdims=False)
    seed_value = lax.dynamic_index_in_dim(seeds, core, 0, keepdims=False)

    def down():
        return [down_nat, *d_mine, *[swap_core(p) for p in d_mine]]

    def up(xs):
        *parts, xs = lax.optimization_barrier((*u_mine, xs))
        return xs, [up_t, skip_t, *parts, *[swap_core(p) for p in parts]]

    def cores_sum(keep, give):
        return (keep + swap_core(give)).reshape(8, -1)

    gd, up_part = clip_gradients(
        ids, clip, step_value, seed_value, x_index, in_weight, out_weight, down, up, cores_sum
    )
    down_part = cores_sum(*gd)
    parts = lax.all_to_all(jnp.concatenate([down_part, up_part], axis=1), "dp", 0, 0, tiled=True)
    total = jnp.sum(parts, axis=0)
    down_sum = taps(total[: down_part.shape[1]].reshape(5, -1))
    up_sum = total[down_part.shape[1] :].reshape(10, -1)
    return down_sum[None], taps(up_sum[:, : 3 * CH])[None], up_sum[:, 3 * CH :][None]


def solution(mesh):
    devices = mesh.devices
    grid = Mesh(devices.reshape(devices.shape[0], devices.shape[1], 4, 2), ("dp", "segment", "x", "core"))
    tm = ("x", "core")
    return jax.shard_map(
        local,
        mesh=grid,
        in_specs=(
            P("dp", tm, None, None),
            P("dp"),
            P("dp"),
            P(),
            P(),
            P("segment", None, None, None),
            P("segment", None, None, None),
            P("segment", None, None),
        ),
        out_specs=(
            P("segment", None, ("dp",) + tm, None),
            P("segment", None, ("dp",) + tm, None),
            P("segment", ("dp",) + tm, None),
        ),
        check_vma=False,
    )
```

```python
import functools
import math

import jax
import jax.numpy as jnp
import numpy as np
from jax import lax
from jax.experimental import pallas as pl
from jax.experimental.pallas import tpu as pltpu
from jax.sharding import Mesh
from jax.sharding import PartitionSpec as P

CH = 320
GROUPS = 32
SEGS = 4
TOK = 1024
FRAMES = 16
LANES = 128
TILES = TOK // LANES
ROWS = 32
BF = jnp.bfloat16
F32 = jnp.float32
DOWN_SEL = 80
UP_SEL = 160


def mix_bits(value):
    value = value ^ lax.shift_right_logical(value, jnp.int32(16))
    value = value * -2048144789
    value = value ^ lax.shift_right_logical(value, jnp.int32(13))
    value = value * -1028477387
    value = value ^ lax.shift_right_logical(value, jnp.int32(16))
    return value


def noise_field(seed_value, lat_dim, pix_dim):
    lat_ids = lax.broadcasted_iota(jnp.int32, (lat_dim, pix_dim * FRAMES), 0)
    tokens = lax.broadcasted_iota(jnp.int32, (lat_dim, pix_dim * FRAMES), 1)
    frame_ids = tokens % FRAMES
    pix_ids = tokens // FRAMES
    index = (frame_ids * lat_dim + lat_ids) * pix_dim + pix_ids
    salted = seed_value * -1640531535
    first = mix_bits(index * 2 + salted)
    second = mix_bits(index * 2 + 1 + salted)
    unit_a = (lax.shift_right_logical(first, jnp.int32(8)).astype(F32) + 0.5) / 16777216.0
    unit_b = (lax.shift_right_logical(second, jnp.int32(8)).astype(F32) + 0.5) / 16777216.0
    return jnp.sqrt(-2.0 * jnp.log(unit_a)) * jnp.cos(2.0 * math.pi * unit_b)


def time_embedding(step_value, channels):
    half = channels // 2
    frequency = jnp.exp(-math.log(10000.0) * jnp.arange(half, dtype=F32) / half)
    phase = step_value.astype(F32) * frequency
    return jnp.concatenate([jnp.sin(phase), jnp.cos(phase)])


def group_matrix(size):
    ids = np.arange(CH) // size
    return (ids[:, None] == ids[None, :]).astype(np.float32)


def dot(a, b):
    return jnp.dot(a, b, preferred_element_type=F32)


def dot_nt(a, b):
    return lax.dot_general(a, b, (((1,), (1,)), ((), ())), preferred_element_type=F32)


def tile(j):
    return slice(j * LANES, (j + 1) * LANES)


def row_block(r):
    return pl.ds(pl.multiple_of(r * ROWS, ROWS), ROWS)


def fold(value):
    for step in (16, 32, 64):
        value = value + pltpu.roll(value, step, 1)
    return value


def group_sums(group, values, parts):
    pieces = []
    for value in values:
        rest = value
        for _ in range(parts):
            piece = rest.astype(BF)
            pieces.append(piece)
            rest = rest - piece.astype(F32)
    sums = dot(group, jnp.concatenate(pieces, axis=1))
    out = []
    for i in range(len(values)):
        total = sums[:, tile(i * parts)]
        for q in range(1, parts):
            total = total + sums[:, tile(i * parts + q)]
        out.append(fold(total))
    return out


def gn_stats(x_at, group, size, m_scr, q_scr, mean_at, rstd_at):
    def body(r, carry):
        rows = row_block(r)
        parts = [x_at(rows, tile(j)) for j in range(TILES)]
        total = parts[0]
        for p in parts[1:]:
            total = total + p
        mid = total * (1.0 / TILES)
        square = None
        for p in parts:
            d = p - mid
            square = d * d if square is None else square + d * d
        m_scr[rows, :] = mid
        q_scr[rows, :] = square
        return carry

    lax.fori_loop(0, CH // ROWS, body, 0, unroll=True)
    mid = m_scr[...]
    (mean,) = group_sums(group, [mid], 3)
    mean = mean * (1.0 / (8 * size))
    away = mid - mean
    (spread,) = group_sums(group, [q_scr[...] + (TILES * 1.0) * away * away], 2)
    mean_at[...] = mean
    rstd_at[...] = lax.rsqrt(spread * (1.0 / (64 * size)) + 1e-05)


def shift_matrix():
    lane = np.arange(LANES)
    out = np.zeros((LANES, 2 * LANES), np.float32)
    for l in lane:
        if l % FRAMES != 0:
            out[l - 1, l] = 1.0
        if l % FRAMES != FRAMES - 1:
            out[l + 1, LANES + l] = 1.0
    return out


def neighbours(value, shift):
    both = dot(value, shift).astype(BF)
    return both[:, :LANES], both[:, LANES:]


def silu_parts(y):
    sig = 0.5 * jnp.tanh(0.5 * y) + 0.5
    return sig, y * sig


def norm_bwd(ga_ref, ga_off, x_at, group, size, mean_at, rstd_at, emb_ref, m_scr, q_scr, emit):
    def first(r, carry):
        rows = row_block(r)
        grows = pl.ds(pl.multiple_of(ga_off + r * ROWS, ROWS), ROWS)
        mean = mean_at[rows, :]
        rstd = rstd_at[rows, :]
        emb = None if emb_ref is None else emb_ref[rows, :]
        s1 = None
        s2 = None
        for j in range(TILES):
            xhat = (x_at(rows, tile(j)) - mean) * rstd
            y = xhat if emb is None else xhat + emb
            sig, act = silu_parts(y)
            dy = ga_ref[grows, tile(j)] * (sig + act * (1.0 - sig))
            ga_ref[grows, tile(j)] = dy
            s1 = dy if s1 is None else s1 + dy
            s2 = dy * xhat if s2 is None else s2 + dy * xhat
        m_scr[rows, :] = s1
        q_scr[rows, :] = s2
        return carry

    lax.fori_loop(0, CH // ROWS, first, 0, unroll=True)
    s1, s2 = group_sums(group, [m_scr[...], q_scr[...]], 2)
    scale = 1.0 / (64 * size)
    m_scr[...] = s1 * scale
    q_scr[...] = s2 * scale

    def second(r, carry):
        rows = row_block(r)
        grows = pl.ds(pl.multiple_of(ga_off + r * ROWS, ROWS), ROWS)
        mean = mean_at[rows, :]
        rstd = rstd_at[rows, :]
        m1 = m_scr[rows, :] * rstd
        m2 = q_scr[rows, :] * (rstd * rstd)
        for j in range(TILES):
            away = x_at(rows, tile(j)) - mean
            emit(rows, tile(j), rstd * ga_ref[grows, tile(j)] - m1 - away * m2)
        return carry

    lax.fori_loop(0, CH // ROWS, second, 0, unroll=True)


MAIN = 256
REST = CH - MAIN


def copy_bytes(ref, sem):
    return pltpu.make_async_copy(ref, ref, sem)


def section_of(seg, slot):
    return lax.rem(seg + (1, 3, 2)[slot], SEGS)


def start_section(ids, s, own, pieces):
    away = lax.rem(s + SEGS - ids[0], SEGS)
    pl.when(away == 0)(own)
    for slot, distance in enumerate((1, 3, 2)):

        @pl.when(away == distance)
        def _():
            pieces(slot, ids[1])
            pieces(3 + slot, 1 - ids[1])


def start_down_copies(ids, s, own, parts, dest, sems):
    half = 3 * CH // 2

    def pieces(part, place):
        rows = pl.ds(pl.multiple_of(place * half, 32), half)
        pltpu.make_async_copy(parts[part], dest.at[s, rows, :], sems.at[s]).start()

    start_section(ids, s, lambda: pltpu.make_async_copy(own, dest.at[s], sems.at[s]).start(), pieces)


def start_up_copies(ids, s, own_up, own_skip, parts, dest, sems):
    half = CH // 2

    def mine():
        for k in range(4):
            source = own_up.at[k] if k < 3 else own_skip
            pltpu.make_async_copy(source, dest.at[s, :, k * 640 : (k + 1) * 640], sems.at[s]).start()

    def pieces(part, place):
        rows = pl.ds(pl.multiple_of(place * half, 32), half)
        for k in range(4):
            pltpu.make_async_copy(
                parts[part].at[k], dest.at[s, rows, k * 640 : (k + 1) * 640], sems.at[s]
            ).start()

    start_section(ids, s, mine, pieces)


def pick_matrix(ids, per_device, channels):
    row = lax.broadcasted_iota(jnp.int32, (16 * per_device, channels), 0)
    col = lax.broadcasted_iota(jnp.int32, (16 * per_device, channels), 1)
    block = (row * 205) >> (10 if per_device == 5 else 11)
    place = ids[1] ^ (block >> 3)
    want = ((block & 7) * 8 + 2 * ids[2] + place) * per_device + row - block * per_device
    return (col == want).astype(F32).astype(BF)


def activate(x_at, mean_at, rstd_at, emb_ref, put):
    def act(r, carry):
        rows = row_block(r)
        mu = mean_at[rows, :]
        rs = rstd_at[rows, :] * 0.5
        e = None if emb_ref is None else emb_ref[rows, :] * 0.5
        for j in range(TILES):
            half = (x_at(rows, tile(j)) - mu) * rs
            if e is not None:
                half = half + e
            put(rows, tile(j), (half + half * jnp.tanh(half)).astype(BF))
        return carry

    lax.fori_loop(0, CH // ROWS, act, 0, unroll=True)


def down_forward_kernel(
    ids, noisy, in_weight, emb, g10, g20, shift, own, p0, p1, p2, q0, q1, q2,
    xs_out, mean_out, rstd_out, asel, dstack_out, dmean_out, drstd_out,
    xs, mean, rstd, dstack, dmean, drstd, wnat, wt, stack, m_scr, q_scr, sems, osems,
):
    def send(array, out, index, sem):
        pltpu.make_async_copy(array.at[index], out.at[index], osems.at[sem]).start()

    for s in range(SEGS):
        start_down_copies(ids, s, own, (p0, p1, p2, q0, q1, q2), wnat, sems)
    x0 = lax.dot_general(in_weight[...], noisy[...], (((0,), (0,)), ((), ())), preferred_element_type=F32)
    xs[0] = x0.astype(BF)
    send(xs, xs_out, 0, 0)

    def ahead(s):
        x_at = lambda rows, cols: xs[s + 1, rows, cols].astype(F32)
        gn_stats(x_at, g20[...], 20, m_scr.at[1], q_scr.at[1], dmean.at[s], drstd.at[s])

        def put(rows, cols, a):
            dstack[s, 1, rows, cols] = a

        activate(x_at, dmean.at[s], drstd.at[s], None, put)
        for j in range(TILES):
            before, after = neighbours(dstack[s, 1, :, tile(j)], shift[...])
            dstack[s, 0, :, tile(j)] = before
            dstack[s, 2, :, tile(j)] = after
        dstack[s, 3] = xs[s + 1]

    def send_ahead(s):
        send(dstack, dstack_out, s, 3)
        send(dmean, dmean_out, s, 4)
        send(drstd, drstd_out, s, 5)

    def stage(s, behind):
        x_at = lambda rows, cols: xs[s, rows, cols].astype(F32)
        gn_stats(x_at, g10[...], 10, m_scr.at[0], q_scr.at[0], mean.at[s], rstd.at[s])

        def put(rows, cols, a):
            stack[1, rows, cols] = a

        activate(x_at, mean.at[s], rstd.at[s], emb, put)
        for j in range(TILES):
            before, after = neighbours(stack[1, :, tile(j)], shift[...])
            stack[0, :, tile(j)] = before
            stack[2, :, tile(j)] = after

        @pl.when(s == ids[0])
        def _():
            asel[...] = dot(pick_matrix(ids, 5, CH), stack[1]).astype(BF)

        copy_bytes(wnat.at[s], sems.at[s]).wait()
        for begin in range(0, 3 * CH, LANES):
            size = min(LANES, 3 * CH - begin)
            wt[:, begin : begin + size] = wnat[s, begin : begin + size, :].T
        total = dot(wt[...], stack[...].reshape(3 * CH, TOK)) + xs[s].astype(F32)
        xs[s + 1] = total.astype(BF)
        if behind:
            ahead(s - 1)
            send_ahead(s - 1)
        send(xs, xs_out, s + 1, 0)
        send(mean, mean_out, s, 1)
        send(rstd, rstd_out, s, 2)

    stage(0, False)

    def later_stage(s, carry):
        stage(s, True)
        return carry

    lax.fori_loop(1, SEGS, later_stage, 0)
    ahead(SEGS - 1)
    send_ahead(SEGS - 1)
    for sem, array in enumerate((xs, mean, rstd, dstack, dmean, drstd)):
        copy_bytes(array, osems.at[sem]).wait()


def spread_grad(value, shift, gstack):
    for j in range(TILES):
        g = value(tile(j))
        before, after = neighbours(g, shift)
        for k, part in ((0, after), (1, g), (2, before)):
            gstack[k * MAIN : (k + 1) * MAIN, tile(j)] = part[:MAIN]
            gstack[3 * MAIN + k * REST : 3 * MAIN + (k + 1) * REST, tile(j)] = part[MAIN:]


def up_kernel(
    ids, g20, shift, out_t, out_wide, noise,
    xs_in, dmean_in, drstd_in, dstack, own_up, own_skip, p0, p1, p2, q0, q1, q2,
    gu_keep, gu_give, cgrad, kgrad_out,
    xs, dmean, drstd, kgrad, wt, wb, stack, bsel, jsel, es, emean, erstd, ga, thru, gcur, gstack, m_scr, q_scr,
    sems, dsems, isems, *, scale
):
    top = pltpu.make_async_copy(xs_in.at[SEGS], es.at[SEGS], isems.at[0])
    top.start()

    def fetch(s):
        slot = lax.rem(s, 2)
        for k in range(4):
            pltpu.make_async_copy(dstack.at[s, k], stack.at[slot, k, 1], dsems.at[slot, k]).start()

    fetch(jnp.int32(SEGS - 1))
    for s in reversed(range(SEGS)):
        start_up_copies(ids, s, own_up, own_skip, (p0, p1, p2, q0, q1, q2), wt, sems)
    late = [
        pltpu.make_async_copy(a, b, isems.at[1 + i])
        for i, (a, b) in enumerate(((xs_in, xs), (dmean_in, dmean), (drstd_in, drstd)))
    ]
    for c in late:
        c.start()
    top.wait()

    def forward(i, carry):
        s = SEGS - 1 - i
        slot = lax.rem(s, 2)

        @pl.when(s > 0)
        def _():
            fetch(s - 1)

        x_at = lambda rows, cols: es[s + 1, rows, cols].astype(F32)
        gn_stats(x_at, g20[...], 20, m_scr.at[0], q_scr.at[0], emean.at[s], erstd.at[s])

        def put(rows, cols, a):
            stack[slot, 1, 0, rows, cols] = a

        activate(x_at, emean.at[s], erstd.at[s], None, put)
        for j in range(TILES):
            before, after = neighbours(stack[slot, 1, 0, :, tile(j)], shift[...])
            stack[slot, 0, 0, :, tile(j)] = before
            stack[slot, 2, 0, :, tile(j)] = after
        stack[slot, 3, 0] = es[s + 1]
        for k in range(4):
            pltpu.make_async_copy(dstack.at[s, k], stack.at[slot, k, 1], dsems.at[slot, k]).wait()

        @pl.when(s == ids[0])
        def _():
            pick = pick_matrix(ids, 10, 2 * CH)
            bsel[...] = dot(pick, stack[slot, 1].reshape(2 * CH, TOK)).astype(BF)
            jsel[...] = dot(pick, stack[slot, 3].reshape(2 * CH, TOK)).astype(BF)

        copy_bytes(wt.at[s], sems.at[s]).wait()
        es[s] = dot(wt[s], stack[slot].reshape(8 * CH, TOK)).astype(BF)
        return carry

    lax.fori_loop(0, SEGS, forward, 0)

    for c in late:
        c.wait()
    predicted = dot(out_t[...], es[0])
    thru[0:4, :] = (predicted[:4] - noise[...]) * scale

    def seed(r, carry):
        rows = row_block(r)
        for j in range(TILES):
            total = out_wide[rows, 0:1] * thru[0:1, tile(j)]
            for l in range(1, 4):
                total = total + out_wide[rows, l : l + 1] * thru[l : l + 1, tile(j)]
            gcur[rows, tile(j)] = total.astype(BF)
        return carry

    lax.fori_loop(0, CH // ROWS, seed, 0, unroll=True)

    def backward(s, carry):
        for k in range(3):
            for b in range(2):
                wb[:, k * MAIN + b * LANES : k * MAIN + (b + 1) * LANES] = wt[
                    s, b * LANES : (b + 1) * LANES, k * 640 : (k + 1) * 640
                ].T
        tops = [wt[s, MAIN:, k * 640 : (k + 1) * 640] for k in range(3)]
        wb[:, 3 * MAIN : 3 * MAIN + LANES] = jnp.concatenate(tops[:2], axis=0).T
        wb[:, 3 * MAIN + LANES : 3 * CH] = tops[2].T
        for b in range(2):
            wb[:, 1024 + b * LANES : 1024 + (b + 1) * LANES] = wt[s, b * LANES : (b + 1) * LANES, 1920:].T
        wb[:, 1024 + MAIN : 1024 + CH] = wt[s, MAIN:, 1920:].T
        spread_grad(lambda cols: gcur[:, cols], shift[...], gstack)

        @pl.when(s == ids[0])
        def _():
            for i, gu in enumerate((gu_keep, gu_give)):
                rows = slice(i * (UP_SEL // 2), (i + 1) * (UP_SEL // 2))
                gu[:, : 3 * CH] = dot_nt(bsel[rows, :], gstack[...])
                gu[:, 3 * CH :] = dot_nt(jsel[rows, :], gcur[...])

        ga[...] = dot(wb[:, : 3 * CH], gstack[...])
        thru[...] = dot(wb[:, 1024 : 1024 + CH], gcur[...])

        def emit_e(rows, cols, dx):
            gcur[rows, cols] = (dx + thru[rows, cols]).astype(BF)

        def emit_d(rows, cols, dx):
            trows = pl.ds(pl.multiple_of(rows.start + CH, ROWS), ROWS)
            kgrad[s, rows, cols] = (dx + thru[trows, cols]).astype(BF)

        e_at = lambda rows, cols: es[s + 1, rows, cols].astype(F32)
        d_at = lambda rows, cols: xs[s + 1, rows, cols].astype(F32)
        norm_bwd(ga, 0, e_at, g20[...], 20, emean.at[s], erstd.at[s], None, m_scr.at[0], q_scr.at[0], emit_e)
        norm_bwd(ga, CH, d_at, g20[...], 20, dmean.at[s], drstd.at[s], None, m_scr.at[1], q_scr.at[1], emit_d)
        pltpu.make_async_copy(kgrad.at[s], kgrad_out.at[s], isems.at[4]).start()
        return carry

    lax.fori_loop(0, SEGS, backward, 0)
    cgrad[...] = gcur[...]
    copy_bytes(kgrad, isems.at[4]).wait()


def down_backward_kernel(
    ids, asel, emb, g10, shift, cgrad,
    xs_in, mean_in, rstd_in, kgrad_in, own, p0, p1, p2, q0, q1, q2,
    gd_keep, gd_give,
    xs, mean, rstd, kgrad, wnat, wb, hstack, hcur, ga, ccur, m_scr, q_scr, sems, isems,
):
    arrays = ((kgrad_in, kgrad), (xs_in, xs), (mean_in, mean), (rstd_in, rstd))

    def inputs(s):
        return [pltpu.make_async_copy(a.at[s], b.at[s], isems.at[i, s]) for i, (a, b) in enumerate(arrays)]

    for s in reversed(range(SEGS)):
        inputs(s)[0].start()
        start_down_copies(ids, s, own, (p0, p1, p2, q0, q1, q2), wnat, sems)
        for c in inputs(s)[1:]:
            c.start()
    ccur[...] = cgrad[...]

    def take(s):
        for c in inputs(s):
            c.wait()
        copy_bytes(wnat.at[s], sems.at[s]).wait()

        def value(cols):
            h = (kgrad[s, :, cols].astype(F32) + ccur[:, cols].astype(F32)).astype(BF)
            hcur[:, cols] = h
            return h

        spread_grad(value, shift[...], hstack)

        @pl.when(s == ids[0])
        def _():
            for i, gd in enumerate((gd_keep, gd_give)):
                gd[...] = dot_nt(asel[i * (DOWN_SEL // 2) : (i + 1) * (DOWN_SEL // 2), :], hstack[...])

    def stage(i, carry):
        s = SEGS - 1 - i
        take(s)
        for k in range(3):
            wb[:, k * MAIN : (k + 1) * MAIN] = wnat[s, k * CH : (k + 1) * CH, :MAIN]
            wb[:, 3 * MAIN + k * REST : 3 * MAIN + (k + 1) * REST] = wnat[s, k * CH : (k + 1) * CH, MAIN:]
        ga[...] = dot(wb[...], hstack[...])
        x_at = lambda rows, cols: xs[s, rows, cols].astype(F32)

        def emit(rows, cols, dx):
            ccur[rows, cols] = (hcur[rows, cols].astype(F32) + dx).astype(BF)

        norm_bwd(ga, 0, x_at, g10[...], 10, mean.at[s], rstd.at[s], emb, m_scr, q_scr, emit)
        return carry

    lax.fori_loop(0, SEGS - 1, stage, 0)
    take(0)


VMEM = pl.BlockSpec(memory_space=pltpu.VMEM)
SMEM = pl.BlockSpec(memory_space=pltpu.SMEM)
ANY = pl.BlockSpec(memory_space=pl.ANY)
PARAMS = pltpu.CompilerParams(vmem_limit_bytes=60 * 1024 * 1024)


def shape(dims, dtype=BF):
    return jax.ShapeDtypeStruct(dims, dtype)


def cost(microseconds):
    return pl.CostEstimate(flops=int(microseconds * 1e9), bytes_accessed=0, transcendentals=0)


def run_down_forward(*args):
    return pl.pallas_call(
        down_forward_kernel,
        name="down_forward",
        out_shape=(
            shape((SEGS + 1, CH, TOK)),
            shape((SEGS, CH, LANES), F32),
            shape((SEGS, CH, LANES), F32),
            shape((DOWN_SEL, TOK)),
            shape((SEGS, 4, CH, TOK)),
            shape((SEGS, CH, LANES), F32),
            shape((SEGS, CH, LANES), F32),
        ),
        in_specs=[SMEM] + [VMEM] * 6 + [ANY] * 7,
        out_specs=(ANY,) * 3 + (VMEM,) + (ANY,) * 3,
        scratch_shapes=[
            pltpu.VMEM((SEGS + 1, CH, TOK), BF),
            pltpu.VMEM((SEGS, CH, LANES), F32),
            pltpu.VMEM((SEGS, CH, LANES), F32),
            pltpu.VMEM((SEGS, 4, CH, TOK), BF),
            pltpu.VMEM((SEGS, CH, LANES), F32),
            pltpu.VMEM((SEGS, CH, LANES), F32),
            pltpu.VMEM((SEGS, 3 * CH, CH), BF),
            pltpu.VMEM((CH, 3 * CH), BF),
            pltpu.VMEM((3, CH, TOK), BF),
            pltpu.VMEM((2, CH, LANES), F32),
            pltpu.VMEM((2, CH, LANES), F32),
            pltpu.SemaphoreType.DMA((SEGS,)),
            pltpu.SemaphoreType.DMA((6,)),
        ],
        compiler_params=PARAMS,
        cost_estimate=cost(1),
    )(*args)


def run_up(*args, scale):
    return pl.pallas_call(
        functools.partial(up_kernel, scale=scale),
        name="up_both",
        out_shape=(
            shape((UP_SEL // 2, 4 * CH), F32),
            shape((UP_SEL // 2, 4 * CH), F32),
            shape((CH, TOK)),
            shape((SEGS, CH, TOK)),
        ),
        in_specs=[SMEM] + [VMEM] * 5 + [ANY] * 12,
        out_specs=(VMEM,) * 3 + (ANY,),
        scratch_shapes=[
            pltpu.VMEM((SEGS + 1, CH, TOK), BF),
            pltpu.VMEM((SEGS, CH, LANES), F32),
            pltpu.VMEM((SEGS, CH, LANES), F32),
            pltpu.VMEM((SEGS, CH, TOK), BF),
            pltpu.VMEM((SEGS, CH, 8 * CH), BF),
            pltpu.VMEM((2 * CH, 1024 + 384), BF),
            pltpu.VMEM((2, 4, 2, CH, TOK), BF),
            pltpu.VMEM((UP_SEL, TOK), BF),
            pltpu.VMEM((UP_SEL, TOK), BF),
            pltpu.VMEM((SEGS + 1, CH, TOK), BF),
            pltpu.VMEM((SEGS, CH, LANES), F32),
            pltpu.VMEM((SEGS, CH, LANES), F32),
            pltpu.VMEM((2 * CH, TOK), F32),
            pltpu.VMEM((2 * CH, TOK), F32),
            pltpu.VMEM((CH, TOK), BF),
            pltpu.VMEM((3 * CH, TOK), BF),
            pltpu.VMEM((2, CH, LANES), F32),
            pltpu.VMEM((2, CH, LANES), F32),
            pltpu.SemaphoreType.DMA((SEGS,)),
            pltpu.SemaphoreType.DMA((2, 4)),
            pltpu.SemaphoreType.DMA((5,)),
        ],
        compiler_params=PARAMS,
        cost_estimate=cost(50),
    )(*args)


def run_down_backward(*args):
    return pl.pallas_call(
        down_backward_kernel,
        name="down_backward",
        out_shape=(shape((DOWN_SEL // 2, 3 * CH), F32),) * 2,
        in_specs=[SMEM] + [VMEM] * 5 + [ANY] * 11,
        out_specs=(VMEM,) * 2,
        scratch_shapes=[
            pltpu.VMEM((SEGS, CH, TOK), BF),
            pltpu.VMEM((SEGS, CH, LANES), F32),
            pltpu.VMEM((SEGS, CH, LANES), F32),
            pltpu.VMEM((SEGS, CH, TOK), BF),
            pltpu.VMEM((SEGS, 3 * CH, CH), BF),
            pltpu.VMEM((CH, 3 * CH), BF),
            pltpu.VMEM((3 * CH, TOK), BF),
            pltpu.VMEM((CH, TOK), BF),
            pltpu.VMEM((CH, TOK), F32),
            pltpu.VMEM((CH, TOK), BF),
            pltpu.VMEM((CH, LANES), F32),
            pltpu.VMEM((CH, LANES), F32),
            pltpu.SemaphoreType.DMA((SEGS,)),
            pltpu.SemaphoreType.DMA((4, SEGS)),
        ],
        compiler_params=PARAMS,
        cost_estimate=cost(15),
    )(*args)


def clip_inputs(clip, step_value, seed_value, out_weight):
    lat_dim, pix_dim, frames = clip.shape
    noise = noise_field(seed_value, lat_dim, pix_dim)
    theta = step_value.astype(F32) * (0.5 * math.pi / 1000.0)
    noisy = (
        jnp.cos(theta) * clip.reshape(lat_dim, pix_dim * frames).astype(F32) + jnp.sin(theta) * noise
    ).astype(BF)
    out_t = jnp.pad(out_weight.T, ((0, 16 - lat_dim), (0, 0)))
    emb = jnp.broadcast_to(time_embedding(step_value, CH)[:, None], (CH, LANES))
    return noise, noisy, out_t, emb


def swap_core(value):
    return lax.ppermute(value, "core", [(0, 1), (1, 0)])


def from_segment(value, away):
    return lax.ppermute(value, "segment", [((i + away) % SEGS, i) for i in range(SEGS)])


def fetch_sections(half):
    return [from_segment(half, away) for away in (1, 3, 2)]


def taps(value):
    return jnp.stack(
        [
            jnp.concatenate(
                [
                    value[:, k * MAIN : (k + 1) * MAIN],
                    value[:, 3 * MAIN + k * REST : 3 * MAIN + (k + 1) * REST],
                ],
                axis=1,
            )
            for k in range(3)
        ]
    )


def clip_gradients(ids, clip, step_value, seed_value, in_weight, out_weight, down, up, reduce_up):
    noise, noisy, out_t, emb = clip_inputs(clip, step_value, seed_value, out_weight)
    g10 = jnp.asarray(group_matrix(10), BF)
    g20 = jnp.asarray(group_matrix(20), BF)
    shift = jnp.asarray(shift_matrix(), BF)
    weights = down()
    xs, mean, rstd, asel, dstack, dmean, drstd = run_down_forward(
        ids, noisy, in_weight, emb, g10, g20, shift, *weights
    )
    xs, up_args = up(xs)
    gu_keep, gu_give, cgrad, kgrad = run_up(
        ids, g20, shift, out_t, out_weight.astype(F32), noise, xs, dmean, drstd, dstack, *up_args,
        scale=64.0 / math.sqrt(16 * FRAMES * 4 * 64),
    )
    up_part = reduce_up(gu_keep, gu_give)
    gd = run_down_backward(ids, asel, emb, g10, shift, cgrad, xs, mean, rstd, kgrad, *weights)
    return gd, up_part


def clip_parts(latents, core):
    own = jnp.where(core == 0, latents[0], latents[1])
    got = swap_core(jnp.where(core == 0, latents[1], latents[0]))
    half = lax.broadcasted_iota(jnp.int32, (2,) + own.shape, 0)
    quad = jnp.where(half == core, own[None], got[None])
    return [quad] + [lax.ppermute(quad, "x", [((i + away) % 4, i) for i in range(4)]) for away in (1, 2, 3)]


def whole_clip(quads, x_index):
    quad = quads[0]
    away = (lax.broadcasted_iota(jnp.int32, (4,) + quad.shape, 0) - x_index) & 3
    whole = quads[3][None]
    for i in (2, 1, 0):
        whole = jnp.where(away == i, quads[i][None], whole)
    return whole.reshape((FRAMES,) + quad.shape[2:])


def local(latents, timesteps, seeds, in_weight, out_weight, down_weight, up_weight, skip_weight):
    seg = lax.axis_index("segment")
    core = lax.axis_index("core")
    x_index = lax.axis_index("x")
    ids = jnp.stack([seg, core, x_index]).astype(jnp.int32)
    down_nat = down_weight[0].reshape(3 * CH, CH)
    up_t = jnp.transpose(up_weight[0], (0, 2, 1))
    skip_t = skip_weight[0].T
    d_half = lax.dynamic_slice_in_dim(down_nat, core * (3 * CH // 2), 3 * CH // 2, 0)
    u_half = jnp.concatenate(
        [
            lax.dynamic_slice_in_dim(up_t, core * (CH // 2), CH // 2, 1),
            lax.dynamic_slice_in_dim(skip_t, core * (CH // 2), CH // 2, 0)[None],
        ],
        axis=0,
    )
    d_mine = fetch_sections(d_half)
    quads = clip_parts(latents, core)
    *moved, u_half = lax.optimization_barrier((*d_mine, *quads, u_half))
    d_mine, quads = moved[:3], moved[3:]
    u_mine = fetch_sections(u_half)

    clip = jnp.transpose(whole_clip(quads, x_index), (1, 2, 0))
    step_value = jnp.where(core == 0, timesteps[0], timesteps[1])
    seed_value = jnp.where(core == 0, seeds[0], seeds[1])

    def down():
        return [down_nat, *d_mine, *[swap_core(p) for p in d_mine]]

    def up(xs):
        *parts, xs = lax.optimization_barrier((*u_mine, xs))
        return xs, [up_t, skip_t, *parts, *[swap_core(p) for p in parts]]

    def cores_sum(keep, give):
        return (keep + swap_core(give)).reshape(8, -1)

    gd, up_part = clip_gradients(
        ids, clip, step_value, seed_value, in_weight, out_weight, down, up, cores_sum
    )
    down_part = cores_sum(*gd)
    parts = lax.all_to_all(jnp.concatenate([down_part, up_part], axis=1), "dp", 0, 0, tiled=True)
    total = jnp.sum(parts, axis=0)
    down_sum = taps(total[: down_part.shape[1]].reshape(5, -1))
    up_sum = total[down_part.shape[1] :].reshape(10, -1)
    return down_sum[None], taps(up_sum[:, : 3 * CH])[None], up_sum[:, 3 * CH :][None]


def solution(mesh):
    devices = mesh.devices
    grid = Mesh(devices.reshape(devices.shape[0], devices.shape[1], 4, 2), ("dp", "segment", "x", "core"))
    tm = ("x", "core")
    return jax.shard_map(
        local,
        mesh=grid,
        in_specs=(
            P("dp", tm, None, None),
            P("dp"),
            P("dp"),
            P(),
            P(),
            P("segment", None, None, None),
            P("segment", None, None, None),
            P("segment", None, None),
        ),
        out_specs=(
            P("segment", None, ("dp",) + tm, None),
            P("segment", None, ("dp",) + tm, None),
            P("segment", ("dp",) + tm, None),
        ),
        check_vma=False,
    )
```

```python
import functools
import math

import jax
import jax.numpy as jnp
import numpy as np
from jax import lax
from jax.experimental import pallas as pl
from jax.experimental.pallas import tpu as pltpu
from jax.sharding import Mesh
from jax.sharding import PartitionSpec as P

CH = 320
GROUPS = 32
SEGS = 4
TOK = 1024
FRAMES = 16
LANES = 128
TILES = TOK // LANES
ROWS = 32
BF = jnp.bfloat16
F32 = jnp.float32
DOWN_SEL = 80
UP_SEL = 160


def mix_bits(value):
    value = value ^ lax.shift_right_logical(value, jnp.int32(16))
    value = value * -2048144789
    value = value ^ lax.shift_right_logical(value, jnp.int32(13))
    value = value * -1028477387
    value = value ^ lax.shift_right_logical(value, jnp.int32(16))
    return value


def noise_field(seed_value, lat_dim, pix_dim):
    lat_ids = lax.broadcasted_iota(jnp.int32, (lat_dim, pix_dim * FRAMES), 0)
    tokens = lax.broadcasted_iota(jnp.int32, (lat_dim, pix_dim * FRAMES), 1)
    frame_ids = tokens % FRAMES
    pix_ids = tokens // FRAMES
    index = (frame_ids * lat_dim + lat_ids) * pix_dim + pix_ids
    salted = seed_value * -1640531535
    first = mix_bits(index * 2 + salted)
    second = mix_bits(index * 2 + 1 + salted)
    unit_a = (lax.shift_right_logical(first, jnp.int32(8)).astype(F32) + 0.5) / 16777216.0
    unit_b = (lax.shift_right_logical(second, jnp.int32(8)).astype(F32) + 0.5) / 16777216.0
    return jnp.sqrt(-2.0 * jnp.log(unit_a)) * jnp.cos(2.0 * math.pi * unit_b)


def time_embedding(step_value, channels):
    half = channels // 2
    frequency = jnp.exp(-math.log(10000.0) * jnp.arange(half, dtype=F32) / half)
    phase = step_value.astype(F32) * frequency
    return jnp.concatenate([jnp.sin(phase), jnp.cos(phase)])


def group_matrix(size):
    ids = np.arange(CH) // size
    return (ids[:, None] == ids[None, :]).astype(np.float32)


def dot(a, b):
    return jnp.dot(a, b, preferred_element_type=F32)


def dot_nt(a, b):
    return lax.dot_general(a, b, (((1,), (1,)), ((), ())), preferred_element_type=F32)


def tile(j):
    return slice(j * LANES, (j + 1) * LANES)


def row_block(r):
    return pl.ds(pl.multiple_of(r * ROWS, ROWS), ROWS)


def fold(value):
    for step in (16, 32, 64):
        value = value + pltpu.roll(value, step, 1)
    return value


def group_sums(group, values, parts):
    pieces = []
    for value in values:
        rest = value
        for _ in range(parts):
            piece = rest.astype(BF)
            pieces.append(piece)
            rest = rest - piece.astype(F32)
    sums = dot(group, jnp.concatenate(pieces, axis=1))
    out = []
    for i in range(len(values)):
        total = sums[:, tile(i * parts)]
        for q in range(1, parts):
            total = total + sums[:, tile(i * parts + q)]
        out.append(fold(total))
    return out


def gn_stats(x_at, group, size, m_scr, q_scr, mean_at, rstd_at):
    def body(r, carry):
        rows = row_block(r)
        parts = [x_at(rows, tile(j)) for j in range(TILES)]
        total = parts[0]
        for p in parts[1:]:
            total = total + p
        mid = total * (1.0 / TILES)
        square = None
        for p in parts:
            d = p - mid
            square = d * d if square is None else square + d * d
        m_scr[rows, :] = mid
        q_scr[rows, :] = square
        return carry

    lax.fori_loop(0, CH // ROWS, body, 0, unroll=True)
    mid = m_scr[...]
    (mean,) = group_sums(group, [mid], 3)
    mean = mean * (1.0 / (8 * size))
    away = mid - mean
    (spread,) = group_sums(group, [q_scr[...] + (TILES * 1.0) * away * away], 2)
    mean_at[...] = mean
    rstd_at[...] = lax.rsqrt(spread * (1.0 / (64 * size)) + 1e-05)


def shift_matrix():
    lane = np.arange(LANES)
    out = np.zeros((LANES, 2 * LANES), np.float32)
    for l in lane:
        if l % FRAMES != 0:
            out[l - 1, l] = 1.0
        if l % FRAMES != FRAMES - 1:
            out[l + 1, LANES + l] = 1.0
    return out


def neighbours(value, shift):
    both = dot(value, shift).astype(BF)
    return both[:, :LANES], both[:, LANES:]


def silu_parts(y):
    sig = 0.5 * jnp.tanh(0.5 * y) + 0.5
    return sig, y * sig


def norm_bwd(ga_ref, ga_off, x_at, group, size, mean_at, rstd_at, emb_ref, m_scr, q_scr, emit):
    def first(r, carry):
        rows = row_block(r)
        grows = pl.ds(pl.multiple_of(ga_off + r * ROWS, ROWS), ROWS)
        mean = mean_at[rows, :]
        rstd = rstd_at[rows, :]
        emb = None if emb_ref is None else emb_ref[rows, :]
        s1 = None
        s2 = None
        for j in range(TILES):
            xhat = (x_at(rows, tile(j)) - mean) * rstd
            y = xhat if emb is None else xhat + emb
            sig, act = silu_parts(y)
            dy = ga_ref[grows, tile(j)] * (sig + act * (1.0 - sig))
            ga_ref[grows, tile(j)] = dy
            s1 = dy if s1 is None else s1 + dy
            s2 = dy * xhat if s2 is None else s2 + dy * xhat
        m_scr[rows, :] = s1
        q_scr[rows, :] = s2
        return carry

    lax.fori_loop(0, CH // ROWS, first, 0, unroll=True)
    s1, s2 = group_sums(group, [m_scr[...], q_scr[...]], 2)
    scale = 1.0 / (64 * size)
    m_scr[...] = s1 * scale
    q_scr[...] = s2 * scale

    def second(r, carry):
        rows = row_block(r)
        grows = pl.ds(pl.multiple_of(ga_off + r * ROWS, ROWS), ROWS)
        mean = mean_at[rows, :]
        rstd = rstd_at[rows, :]
        m1 = m_scr[rows, :] * rstd
        m2 = q_scr[rows, :] * (rstd * rstd)
        for j in range(TILES):
            away = x_at(rows, tile(j)) - mean
            emit(rows, tile(j), rstd * ga_ref[grows, tile(j)] - m1 - away * m2)
        return carry

    lax.fori_loop(0, CH // ROWS, second, 0, unroll=True)


MAIN = 256
REST = CH - MAIN


def copy_bytes(ref, sem):
    return pltpu.make_async_copy(ref, ref, sem)


def section_of(seg, slot):
    return lax.rem(seg + (1, 3, 2)[slot], SEGS)


def start_down_copies(ids, own, parts, dest, sems):
    half = 3 * CH // 2
    pltpu.make_async_copy(own, dest.at[ids[0]], sems.at[ids[0]]).start()
    for slot in range(3):
        s = section_of(ids[0], slot)
        for source, place in ((parts[slot], ids[1]), (parts[3 + slot], 1 - ids[1])):
            rows = pl.ds(pl.multiple_of(place * half, 32), half)
            pltpu.make_async_copy(source, dest.at[s, rows, :], sems.at[s]).start()


def start_up_copies(ids, own_up, own_skip, parts, dest, sems):
    half = CH // 2
    seg = ids[0]
    for k in range(4):
        source = own_up.at[k] if k < 3 else own_skip
        pltpu.make_async_copy(source, dest.at[seg, :, k * 640 : (k + 1) * 640], sems.at[seg]).start()
    for slot in range(3):
        s = section_of(seg, slot)
        for source, place in ((parts[slot], ids[1]), (parts[3 + slot], 1 - ids[1])):
            rows = pl.ds(pl.multiple_of(place * half, 32), half)
            for k in range(4):
                pltpu.make_async_copy(
                    source.at[k], dest.at[s, rows, k * 640 : (k + 1) * 640], sems.at[s]
                ).start()


def pick_matrix(ids, per_device, channels):
    row = lax.broadcasted_iota(jnp.int32, (16 * per_device, channels), 0)
    col = lax.broadcasted_iota(jnp.int32, (16 * per_device, channels), 1)
    block = (row * 205) >> (10 if per_device == 5 else 11)
    place = ids[1] ^ (block >> 3)
    want = ((block & 7) * 8 + 2 * ids[2] + place) * per_device + row - block * per_device
    return (col == want).astype(F32).astype(BF)


def activate(x_at, mean_at, rstd_at, emb_ref, put):
    def act(r, carry):
        rows = row_block(r)
        mu = mean_at[rows, :]
        rs = rstd_at[rows, :] * 0.5
        e = None if emb_ref is None else emb_ref[rows, :] * 0.5
        for j in range(TILES):
            half = (x_at(rows, tile(j)) - mu) * rs
            if e is not None:
                half = half + e
            put(rows, tile(j), (half + half * jnp.tanh(half)).astype(BF))
        return carry

    lax.fori_loop(0, CH // ROWS, act, 0, unroll=True)


def down_forward_kernel(
    ids, noisy, in_weight, emb, g10, g20, shift, own, p0, p1, p2, q0, q1, q2,
    xs, mean, rstd, asel, wnat, dstack, dmean, drstd,
    wt, stack, m_scr, q_scr, sems,
):
    start_down_copies(ids, own, (p0, p1, p2, q0, q1, q2), wnat, sems)
    x0 = lax.dot_general(in_weight[...], noisy[...], (((0,), (0,)), ((), ())), preferred_element_type=F32)
    xs[0] = x0.astype(BF)

    def stage(s, carry):
        x_at = lambda rows, cols: xs[s, rows, cols].astype(F32)
        gn_stats(x_at, g10[...], 10, m_scr, q_scr, mean.at[s], rstd.at[s])

        def put(rows, cols, a):
            stack[1, rows, cols] = a

        activate(x_at, mean.at[s], rstd.at[s], emb, put)
        for j in range(TILES):
            before, after = neighbours(stack[1, :, tile(j)], shift[...])
            stack[0, :, tile(j)] = before
            stack[2, :, tile(j)] = after

        @pl.when(s == ids[0])
        def _():
            asel[...] = dot(pick_matrix(ids, 5, CH), stack[1]).astype(BF)

        copy_bytes(wnat.at[s], sems.at[s]).wait()
        for begin in range(0, 3 * CH, LANES):
            size = min(LANES, 3 * CH - begin)
            wt[:, begin : begin + size] = wnat[s, begin : begin + size, :].T
        total = dot(wt[...], stack[...].reshape(3 * CH, TOK)) + xs[s].astype(F32)
        xs[s + 1] = total.astype(BF)
        return carry

    lax.fori_loop(0, SEGS, stage, 0)

    def ahead(s, carry):
        x_at = lambda rows, cols: xs[s + 1, rows, cols].astype(F32)
        gn_stats(x_at, g20[...], 20, m_scr, q_scr, dmean.at[s], drstd.at[s])

        def put(rows, cols, a):
            dstack[s, 1, rows, cols] = a

        activate(x_at, dmean.at[s], drstd.at[s], None, put)
        for j in range(TILES):
            before, after = neighbours(dstack[s, 1, :, tile(j)], shift[...])
            dstack[s, 0, :, tile(j)] = before
            dstack[s, 2, :, tile(j)] = after
        dstack[s, 3] = xs[s + 1]
        return carry

    lax.fori_loop(0, SEGS, ahead, 0)


def spread_grad(value, shift, gstack):
    for j in range(TILES):
        g = value(tile(j))
        before, after = neighbours(g, shift)
        for k, part in ((0, after), (1, g), (2, before)):
            gstack[k * MAIN : (k + 1) * MAIN, tile(j)] = part[:MAIN]
            gstack[3 * MAIN + k * REST : 3 * MAIN + (k + 1) * REST, tile(j)] = part[MAIN:]


def up_kernel(
    ids, xs, dmean, drstd, g20, shift, out_t, out_wide, noise,
    dstack, own_up, own_skip, p0, p1, p2, q0, q1, q2,
    gu_keep, gu_give, kgrad, cgrad,
    wt, wb, stack, bsel, jsel, es, emean, erstd, ga, thru, gcur, gstack, m_scr, q_scr, sems, dsems, *, scale
):
    start_up_copies(ids, own_up, own_skip, (p0, p1, p2, q0, q1, q2), wt, sems)

    def fetch(s):
        slot = lax.rem(s, 2)
        for k in range(4):
            pltpu.make_async_copy(dstack.at[s, k], stack.at[slot, k, 1], dsems.at[slot, k]).start()

    fetch(jnp.int32(SEGS - 1))
    es[SEGS] = xs[SEGS]

    def forward(i, carry):
        s = SEGS - 1 - i
        slot = lax.rem(s, 2)

        @pl.when(s > 0)
        def _():
            fetch(s - 1)

        x_at = lambda rows, cols: es[s + 1, rows, cols].astype(F32)
        gn_stats(x_at, g20[...], 20, m_scr.at[0], q_scr.at[0], emean.at[s], erstd.at[s])

        def put(rows, cols, a):
            stack[slot, 1, 0, rows, cols] = a

        activate(x_at, emean.at[s], erstd.at[s], None, put)
        for j in range(TILES):
            before, after = neighbours(stack[slot, 1, 0, :, tile(j)], shift[...])
            stack[slot, 0, 0, :, tile(j)] = before
            stack[slot, 2, 0, :, tile(j)] = after
        stack[slot, 3, 0] = es[s + 1]
        for k in range(4):
            pltpu.make_async_copy(dstack.at[s, k], stack.at[slot, k, 1], dsems.at[slot, k]).wait()

        @pl.when(s == ids[0])
        def _():
            pick = pick_matrix(ids, 10, 2 * CH)
            bsel[...] = dot(pick, stack[slot, 1].reshape(2 * CH, TOK)).astype(BF)
            jsel[...] = dot(pick, stack[slot, 3].reshape(2 * CH, TOK)).astype(BF)

        copy_bytes(wt.at[s], sems.at[s]).wait()
        es[s] = dot(wt[s], stack[slot].reshape(8 * CH, TOK)).astype(BF)
        return carry

    lax.fori_loop(0, SEGS, forward, 0)

    predicted = dot(out_t[...], es[0])
    thru[0:4, :] = (predicted[:4] - noise[...]) * scale

    def seed(r, carry):
        rows = row_block(r)
        for j in range(TILES):
            total = out_wide[rows, 0:1] * thru[0:1, tile(j)]
            for l in range(1, 4):
                total = total + out_wide[rows, l : l + 1] * thru[l : l + 1, tile(j)]
            gcur[rows, tile(j)] = total.astype(BF)
        return carry

    lax.fori_loop(0, CH // ROWS, seed, 0, unroll=True)

    def backward(s, carry):
        for k in range(3):
            for b in range(2):
                wb[:, k * MAIN + b * LANES : k * MAIN + (b + 1) * LANES] = wt[
                    s, b * LANES : (b + 1) * LANES, k * 640 : (k + 1) * 640
                ].T
        tops = [wt[s, MAIN:, k * 640 : (k + 1) * 640] for k in range(3)]
        wb[:, 3 * MAIN : 3 * MAIN + LANES] = jnp.concatenate(tops[:2], axis=0).T
        wb[:, 3 * MAIN + LANES : 3 * CH] = tops[2].T
        for b in range(2):
            wb[:, 1024 + b * LANES : 1024 + (b + 1) * LANES] = wt[s, b * LANES : (b + 1) * LANES, 1920:].T
        wb[:, 1024 + MAIN : 1024 + CH] = wt[s, MAIN:, 1920:].T
        spread_grad(lambda cols: gcur[:, cols], shift[...], gstack)

        @pl.when(s == ids[0])
        def _():
            for i, gu in enumerate((gu_keep, gu_give)):
                rows = slice(i * (UP_SEL // 2), (i + 1) * (UP_SEL // 2))
                gu[:, : 3 * CH] = dot_nt(bsel[rows, :], gstack[...])
                gu[:, 3 * CH :] = dot_nt(jsel[rows, :], gcur[...])

        ga[...] = dot(wb[:, : 3 * CH], gstack[...])
        thru[...] = dot(wb[:, 1024 : 1024 + CH], gcur[...])

        def emit_e(rows, cols, dx):
            gcur[rows, cols] = (dx + thru[rows, cols]).astype(BF)

        def emit_d(rows, cols, dx):
            trows = pl.ds(pl.multiple_of(rows.start + CH, ROWS), ROWS)
            kgrad[s, rows, cols] = (dx + thru[trows, cols]).astype(BF)

        e_at = lambda rows, cols: es[s + 1, rows, cols].astype(F32)
        d_at = lambda rows, cols: xs[s + 1, rows, cols].astype(F32)
        norm_bwd(ga, 0, e_at, g20[...], 20, emean.at[s], erstd.at[s], None, m_scr.at[0], q_scr.at[0], emit_e)
        norm_bwd(ga, CH, d_at, g20[...], 20, dmean.at[s], drstd.at[s], None, m_scr.at[1], q_scr.at[1], emit_d)
        return carry

    lax.fori_loop(0, SEGS, backward, 0)
    cgrad[...] = gcur[...]


def down_backward_kernel(
    ids, xs, mean, rstd, asel, wnat, emb, g10, shift, kgrad, cgrad,
    gd_keep, gd_give,
    wb, hstack, hcur, ga, ccur, m_scr, q_scr,
):
    ccur[...] = cgrad[...]

    def take(s):
        def value(cols):
            h = (kgrad[s, :, cols].astype(F32) + ccur[:, cols].astype(F32)).astype(BF)
            hcur[:, cols] = h
            return h

        spread_grad(value, shift[...], hstack)

        @pl.when(s == ids[0])
        def _():
            for i, gd in enumerate((gd_keep, gd_give)):
                gd[...] = dot_nt(asel[i * (DOWN_SEL // 2) : (i + 1) * (DOWN_SEL // 2), :], hstack[...])

    def stage(i, carry):
        s = SEGS - 1 - i
        take(s)
        for k in range(3):
            wb[:, k * MAIN : (k + 1) * MAIN] = wnat[s, k * CH : (k + 1) * CH, :MAIN]
            wb[:, 3 * MAIN + k * REST : 3 * MAIN + (k + 1) * REST] = wnat[s, k * CH : (k + 1) * CH, MAIN:]
        ga[...] = dot(wb[...], hstack[...])
        x_at = lambda rows, cols: xs[s, rows, cols].astype(F32)

        def emit(rows, cols, dx):
            ccur[rows, cols] = (hcur[rows, cols].astype(F32) + dx).astype(BF)

        norm_bwd(ga, 0, x_at, g10[...], 10, mean.at[s], rstd.at[s], emb, m_scr, q_scr, emit)
        return carry

    lax.fori_loop(0, SEGS - 1, stage, 0)
    take(0)


VMEM = pl.BlockSpec(memory_space=pltpu.VMEM)
SMEM = pl.BlockSpec(memory_space=pltpu.SMEM)
ANY = pl.BlockSpec(memory_space=pl.ANY)
PARAMS = pltpu.CompilerParams(vmem_limit_bytes=60 * 1024 * 1024)


def shape(dims, dtype=BF):
    return jax.ShapeDtypeStruct(dims, dtype)


def cost(microseconds):
    return pl.CostEstimate(flops=int(microseconds * 1e9), bytes_accessed=0, transcendentals=0)


def run_down_forward(*args):
    return pl.pallas_call(
        down_forward_kernel,
        name="down_forward",
        out_shape=(
            shape((SEGS + 1, CH, TOK)),
            shape((SEGS, CH, LANES), F32),
            shape((SEGS, CH, LANES), F32),
            shape((DOWN_SEL, TOK)),
            shape((SEGS, 3 * CH, CH)),
            shape((SEGS, 4, CH, TOK)),
            shape((SEGS, CH, LANES), F32),
            shape((SEGS, CH, LANES), F32),
        ),
        in_specs=[SMEM] + [VMEM] * 6 + [ANY] * 7,
        out_specs=(VMEM,) * 8,
        scratch_shapes=[
            pltpu.VMEM((CH, 3 * CH), BF),
            pltpu.VMEM((3, CH, TOK), BF),
            pltpu.VMEM((CH, LANES), F32),
            pltpu.VMEM((CH, LANES), F32),
            pltpu.SemaphoreType.DMA((SEGS,)),
        ],
        compiler_params=PARAMS,
        cost_estimate=cost(1),
    )(*args)


def run_up(*args, scale):
    return pl.pallas_call(
        functools.partial(up_kernel, scale=scale),
        name="up_both",
        out_shape=(
            shape((UP_SEL // 2, 4 * CH), F32),
            shape((UP_SEL // 2, 4 * CH), F32),
            shape((SEGS, CH, TOK)),
            shape((CH, TOK)),
        ),
        in_specs=[SMEM] + [VMEM] * 8 + [ANY] * 9,
        out_specs=(VMEM,) * 4,
        scratch_shapes=[
            pltpu.VMEM((SEGS, CH, 8 * CH), BF),
            pltpu.VMEM((2 * CH, 1024 + 384), BF),
            pltpu.VMEM((2, 4, 2, CH, TOK), BF),
            pltpu.VMEM((UP_SEL, TOK), BF),
            pltpu.VMEM((UP_SEL, TOK), BF),
            pltpu.VMEM((SEGS + 1, CH, TOK), BF),
            pltpu.VMEM((SEGS, CH, LANES), F32),
            pltpu.VMEM((SEGS, CH, LANES), F32),
            pltpu.VMEM((2 * CH, TOK), F32),
            pltpu.VMEM((2 * CH, TOK), F32),
            pltpu.VMEM((CH, TOK), BF),
            pltpu.VMEM((3 * CH, TOK), BF),
            pltpu.VMEM((2, CH, LANES), F32),
            pltpu.VMEM((2, CH, LANES), F32),
            pltpu.SemaphoreType.DMA((SEGS,)),
            pltpu.SemaphoreType.DMA((2, 4)),
        ],
        compiler_params=PARAMS,
        cost_estimate=cost(50),
    )(*args)


def run_down_backward(*args):
    return pl.pallas_call(
        down_backward_kernel,
        name="down_backward",
        out_shape=(shape((DOWN_SEL // 2, 3 * CH), F32),) * 2,
        in_specs=[SMEM] + [VMEM] * 10,
        out_specs=(VMEM,) * 2,
        scratch_shapes=[
            pltpu.VMEM((CH, 3 * CH), BF),
            pltpu.VMEM((3 * CH, TOK), BF),
            pltpu.VMEM((CH, TOK), BF),
            pltpu.VMEM((CH, TOK), F32),
            pltpu.VMEM((CH, TOK), BF),
            pltpu.VMEM((CH, LANES), F32),
            pltpu.VMEM((CH, LANES), F32),
        ],
        compiler_params=PARAMS,
        cost_estimate=cost(15),
    )(*args)


def clip_inputs(clip, step_value, seed_value, out_weight):
    lat_dim, pix_dim, frames = clip.shape
    noise = noise_field(seed_value, lat_dim, pix_dim)
    theta = step_value.astype(F32) * (0.5 * math.pi / 1000.0)
    noisy = (
        jnp.cos(theta) * clip.reshape(lat_dim, pix_dim * frames).astype(F32) + jnp.sin(theta) * noise
    ).astype(BF)
    out_t = jnp.pad(out_weight.T, ((0, 16 - lat_dim), (0, 0)))
    emb = jnp.broadcast_to(time_embedding(step_value, CH)[:, None], (CH, LANES))
    return noise, noisy, out_t, emb


def swap_core(value):
    return lax.ppermute(value, "core", [(0, 1), (1, 0)])


def from_segment(value, away):
    return lax.ppermute(value, "segment", [((i + away) % SEGS, i) for i in range(SEGS)])


def fetch_sections(half):
    return [from_segment(half, away) for away in (1, 3, 2)]


def cores_sum(keep, give):
    return (keep + swap_core(give)).reshape(8, -1)


def taps(value):
    return jnp.stack(
        [
            jnp.concatenate(
                [
                    value[:, k * MAIN : (k + 1) * MAIN],
                    value[:, 3 * MAIN + k * REST : 3 * MAIN + (k + 1) * REST],
                ],
                axis=1,
            )
            for k in range(3)
        ]
    )


def clip_gradients(ids, clip, step_value, seed_value, in_weight, out_weight, down, up, reduce_up):
    noise, noisy, out_t, emb = clip_inputs(clip, step_value, seed_value, out_weight)
    g10 = jnp.asarray(group_matrix(10), BF)
    g20 = jnp.asarray(group_matrix(20), BF)
    shift = jnp.asarray(shift_matrix(), BF)
    xs, mean, rstd, asel, wnat, dstack, dmean, drstd = run_down_forward(
        ids, noisy, in_weight, emb, g10, g20, shift, *down()
    )
    xs, up_args = up(xs)
    gu_keep, gu_give, kgrad, cgrad = run_up(
        ids, xs, dmean, drstd, g20, shift, out_t, out_weight.astype(F32), noise, dstack, *up_args,
        scale=64.0 / math.sqrt(16 * FRAMES * 4 * 64),
    )
    up_part = reduce_up(gu_keep, gu_give)
    gd = run_down_backward(ids, xs, mean, rstd, asel, wnat, emb, g10, shift, kgrad, cgrad)
    return gd, up_part


def clip_parts(latents, core):
    own = jnp.where(core == 0, latents[0], latents[1])
    got = swap_core(jnp.where(core == 0, latents[1], latents[0]))
    half = lax.broadcasted_iota(jnp.int32, (2,) + own.shape, 0)
    quad = jnp.where(half == core, own[None], got[None])
    return [quad] + [lax.ppermute(quad, "x", [((i + away) % 4, i) for i in range(4)]) for away in (1, 2, 3)]


def whole_clip(quads, x_index):
    quad = quads[0]
    away = (lax.broadcasted_iota(jnp.int32, (4,) + quad.shape, 0) - x_index) & 3
    whole = quads[3][None]
    for i in (2, 1, 0):
        whole = jnp.where(away == i, quads[i][None], whole)
    return whole.reshape((FRAMES,) + quad.shape[2:])


def local(latents, timesteps, seeds, in_weight, out_weight, down_weight, up_weight, skip_weight):
    seg = lax.axis_index("segment")
    core = lax.axis_index("core")
    x_index = lax.axis_index("x")
    ids = jnp.stack([seg, core, x_index]).astype(jnp.int32)
    down_nat = down_weight[0].reshape(3 * CH, CH)
    up_t = jnp.transpose(up_weight[0], (0, 2, 1))
    skip_t = skip_weight[0].T
    d_half = lax.dynamic_slice_in_dim(down_nat, core * (3 * CH // 2), 3 * CH // 2, 0)
    u_half = jnp.concatenate(
        [
            lax.dynamic_slice_in_dim(up_t, core * (CH // 2), CH // 2, 1),
            lax.dynamic_slice_in_dim(skip_t, core * (CH // 2), CH // 2, 0)[None],
        ],
        axis=0,
    )
    d_mine = fetch_sections(d_half)
    quads = clip_parts(latents, core)
    *moved, u_half = lax.optimization_barrier((*d_mine, *quads, u_half))
    d_mine, quads = moved[:3], moved[3:]
    u_mine = fetch_sections(u_half)

    clip = jnp.transpose(whole_clip(quads, x_index), (1, 2, 0))
    step_value = jnp.where(core == 0, timesteps[0], timesteps[1])
    seed_value = jnp.where(core == 0, seeds[0], seeds[1])

    def down():
        return [down_nat, *d_mine, *[swap_core(p) for p in d_mine]]

    def up(xs):
        *parts, xs = lax.optimization_barrier((*u_mine, xs))
        return xs, [up_t, skip_t, *parts, *[swap_core(p) for p in parts]]

    gd, up_part = clip_gradients(
        ids, clip, step_value, seed_value, in_weight, out_weight, down, up, cores_sum
    )
    down_part = cores_sum(*gd)
    parts = lax.all_to_all(jnp.concatenate([down_part, up_part], axis=1), "dp", 0, 0, tiled=True)
    total = jnp.sum(parts, axis=0)
    down_sum = taps(total[: down_part.shape[1]].reshape(5, -1))
    up_sum = total[down_part.shape[1] :].reshape(10, -1)
    return down_sum[None], taps(up_sum[:, : 3 * CH])[None], up_sum[:, 3 * CH :][None]


def solution(mesh):
    devices = mesh.devices
    grid = Mesh(devices.reshape(devices.shape[0], devices.shape[1], 4, 2), ("dp", "segment", "x", "core"))
    tm = ("x", "core")
    return jax.shard_map(
        local,
        mesh=grid,
        in_specs=(
            P("dp", tm, None, None),
            P("dp"),
            P("dp"),
            P(),
            P(),
            P("segment", None, None, None),
            P("segment", None, None, None),
            P("segment", None, None),
        ),
        out_specs=(
            P("segment", None, ("dp",) + tm, None),
            P("segment", None, ("dp",) + tm, None),
            P("segment", ("dp",) + tm, None),
        ),
        check_vma=False,
    )
```
